256 devices in a mesh: tm: 16 (over y, x), rows: 8 (over z), sect: 2 (over core).
Axes of the slice: x: 4, y: 4, z: 8, core: 2. Of those that a mesh axis runs over, the one named last changes fastest.
Arguments:
- activations: bfloat16 [64, 64, 64, 128], P('tm', 'rows', 'sect'), as said below
- group_norm_gain: float32 [128], replicated, may hold values from 0.1 to 1.9
- group_norm_bias: float32 [128], replicated, may hold values from -3 to 3
- upstream: bfloat16 [64, 64, 64, 128], P('tm', 'rows', 'sect'), may hold values from -6 to 6
- kernel: bfloat16 [3, 3, 3, 128, 128], replicated, may hold values from -0.109375 to 0.109375
Outputs:
- input_gradient: bfloat16 [64, 64, 64, 128], P('tm', 'rows', 'sect')
- gain_grad: float32 [128], replicated
- bias_grad: float32 [128], replicated
- weight_grad: float32 [3, 3, 3, 128, 128], P(None, None, None, None, 'tm')
The draws below stay inside these ranges and needn't reach their ends.
Inputs may be any that keep to these rules, and one draw needn't show every extreme that they name: activations vary in scale over frames, rows and channels and have channel offsets.
All inputs are finite; a program needn't handle non-finite values.
Results may differ from the reference program's by a relative error of at most 0.003.
Values may be sent and summed in bfloat16 or wider, within the bound.
No kernel may reach another device: no remote copies, remote signals or barrier semaphores. Data moves between devices by JAX's collectives and lax.ppermute only.
A program may use at most 64 MiB of HBM per device.

```python
import jax
import jax.numpy as jnp
from jax import lax

C = 128
GROUPS = 32
NT = 64
NH = 64
NW = 64
CELLS = 262144


def draw_activations(key, part):
    subkeys = jax.random.split(key, 4)
    normal_part = jax.random.normal(subkeys[0], (NT, NH, NW, C), jnp.float32)
    roughness = jnp.exp(jax.random.uniform(subkeys[1], (NT, NH, 1, 1), jnp.float32, -0.8, 0.8))
    channel_spread = jnp.exp(jax.random.uniform(subkeys[2], (C,), jnp.float32, -0.8, 0.8))
    offset = jax.random.uniform(subkeys[3], (C,), jnp.float32, -1.0, 1.0)
    ramp = (1.0 + 2.0 * jnp.arange(NT, dtype=jnp.float32) / max(NT - 1, 1)).reshape(NT, 1, 1, 1)
    return ((normal_part * roughness * channel_spread + offset) * ramp).astype(jnp.bfloat16)


def block_levels(key, extent, cuts, smallest, high):
    def one(position, shards_of):
        heights = jax.random.uniform(jax.random.fold_in(jax.random.fold_in(key, 6), position), (shards_of,), jnp.float32, smallest / len(cuts), high / len(cuts))
        return jnp.repeat(jnp.exp(heights), extent[position] // shards_of).reshape((-1,) + (1,) * (len(extent) - position - 1))

    factor_of = one(*cuts[0])
    for cut in cuts[1:]:
        factor_of = factor_of * one(*cut)
    return factor_of


def centred(rng, extent, width, most, shards=(), held_as=jnp.bfloat16):
    factor_of = block_levels(rng, extent, shards, -0.22, 0.18) if shards else 1.0
    array = jax.random.normal(rng, extent, jnp.float32) * width * factor_of
    return jnp.minimum(jnp.maximum(array, -most), most).astype(held_as)


def setup_inputs(seed: int = 0) -> dict:
    streams_of = jax.random.split(jax.random.key(seed), 6)
    activations = draw_activations(jax.random.fold_in(streams_of[5], 71), 0)
    group_norm_gain = jnp.clip(1.0 + 0.18 * jax.random.normal(streams_of[1], (C,), jnp.float32), 0.1, 1.9)
    group_norm_bias = centred(streams_of[2], (C,), 0.5, 3.0, (), jnp.float32)
    upstream = centred(streams_of[3], (NT, NH, NW, C), 1.0, 6.0, ((0, 16), (1, 8), (2, 2)))
    kernel = centred(streams_of[4], (3, 3, 3, C, C), (27 * C) ** -0.5, 0.109375)
    return {"activations": activations, "group_norm_gain": group_norm_gain, "group_norm_bias": group_norm_bias, "upstream": upstream, "kernel": kernel}


def fold_edges(padded_grad):
    folded = padded_grad[2:].at[0].add(padded_grad[0] + padded_grad[1])
    folded = folded.at[:, 1].add(folded[:, 0]).at[:, -2].add(folded[:, -1])[:, 1:-1]
    folded = folded.at[:, :, 1].add(folded[:, :, 0]).at[:, :, -2].add(folded[:, :, -1])[:, :, 1:-1]
    return folded

def reference(activations, group_norm_gain, group_norm_bias, upstream, kernel):
    group_size = C // GROUPS
    input_tensor = activations.astype(jnp.float32)
    channel_total = lax.optimization_barrier(jnp.sum(input_tensor, axis=(0, 1, 2)))
    channel_square = lax.optimization_barrier(jnp.sum(input_tensor * input_tensor, axis=(0, 1, 2)))
    counted = float(CELLS * group_size)
    group_mean = lax.optimization_barrier(jnp.sum(channel_total.reshape(GROUPS, group_size), axis=1)) / counted
    group_square = lax.optimization_barrier(jnp.sum(channel_square.reshape(GROUPS, group_size), axis=1)) / counted
    group_rstd = lax.rsqrt(group_square - group_mean * group_mean + 1e-06)
    channel_mean = jnp.repeat(group_mean, group_size)
    channel_inverse_deviation = jnp.repeat(group_rstd, group_size)
    normalized_input = (input_tensor - channel_mean) * channel_inverse_deviation
    preactivation = normalized_input * group_norm_gain + group_norm_bias
    hidden = jax.nn.silu(preactivation).astype(jnp.bfloat16)
    hidden_pad = jnp.pad(hidden, ((2, 0), (1, 1), (1, 1), (0, 0)), mode='edge')
    grad_pad = jnp.pad(upstream, ((2, 2), (2, 2), (2, 2), (0, 0)))
    flat_grad = upstream.reshape(-1, C)
    padded_grad = jnp.zeros(((NT + 2) * (NH + 2) * (NW + 2), C), jnp.float32)
    kernel_terms = []
    for tap_time in range(3):
        for tap_row in range(3):
            for tap_col in range(3):
                grad_slice = grad_pad[2 - tap_time:2 - tap_time + NT + 2, 2 - tap_row:2 - tap_row + NH + 2, 2 - tap_col:2 - tap_col + NW + 2].reshape(-1, C)
                padded_grad = padded_grad + jnp.dot(grad_slice, kernel[tap_time, tap_row, tap_col].T, preferred_element_type=jnp.float32)
                hidden_slice = hidden_pad[tap_time:tap_time + NT, tap_row:tap_row + NH, tap_col:tap_col + NW].reshape(-1, C)
                kernel_terms.append(jnp.dot(hidden_slice.T, flat_grad, preferred_element_type=jnp.float32))
    hidden_grad = fold_edges(padded_grad.reshape(NT + 2, NH + 2, NW + 2, C))
    sigmoid = jax.nn.sigmoid(preactivation)
    activation_gradient = hidden_grad * sigmoid * (1.0 + preactivation * (1.0 - sigmoid))
    bias_sum = lax.optimization_barrier(jnp.sum(activation_gradient, axis=(0, 1, 2)))
    gain_total_accum = lax.optimization_barrier(jnp.sum(activation_gradient * normalized_input, axis=(0, 1, 2)))
    leading_average = jnp.repeat(lax.optimization_barrier(jnp.sum((group_norm_gain * bias_sum).reshape(GROUPS, group_size), axis=1)) / counted, group_size)
    trailing_average = jnp.repeat(lax.optimization_barrier(jnp.sum((group_norm_gain * gain_total_accum).reshape(GROUPS, group_size), axis=1)) / counted, group_size)
    input_gradient = (channel_inverse_deviation * (activation_gradient * group_norm_gain - leading_average - normalized_input * trailing_average)).astype(jnp.bfloat16)
    scaling = float(CELLS) ** (-0.5)
    weight_grad = jnp.stack(kernel_terms).reshape(3, 3, 3, C, C) * scaling
    return (input_gradient, gain_total_accum * scaling, bias_sum * scaling, weight_grad)
```

```python
import functools

import jax
import jax.numpy as jnp
from jax import lax
from jax.experimental import pallas as pl
from jax.experimental.pallas import tpu as pltpu
from jax.sharding import PartitionSpec as P

GROUPS = 32
TAPS = 27
HALF = 14
SLOTS = HALF + 1
F32 = jnp.float32
BF16 = jnp.bfloat16
VMEM = pl.BlockSpec(memory_space=pltpu.VMEM)
SMEM = pl.BlockSpec(memory_space=pltpu.SMEM)


def call(body, outs, args, scratch=(), flops=0, smem_first=False):
    specs = [VMEM] * len(args)
    if smem_first:
        specs[0] = SMEM
    moved = sum(x.size * x.dtype.itemsize for x in list(args) + list(outs))
    return pl.pallas_call(
        body,
        out_shape=outs,
        in_specs=specs,
        out_specs=[VMEM] * len(outs),
        scratch_shapes=list(scratch),
        cost_estimate=pl.CostEstimate(flops=flops, bytes_accessed=moved, transcendentals=0),
        compiler_params=pltpu.CompilerParams(vmem_limit_bytes=48 * 1024 * 1024),
    )(*args)


def lanes_of(shape):
    return lax.broadcasted_iota(jnp.int32, shape, len(shape) - 1)


def sublanes_of(shape):
    return lax.broadcasted_iota(jnp.int32, shape, len(shape) - 2)


def group_total(v):
    lane = lanes_of(v.shape)
    v = v + jnp.where(lane % 2 == 0, pltpu.roll(v, 127, 1), pltpu.roll(v, 1, 1))
    return v + jnp.where(lane % 4 < 2, pltpu.roll(v, 126, 1), pltpu.roll(v, 2, 1))


def column_sum(v):
    part = jnp.sum(v.reshape(-1, 8, v.shape[-1]), axis=0)
    return jnp.broadcast_to(jnp.sum(part, axis=0, keepdims=True), part.shape)


def stats_kernel(x_ref, out_ref):
    x = x_ref[...].astype(F32).reshape(-1, x_ref.shape[-1])
    total = group_total(column_sum(x))
    square = group_total(column_sum(x * x))
    row = jnp.where(lanes_of(total.shape) % 4 < 2, total, square)
    out_ref[...] = jnp.broadcast_to(row[None], (out_ref.shape[0] // 8, 8, 128)).reshape(out_ref.shape)


def grad_kernel(place_ref, own_ref, side_ref, above_ref, below_ref, later_ref, kernel_ref, v_ref, dh_ref, taps_ref):
    time_first = place_ref[0] == 0
    row_first = place_ref[1] == 0
    row_last = place_ref[1] == place_ref[2] - 1
    left = place_ref[3] == 0
    column = sublanes_of((10, 32, 128))

    for a in range(3):
        for b in range(3):
            for e in range(3):
                j = (b * 3 + e) * 128
                taps_ref[a, :, j : j + 128] = kernel_ref[a, b, e]

    for f in range(6):
        if f < 4:
            mid = jnp.concatenate([own_ref[f].astype(F32), side_ref[f].astype(F32)], axis=1)
            rows = jnp.concatenate(
                [above_ref[f].astype(F32)[None], mid, below_ref[f].astype(F32)[None]], axis=0
            )
        else:
            rows = later_ref[f - 4].astype(F32)
        core = rows[:, :32]
        zero = jnp.zeros_like(core)
        ahead = pltpu.roll(rows, 47, 1)[:, :32]
        behind = pltpu.roll(rows, 1, 1)[:, :32]
        first = column == 0
        last = column == 31
        ahead = jnp.where(left, ahead + jnp.where(first, core, zero), jnp.where(last, zero, ahead))
        behind = jnp.where(left, jnp.where(first, zero, behind), behind + jnp.where(last, core, zero))
        for e, part in enumerate((ahead, core, behind)):
            for b in range(3):
                j = (b * 3 + e) * 128
                shifted = part[2 - b : 10 - b]
                if b == 0:
                    edge = shifted[0] + jnp.where(row_first, part[1], jnp.zeros_like(part[1]))
                    shifted = jnp.concatenate([edge[None], shifted[1:]], axis=0)
                if b == 2:
                    edge = shifted[7] + jnp.where(row_last, part[8], jnp.zeros_like(part[8]))
                    shifted = jnp.concatenate([shifted[:7], edge[None]], axis=0)
                v_ref[f, :, j : j + 128] = shifted.astype(BF16).reshape(256, 128)


    @pl.when(time_first)
    def _():
        both = v_ref[1].astype(F32) + v_ref[0].astype(F32)
        v_ref[6] = both.astype(BF16)
        v_ref[7] = (both + v_ref[2].astype(F32)).astype(BF16)

    @pl.when(jnp.logical_not(time_first))
    def _():
        v_ref[6] = v_ref[1]
        v_ref[7] = v_ref[2]

    dims = (((1,), (1,)), ((), ()))
    for f in range(4):
        total = None
        for a in range(3):
            source = f + 2 - a
            if f == 0 and a < 2:
                source = 7 - a
            term = lax.dot_general(v_ref[source], taps_ref[a], dims, preferred_element_type=F32)
            total = term if total is None else total + term
        dh_ref[pl.ds(f * 256, 256)] = total


def sums_to_pair(row):
    lane = lanes_of(row.shape)
    total = jnp.where(lane % 4 < 2, row, pltpu.roll(row, 2, 1))
    square = jnp.where(lane % 4 < 2, pltpu.roll(row, 126, 1), row)
    return total, square


def main_kernel(counted, place_ref, x_ref, stat_ref, gain_ref, bias_ref, dh_ref, v_ref, w_ref, da_ref, norm_ref):
    total, square = sums_to_pair(column_sum(stat_ref[...]))
    mean = total / counted
    rstd = lax.rsqrt(square / counted - mean * mean + 1e-06)
    norm_ref[0:8] = mean
    norm_ref[8:16] = rstd
    mean = mean[:1]
    rstd = rstd[:1]
    xhat = (x_ref[...].astype(F32).reshape(-1, 128) - mean) * rstd
    pre = xhat * gain_ref[...] + bias_ref[...]
    sig = 1.0 / (1.0 + jnp.exp(-pre))
    hidden = pre * sig
    da = dh_ref[...] * sig * (1.0 + pre * (1.0 - sig))
    da_ref[...] = da
    sums = jnp.where(sublanes_of((8, 128)) == 0, column_sum(da), column_sum(da * xhat))
    for half in range(2):
        w_ref[half, :, HALF] = jnp.broadcast_to(sums[None], (16, 8, 128))
    turned = hidden.T.astype(BF16)
    sect = place_ref[3]
    for a in range(3):
        if a == 2:
            product = jnp.dot(turned, v_ref[0:4].reshape(1024, 1152), preferred_element_type=F32)
        else:
            product = jnp.dot(turned[:, :256], v_ref[7 - a], preferred_element_type=F32) + jnp.dot(
                turned[:, 256:], v_ref[3 - a : 6 - a].reshape(768, 1152), preferred_element_type=F32
            )
        for j in range(9):
            tap = a * 9 + j
            block = product[:, j * 128 : (j + 1) * 128].T.reshape(16, 8, 128)
            w_ref[(tap // HALF) ^ sect, :, tap % HALF] = block
    w_ref[1 ^ sect, :, HALF - 1] = jnp.zeros((16, 8, 128), F32)


def split_sums(sums):
    row = sublanes_of(sums.shape)
    high = sums.astype(BF16).astype(F32)
    middle = (sums - high).astype(BF16).astype(F32)
    low = sums - high - middle
    return jnp.where(
        row < 2, high, jnp.where(row < 4, pltpu.roll(middle, 2, 0), pltpu.roll(low, 4, 0))
    )


def join_sums(parts):
    return parts + pltpu.roll(parts, 6, 0) + pltpu.roll(parts, 4, 0)


def pair_kernel(own_ref, other_ref, out_ref):
    rows = HALF * 8
    slot = split_sums(own_ref[0, HALF] + other_ref[0, HALF])
    for i in range(16):
        body = (own_ref[i, :HALF] + other_ref[i, :HALF]).reshape(rows, 128)
        out_ref[i] = jnp.concatenate([body, slot], axis=0).astype(BF16)


def share_kernel(in_ref, out_ref):
    rows = HALF * 8
    total = in_ref[0].astype(F32)
    for i in range(1, in_ref.shape[0]):
        total = total + in_ref[i].astype(F32)
    slot = split_sums(join_sums(total[rows:]))
    sent = jnp.concatenate([total[:rows], slot], axis=0).astype(BF16)
    for i in range(out_ref.shape[0]):
        out_ref[i] = sent


def last_sum_kernel(scaling, in_ref, half_ref, sums_ref):
    rows = HALF * 8
    total = in_ref[0].astype(F32)
    for i in range(1, in_ref.shape[0]):
        total = total + in_ref[i].astype(F32)
    half_ref[...] = total[:rows] * scaling
    sums_ref[...] = join_sums(total[rows:])


def finish_kernel(counted, scaling, x_ref, da_ref, norm_ref, sums_ref, gain_ref, out_ref, grads_ref):
    gain = gain_ref[...]
    mean = norm_ref[0:1]
    rstd = norm_ref[8:9]
    sums = sums_ref[...]
    grads_ref[...] = sums * scaling
    averages = group_total(gain * sums) / counted
    leading = averages[0:1]
    trailing = averages[1:2]
    xhat = (x_ref[...].astype(F32).reshape(-1, 128) - mean) * rstd
    grad = rstd * (da_ref[...] * gain - leading - xhat * trailing)
    out_ref[...] = grad.astype(BF16).reshape(out_ref.shape)


def shape_of(shape, dtype=F32):
    return jax.ShapeDtypeStruct(shape, dtype)


def local(activations, group_norm_gain, group_norm_bias, upstream, kernel):
    frames, height, columns, channels = activations.shape
    n_time, n_rows, n_sect = (lax.axis_size(axis) for axis in ("tm", "rows", "sect"))
    cells = frames * height * columns
    total_cells = cells * n_time * n_rows * n_sect
    counted = float(total_cells * (channels // GROUPS))
    scaling = float(total_cells) ** (-0.5)
    tm, rows, sect = (lax.axis_index(axis) for axis in ("tm", "rows", "sect"))
    place = jnp.stack([tm, rows, jnp.int32(n_rows), sect]).astype(jnp.int32)
    swap = [(0, 1), (1, 0)]

    facing = jnp.where(sect == 0, upstream[:, :, 16:], upstream[:, :, :16])
    side = lax.ppermute(facing, "sect", swap)
    (stat,) = call(stats_kernel, [shape_of((32, 128))], [activations])
    stat = lax.all_to_all(stat.reshape(32, 1, 128), ("tm", "sect"), 0, 0)
    last_row = jnp.concatenate([upstream[:, height - 1], side[:, height - 1]], axis=1)
    first_row = jnp.concatenate([upstream[:, 0], side[:, 0]], axis=1)
    above = lax.ppermute(last_row, "rows", [(i, i + 1) for i in range(n_rows - 1)])
    below = lax.ppermute(first_row, "rows", [(i + 1, i) for i in range(n_rows - 1)])
    early = jnp.concatenate(
        [above[:2, None], jnp.concatenate([upstream[:2], side[:2]], axis=2), below[:2, None]], axis=1
    )
    later = lax.ppermute(early, "tm", [(i + 1, i) for i in range(n_time - 1)])
    stat = jnp.broadcast_to(jnp.sum(stat, axis=0)[None], (n_rows, 1, 128))
    stat = lax.all_to_all(stat, "rows", 0, 0).reshape(n_rows, 128)
    spread, hidden_grad = call(
        grad_kernel,
        [shape_of((8, 256, 1152), BF16), shape_of((cells, channels))],
        [place, upstream, side, above, below, later, kernel],
        [pltpu.VMEM((3, 128, 1152), BF16)],
        flops=2 * cells * TAPS * channels * channels,
        smem_first=True,
    )
    gain = group_norm_gain.reshape(1, channels)
    bias = group_norm_bias.reshape(1, channels)
    terms, da, norm = call(
        functools.partial(main_kernel, counted),
        [shape_of((2, 16, SLOTS, 8, 128)), shape_of((cells, channels)), shape_of((16, channels))],
        [place, activations, stat, gain, bias, hidden_grad, spread],
        flops=2 * cells * TAPS * channels * channels,
        smem_first=True,
    )
    other = lax.ppermute(terms[1], "sect", swap)
    (sent,) = call(pair_kernel, [shape_of((16, SLOTS * 8, 128), BF16)], [terms[0], other])
    gathered = lax.all_to_all(sent, "tm", 0, 0)
    (sent,) = call(share_kernel, [shape_of((n_rows, SLOTS * 8, 128), BF16)], [gathered])
    gathered = lax.all_to_all(sent, "rows", 0, 0)
    half, sums = call(
        functools.partial(last_sum_kernel, scaling),
        [shape_of((HALF * 8, 128)), shape_of((8, 128))],
        [gathered],
    )
    other = lax.ppermute(half, "sect", swap)
    input_gradient, grads = call(
        functools.partial(finish_kernel, counted, scaling),
        [shape_of(activations.shape, BF16), shape_of((8, 128))],
        [activations, da, norm, sums, gain],
    )
    whole = jnp.concatenate(
        [jnp.where(sect == 0, half, other), jnp.where(sect == 0, other, half)], axis=0
    )
    weight_grad = whole[: TAPS * 8].reshape(3, 3, 3, 8, 128).transpose(0, 1, 2, 4, 3)
    return (input_gradient, grads[1], grads[0], weight_grad)


def solution(mesh):
    return jax.shard_map(
        local,
        mesh=mesh,
        in_specs=(P("tm", "rows", "sect", None), P(), P(), P("tm", "rows", "sect", None), P()),
        out_specs=(P("tm", "rows", "sect", None), P(), P(), P(None, None, None, None, "tm")),
        check_vma=False,
    )
```

```python
import functools

import jax
import jax.numpy as jnp
from jax import lax
from jax.experimental import pallas as pl
from jax.experimental.pallas import tpu as pltpu
from jax.sharding import PartitionSpec as P

GROUPS = 32
TAPS = 27
HALF = 14
SLOTS = HALF + 1
F32 = jnp.float32
BF16 = jnp.bfloat16
VMEM = pl.BlockSpec(memory_space=pltpu.VMEM)
SMEM = pl.BlockSpec(memory_space=pltpu.SMEM)


def call(body, outs, args, scratch=(), flops=0, smem_first=False):
    specs = [VMEM] * len(args)
    if smem_first:
        specs[0] = SMEM
    moved = sum(x.size * x.dtype.itemsize for x in list(args) + list(outs))
    return pl.pallas_call(
        body,
        out_shape=outs,
        in_specs=specs,
        out_specs=[VMEM] * len(outs),
        scratch_shapes=list(scratch),
        cost_estimate=pl.CostEstimate(flops=flops, bytes_accessed=moved, transcendentals=0),
        compiler_params=pltpu.CompilerParams(vmem_limit_bytes=48 * 1024 * 1024),
    )(*args)


def lanes_of(shape):
    return lax.broadcasted_iota(jnp.int32, shape, len(shape) - 1)


def sublanes_of(shape):
    return lax.broadcasted_iota(jnp.int32, shape, len(shape) - 2)


def group_total(v):
    lane = lanes_of(v.shape)
    v = v + jnp.where(lane % 2 == 0, pltpu.roll(v, 127, 1), pltpu.roll(v, 1, 1))
    return v + jnp.where(lane % 4 < 2, pltpu.roll(v, 126, 1), pltpu.roll(v, 2, 1))


def column_sum(v):
    part = jnp.sum(v.reshape(-1, 8, v.shape[-1]), axis=0)
    return jnp.broadcast_to(jnp.sum(part, axis=0, keepdims=True), part.shape)


def entry_kernel(place_ref, x_ref, up_ref, stat_ref, facing_ref, edge_ref, early_ref):
    left = place_ref[3] == 0
    up = up_ref[...]
    facing_ref[...] = jnp.where(left, up[:, :, 16:], up[:, :, :16])
    edge_ref[0] = up[:, 7]
    edge_ref[1] = up[:, 0]
    early_ref[...] = up[:2]
    x = x_ref[...].astype(F32).reshape(-1, x_ref.shape[-1])
    total = group_total(column_sum(x))
    square = group_total(column_sum(x * x))
    row = jnp.where(lanes_of(total.shape) % 4 < 2, total, square)
    stat_ref[...] = jnp.broadcast_to(row[None], (stat_ref.shape[0] // 8, 8, 128)).reshape(stat_ref.shape)


def grad_kernel(place_ref, own_ref, side_ref, above_ref, below_ref, later_ref, kernel_ref, v_ref, dh_ref, taps_ref):
    time_first = place_ref[0] == 0
    row_first = place_ref[1] == 0
    row_last = place_ref[1] == place_ref[2] - 1
    left = place_ref[3] == 0
    column = sublanes_of((10, 32, 128))

    for a in range(3):
        for b in range(3):
            for e in range(3):
                j = (b * 3 + e) * 128
                taps_ref[a, :, j : j + 128] = kernel_ref[a, b, e]

    for f in range(6):
        if f < 4:
            mid = jnp.concatenate([own_ref[f].astype(F32), side_ref[f].astype(F32)], axis=1)
            rows = jnp.concatenate(
                [above_ref[f].astype(F32)[None], mid, below_ref[f].astype(F32)[None]], axis=0
            )
        else:
            rows = later_ref[f - 4].astype(F32)
        core = rows[:, :32]
        zero = jnp.zeros_like(core)
        ahead = pltpu.roll(rows, 47, 1)[:, :32]
        behind = pltpu.roll(rows, 1, 1)[:, :32]
        first = column == 0
        last = column == 31
        ahead = jnp.where(left, ahead + jnp.where(first, core, zero), jnp.where(last, zero, ahead))
        behind = jnp.where(left, jnp.where(first, zero, behind), behind + jnp.where(last, core, zero))
        for e, part in enumerate((ahead, core, behind)):
            for b in range(3):
                j = (b * 3 + e) * 128
                shifted = part[2 - b : 10 - b]
                if b == 0:
                    edge = shifted[0] + jnp.where(row_first, part[1], jnp.zeros_like(part[1]))
                    shifted = jnp.concatenate([edge[None], shifted[1:]], axis=0)
                if b == 2:
                    edge = shifted[7] + jnp.where(row_last, part[8], jnp.zeros_like(part[8]))
                    shifted = jnp.concatenate([shifted[:7], edge[None]], axis=0)
                v_ref[f, :, j : j + 128] = shifted.astype(BF16).reshape(256, 128)


    @pl.when(time_first)
    def _():
        both = v_ref[1].astype(F32) + v_ref[0].astype(F32)
        v_ref[6] = both.astype(BF16)
        v_ref[7] = (both + v_ref[2].astype(F32)).astype(BF16)

    @pl.when(jnp.logical_not(time_first))
    def _():
        v_ref[6] = v_ref[1]
        v_ref[7] = v_ref[2]

    dims = (((1,), (1,)), ((), ()))
    for f in range(4):
        total = None
        for a in range(3):
            source = f + 2 - a
            if f == 0 and a < 2:
                source = 7 - a
            term = lax.dot_general(v_ref[source], taps_ref[a], dims, preferred_element_type=F32)
            total = term if total is None else total + term
        dh_ref[pl.ds(f * 256, 256)] = total


def sums_to_pair(row):
    lane = lanes_of(row.shape)
    total = jnp.where(lane % 4 < 2, row, pltpu.roll(row, 2, 1))
    square = jnp.where(lane % 4 < 2, pltpu.roll(row, 126, 1), row)
    return total, square


def product_of(turned, v_ref, a, lo, hi):
    if a == 2:
        return jnp.dot(turned, v_ref[0:4, :, lo:hi].reshape(1024, hi - lo), preferred_element_type=F32)
    first = jnp.dot(turned[:, :256], v_ref[7 - a, :, lo:hi], preferred_element_type=F32)
    rest = v_ref[3 - a : 6 - a, :, lo:hi].reshape(768, hi - lo)
    return first + jnp.dot(turned[:, 256:], rest, preferred_element_type=F32)


def half_product(half, turned, v_ref, w_ref):
    for a, lo, hi in (((0, 0, 9), (1, 0, 5)), ((1, 5, 9), (2, 0, 9)))[half]:
        product = product_of(turned, v_ref, a, lo * 128, hi * 128)
        for j in range(lo, hi):
            block = product[:, (j - lo) * 128 : (j - lo + 1) * 128].T.reshape(16, 8, 128)
            w_ref[:, (a * 9 + j) % HALF] = block
    if half == 1:
        w_ref[:, HALF - 1] = jnp.zeros((16, 8, 128), F32)


def normalised(x_ref, mean, rstd, gain_ref, bias_ref):
    xhat = (x_ref[...].astype(F32).reshape(-1, 128) - mean) * rstd
    return xhat, xhat * gain_ref[...] + bias_ref[...]


def away_kernel(counted, place_ref, x_ref, stat_ref, gain_ref, bias_ref, v_ref, w_ref, turned_ref, norm_ref):
    total, square = sums_to_pair(column_sum(stat_ref[...]))
    mean = total / counted
    rstd = lax.rsqrt(square / counted - mean * mean + 1e-06)
    norm_ref[0:8] = mean
    norm_ref[8:16] = rstd
    _, pre = normalised(x_ref, mean[:1], rstd[:1], gain_ref, bias_ref)
    turned_ref[...] = (pre * (1.0 / (1.0 + jnp.exp(-pre)))).T.astype(BF16)
    left = place_ref[3] == 0

    @pl.when(left)
    def _():
        half_product(1, turned_ref[...], v_ref, w_ref)

    @pl.when(jnp.logical_not(left))
    def _():
        half_product(0, turned_ref[...], v_ref, w_ref)


def home_kernel(place_ref, x_ref, norm_ref, gain_ref, bias_ref, dh_ref, turned_ref, v_ref, sums_ref, da_ref, w_ref):
    xhat, pre = normalised(x_ref, norm_ref[0:1], norm_ref[8:9], gain_ref, bias_ref)
    sig = 1.0 / (1.0 + jnp.exp(-pre))
    da = dh_ref[...] * sig * (1.0 + pre * (1.0 - sig))
    da_ref[...] = da
    sums_ref[...] = jnp.where(sublanes_of((8, 128)) == 0, column_sum(da), column_sum(da * xhat))
    left = place_ref[3] == 0

    @pl.when(left)
    def _():
        half_product(0, turned_ref[...], v_ref, w_ref)

    @pl.when(jnp.logical_not(left))
    def _():
        half_product(1, turned_ref[...], v_ref, w_ref)


def split_sums(sums):
    row = sublanes_of(sums.shape)
    high = sums.astype(BF16).astype(F32)
    middle = (sums - high).astype(BF16).astype(F32)
    low = sums - high - middle
    return jnp.where(
        row < 2, high, jnp.where(row < 4, pltpu.roll(middle, 2, 0), pltpu.roll(low, 4, 0))
    )


def join_sums(parts):
    return parts + pltpu.roll(parts, 6, 0) + pltpu.roll(parts, 4, 0)


def pair_kernel(own_ref, other_ref, sums_ref, other_sums_ref, out_ref):
    slot = split_sums(sums_ref[...] + other_sums_ref[...])
    for i in range(16):
        body = (own_ref[i] + other_ref[i]).reshape(HALF * 8, 128)
        out_ref[i] = jnp.concatenate([body, slot], axis=0).astype(BF16)


def share_kernel(in_ref, out_ref):
    rows = HALF * 8
    total = in_ref[0].astype(F32)
    for i in range(1, in_ref.shape[0]):
        total = total + in_ref[i].astype(F32)
    sent = jnp.concatenate([total[:rows], join_sums(total[rows:])], axis=0)
    for i in range(out_ref.shape[0]):
        out_ref[i] = sent


def last_sum_kernel(scaling, in_ref, half_ref, sums_ref):
    rows = HALF * 8
    total = in_ref[0]
    for i in range(1, in_ref.shape[0]):
        total = total + in_ref[i]
    half_ref[...] = total[:rows] * scaling
    sums_ref[...] = total[rows:]


def finish_kernel(counted, scaling, x_ref, da_ref, norm_ref, sums_ref, gain_ref, out_ref, gain_grad_ref, bias_grad_ref):
    gain = gain_ref[...]
    mean = norm_ref[0:1]
    rstd = norm_ref[8:9]
    sums = sums_ref[...]
    bias_grad_ref[...] = sums[0:1] * scaling
    gain_grad_ref[...] = sums[1:2] * scaling
    averages = group_total(gain * sums) / counted
    leading = averages[0:1]
    trailing = averages[1:2]
    xhat = (x_ref[...].astype(F32).reshape(-1, 128) - mean) * rstd
    grad = rstd * (da_ref[...] * gain - leading - xhat * trailing)
    out_ref[...] = grad.astype(BF16).reshape(out_ref.shape)


def join_kernel(place_ref, half_ref, other_ref, out_ref):
    left = place_ref[3] == 0
    half = half_ref[...]
    other = other_ref[...]
    out_ref[: HALF * 8] = jnp.where(left, half, other)
    out_ref[HALF * 8 :] = jnp.where(left, other, half)[: (TAPS - HALF) * 8]


def shape_of(shape, dtype=F32):
    return jax.ShapeDtypeStruct(shape, dtype)


def local(activations, group_norm_gain, group_norm_bias, upstream, kernel):
    frames, height, columns, channels = activations.shape
    n_time, n_rows, n_sect = (lax.axis_size(axis) for axis in ("tm", "rows", "sect"))
    cells = frames * height * columns
    total_cells = cells * n_time * n_rows * n_sect
    counted = float(total_cells * (channels // GROUPS))
    scaling = float(total_cells) ** (-0.5)
    tm, rows, sect = (lax.axis_index(axis) for axis in ("tm", "rows", "sect"))
    place = jnp.stack([tm, rows, jnp.int32(n_rows), sect]).astype(jnp.int32)
    swap = [(0, 1), (1, 0)]

    stat, facing, edges, first_frames = call(
        entry_kernel,
        [
            shape_of((32, 128)),
            shape_of((frames, height, 16, channels), BF16),
            shape_of((2, frames, columns, channels), BF16),
            shape_of((2, height, columns, channels), BF16),
        ],
        [place, activations, upstream],
        smem_first=True,
    )
    side = lax.ppermute(facing, "sect", swap)
    last_row = jnp.concatenate([edges[0], side[:, height - 1]], axis=1)
    first_row = jnp.concatenate([edges[1], side[:, 0]], axis=1)
    stat, last_row, first_row = lax.optimization_barrier((stat, last_row, first_row))
    above = lax.ppermute(last_row, "rows", [(i, i + 1) for i in range(n_rows - 1)])
    below = lax.ppermute(first_row, "rows", [(i + 1, i) for i in range(n_rows - 1)])
    stat = lax.all_to_all(stat.reshape(32, 1, 128), ("tm", "sect"), 0, 0)
    stat = jnp.broadcast_to(jnp.sum(stat, axis=0)[None], (n_rows, 1, 128))
    stat, above, below = lax.optimization_barrier((stat, above, below))
    early = jnp.concatenate(
        [above[:2, None], jnp.concatenate([first_frames, side[:2]], axis=2), below[:2, None]], axis=1
    )
    stat, early = lax.optimization_barrier((stat, early))
    later = lax.ppermute(early, "tm", [(i + 1, i) for i in range(n_time - 1)])
    stat = lax.all_to_all(stat, "rows", 0, 0).reshape(n_rows, 128)
    spread, hidden_grad = call(
        grad_kernel,
        [shape_of((8, 256, 1152), BF16), shape_of((cells, channels))],
        [place, upstream, side, above, below, later, kernel],
        [pltpu.VMEM((3, 128, 1152), BF16)],
        flops=2 * cells * TAPS * channels * channels,
        smem_first=True,
    )
    gain = group_norm_gain.reshape(1, channels)
    bias = group_norm_bias.reshape(1, channels)
    away, turned, norm = call(
        functools.partial(away_kernel, counted),
        [shape_of((16, HALF, 8, 128)), shape_of((channels, cells), BF16), shape_of((16, channels))],
        [place, activations, stat, gain, bias, spread],
        flops=cells * TAPS * channels * channels,
        smem_first=True,
    )
    arrived = lax.ppermute(away, "sect", swap)
    sums, da, home = call(
        home_kernel,
        [shape_of((8, channels)), shape_of((cells, channels)), shape_of((16, HALF, 8, 128))],
        [place, activations, norm, gain, bias, hidden_grad, turned, spread],
        flops=cells * TAPS * channels * channels,
        smem_first=True,
    )
    other_sums = lax.ppermute(sums, "sect", swap)
    (sent,) = call(
        pair_kernel, [shape_of((16, SLOTS * 8, 128), BF16)], [home, arrived, sums, other_sums]
    )
    gathered = lax.all_to_all(sent, "tm", 0, 0)
    (sent,) = call(share_kernel, [shape_of((n_rows, SLOTS * 8, 128))], [gathered])
    gathered = lax.all_to_all(sent, "rows", 0, 0)
    half, sums = call(
        functools.partial(last_sum_kernel, scaling),
        [shape_of((HALF * 8, 128)), shape_of((8, 128))],
        [gathered],
    )
    other = lax.ppermute(half, "sect", swap)
    input_gradient, gain_grad, bias_grad = call(
        functools.partial(finish_kernel, counted, scaling),
        [shape_of(activations.shape, BF16), shape_of((1, 128)), shape_of((1, 128))],
        [activations, da, norm, sums, gain],
    )
    (whole,) = call(join_kernel, [shape_of((TAPS * 8, 128))], [place, half, other], smem_first=True)
    weight_grad = whole.reshape(3, 3, 3, 8, 128).transpose(0, 1, 2, 4, 3)
    return (input_gradient, gain_grad.reshape(128), bias_grad.reshape(128), weight_grad)


def solution(mesh):
    return jax.shard_map(
        local,
        mesh=mesh,
        in_specs=(P("tm", "rows", "sect", None), P(), P(), P("tm", "rows", "sect", None), P()),
        out_specs=(P("tm", "rows", "sect", None), P(), P(), P(None, None, None, None, "tm")),
        check_vma=False,
    )
```

```python
import functools

import jax
import jax.numpy as jnp
from jax import lax
from jax.experimental import pallas as pl
from jax.experimental.pallas import tpu as pltpu
from jax.sharding import PartitionSpec as P

GROUPS = 32
TAPS = 27
HALF = 14
SLOTS = HALF + 1
F32 = jnp.float32
BF16 = jnp.bfloat16
VMEM = pl.BlockSpec(memory_space=pltpu.VMEM)
SMEM = pl.BlockSpec(memory_space=pltpu.SMEM)
ANY = pl.BlockSpec(memory_space=pl.ANY)


def call(body, outs, args, specs=None, scratch=(), flops=0):
    moved = sum(x.size * x.dtype.itemsize for x in list(args) + list(outs))
    return pl.pallas_call(
        body,
        out_shape=outs,
        in_specs=specs or [VMEM] * len(args),
        out_specs=[VMEM] * len(outs),
        scratch_shapes=list(scratch),
        cost_estimate=pl.CostEstimate(flops=flops, bytes_accessed=moved, transcendentals=0),
        compiler_params=pltpu.CompilerParams(vmem_limit_bytes=24 * 1024 * 1024),
    )(*args)


def lanes_of(shape):
    return lax.broadcasted_iota(jnp.int32, shape, len(shape) - 1)


def sublanes_of(shape):
    return lax.broadcasted_iota(jnp.int32, shape, len(shape) - 2)


def group_total(v):
    lane = lanes_of(v.shape)
    v = v + jnp.where(lane % 2 == 0, pltpu.roll(v, 127, 1), pltpu.roll(v, 1, 1))
    return v + jnp.where(lane % 4 < 2, pltpu.roll(v, 126, 1), pltpu.roll(v, 2, 1))


def column_sum(v):
    part = jnp.sum(v.reshape(-1, 8, v.shape[-1]), axis=0)
    return jnp.broadcast_to(jnp.sum(part, axis=0, keepdims=True), part.shape)


def split_row(row):
    high = row.astype(BF16).astype(F32)
    middle = (row - high).astype(BF16).astype(F32)
    low = row - high - middle
    index = sublanes_of((8, 128))
    parts = jnp.where(index == 0, high, jnp.where(index == 1, middle, low))
    return jnp.concatenate([parts, parts], axis=0).astype(BF16)


def join_row(parts):
    parts = parts.astype(F32)
    return jnp.broadcast_to(parts[0:1] + parts[1:2] + parts[2:3], (8, 128))


def entry_kernel(place_ref, x_hbm, up_hbm, x_ref, up_ref, facing_ref, stat_ref, x_sem, up_sem):
    up_copy = pltpu.make_async_copy(up_hbm, up_ref, up_sem)
    x_copy = pltpu.make_async_copy(x_hbm, x_ref, x_sem)
    x_copy.start()
    up_copy.start()
    x_copy.wait()
    x = x_ref[...].astype(F32).reshape(-1, 128)
    total = group_total(column_sum(x))
    square = group_total(column_sum(x * x))
    row = jnp.where(lanes_of(total.shape) % 4 < 2, total, square)
    stat_ref[...] = row
    facing_ref[512:] = split_row(row)
    up_copy.wait()
    left = place_ref[3] == 0
    up = up_ref[...]
    facing_ref[:512] = jnp.where(left, up[:, :, 16:], up[:, :, :16]).reshape(512, 128)


def edge_of(up_ref, side_ref, bottom):
    side = side_ref[:512].reshape(4, 8, 16, 128)
    low = jnp.concatenate([up_ref[:, 7], side[:, 7]], axis=1)
    top = jnp.concatenate([up_ref[:, 0], side[:, 0]], axis=1)
    return jnp.where(bottom, low, top).reshape(192, 128)


def first_edge_kernel(place_ref, up_ref, side_ref, stat_ref, out_ref, sum_ref):
    even = place_ref[1] % 2 == 0
    row = stat_ref[...] + join_row(side_ref[512:])
    sum_ref[...] = row
    out_ref[:192] = edge_of(up_ref, side_ref, even)
    out_ref[192:] = split_row(row)


def second_edge_kernel(place_ref, up_ref, side_ref, near_ref, stat_ref, out_ref, sum_ref):
    even = place_ref[1] % 2 == 0
    row = stat_ref[...] + join_row(near_ref[192:])
    sum_ref[...] = row
    out_ref[:192] = edge_of(up_ref, side_ref, jnp.logical_not(even))
    out_ref[192:] = split_row(row)


def beyond(place_ref, near_ref, far_ref):
    even = place_ref[1] % 2 == 0
    outside = jnp.logical_or(place_ref[1] == 0, place_ref[1] == place_ref[2] - 1)
    near = near_ref[:192].reshape(4, 48, 128)
    far = far_ref[:192].reshape(4, 48, 128)
    far = jnp.where(outside, jnp.zeros_like(far), far)
    return jnp.where(even, far, near), jnp.where(even, near, far)


def early_kernel(place_ref, up_ref, side_ref, near_ref, far_ref, stat_ref, early_ref, sent_ref):
    row = stat_ref[...] + join_row(far_ref[192:])
    sent_ref[...] = jnp.broadcast_to(row[None], (sent_ref.shape[0] // 8, 8, 128)).reshape(sent_ref.shape)
    above, below = beyond(place_ref, near_ref, far_ref)
    early_ref[:, 0] = above[:2]
    early_ref[:, 9] = below[:2]
    early_ref[:, 1:9, :32] = up_ref[:2]
    early_ref[:, 1:9, 32:] = side_ref[:256].reshape(2, 8, 16, 128)


def grad_kernel(place_ref, up_ref, side_ref, near_ref, far_ref, later_ref, kernel_hbm, v_ref, dh_ref, kernel_ref, taps_ref, sem):
    weights = pltpu.make_async_copy(kernel_hbm, kernel_ref, sem)
    weights.start()
    time_first = place_ref[0] == 0
    row_first = place_ref[1] == 0
    row_last = place_ref[1] == place_ref[2] - 1
    left = place_ref[3] == 0
    column = sublanes_of((10, 32, 128))
    first = column == 0
    last = column == 31
    above, below = beyond(place_ref, near_ref, far_ref)

    for f in range(6):
        if f < 4:
            side = side_ref[f * 128 : (f + 1) * 128].reshape(8, 16, 128)
            mid = jnp.concatenate([up_ref[f].astype(F32), side.astype(F32)], axis=1)
            rows = jnp.concatenate([above[f : f + 1].astype(F32), mid, below[f : f + 1].astype(F32)], axis=0)
        else:
            rows = later_ref[f - 4].astype(F32)
        core = rows[:, :32]
        zero = jnp.zeros_like(core)
        ahead = pltpu.roll(rows, 47, 1)[:, :32]
        behind = pltpu.roll(rows, 1, 1)[:, :32]
        ahead = jnp.where(left, ahead + jnp.where(first, core, zero), jnp.where(last, zero, ahead))
        behind = jnp.where(left, jnp.where(first, zero, behind), behind + jnp.where(last, core, zero))
        for e, part in enumerate((ahead, core, behind)):
            for b in range(3):
                j = (b * 3 + e) * 128
                shifted = part[2 - b : 10 - b]
                if b == 0:
                    edge = shifted[0] + jnp.where(row_first, part[1], jnp.zeros_like(part[1]))
                    shifted = jnp.concatenate([edge[None], shifted[1:]], axis=0)
                if b == 2:
                    edge = shifted[7] + jnp.where(row_last, part[8], jnp.zeros_like(part[8]))
                    shifted = jnp.concatenate([shifted[:7], edge[None]], axis=0)
                v_ref[f, :, j : j + 128] = shifted.astype(BF16).reshape(256, 128)

    @pl.when(time_first)
    def _():
        both = v_ref[1].astype(F32) + v_ref[0].astype(F32)
        v_ref[6] = both.astype(BF16)
        v_ref[7] = (both + v_ref[2].astype(F32)).astype(BF16)

    @pl.when(jnp.logical_not(time_first))
    def _():
        v_ref[6] = v_ref[1]
        v_ref[7] = v_ref[2]

    weights.wait()
    for a in range(3):
        for b in range(3):
            for e in range(3):
                j = (b * 3 + e) * 128
                taps_ref[a, :, j : j + 128] = kernel_ref[a, b, e]
    dims = (((1,), (1,)), ((), ()))
    for f in range(4):
        total = None
        for a in range(3):
            source = f + 2 - a
            if f == 0 and a < 2:
                source = 7 - a
            term = lax.dot_general(v_ref[source], taps_ref[a], dims, preferred_element_type=F32)
            total = term if total is None else total + term
        dh_ref[f * 256 : (f + 1) * 256] = total


def sums_to_pair(row):
    lane = lanes_of(row.shape)
    total = jnp.where(lane % 4 < 2, row, pltpu.roll(row, 2, 1))
    square = jnp.where(lane % 4 < 2, pltpu.roll(row, 126, 1), row)
    return total, square


def product_of(turned, v_ref, a, lo, hi):
    if a == 2:
        return jnp.dot(turned, v_ref[0:4, :, lo:hi].reshape(1024, hi - lo), preferred_element_type=F32)
    first = jnp.dot(turned[:, :256], v_ref[7 - a, :, lo:hi], preferred_element_type=F32)
    rest = v_ref[3 - a : 6 - a, :, lo:hi].reshape(768, hi - lo)
    return first + jnp.dot(turned[:, 256:], rest, preferred_element_type=F32)


def half_product(half, turned, v_ref, w_ref):
    for a, lo, hi in (((0, 0, 9), (1, 0, 5)), ((1, 5, 9), (2, 0, 9)))[half]:
        product = product_of(turned, v_ref, a, lo * 128, hi * 128)
        for j in range(lo, hi):
            block = product[:, (j - lo) * 128 : (j - lo + 1) * 128].T.reshape(16, 8, 128)
            w_ref[:, (a * 9 + j) % HALF] = block
    if half == 1:
        w_ref[:, HALF - 1] = jnp.zeros((16, 8, 128), F32)


def away_kernel(
    counted, place_ref, x_ref, stat_ref, gain_ref, bias_ref, dh_ref, v_ref, w_ref, turned_ref, norm_ref, da_ref, sums_ref
):
    total, square = sums_to_pair(column_sum(stat_ref[...]))
    mean = total / counted
    rstd = lax.rsqrt(square / counted - mean * mean + 1e-06)
    norm_ref[0:8] = mean
    norm_ref[8:16] = rstd
    mean, rstd = mean[:1], rstd[:1]
    gain = gain_ref[...]
    bias = bias_ref[...]
    bias_sum = jnp.zeros((8, 128), F32)
    gain_sum = jnp.zeros((8, 128), F32)
    for block in range(8):
        xhat = (x_ref[block // 2, (block % 2) * 4 : (block % 2) * 4 + 4].astype(F32).reshape(128, 128) - mean) * rstd
        pre = xhat * gain + bias
        sig = 1.0 / (1.0 + jnp.exp(-pre))
        turned_ref[:, block * 128 : (block + 1) * 128] = (pre * sig).T.astype(BF16)
        da = dh_ref[block * 128 : (block + 1) * 128] * sig * (1.0 + pre * (1.0 - sig))
        da_ref[block * 128 : (block + 1) * 128] = da
        bias_sum = bias_sum + jnp.sum(da.reshape(16, 8, 128), axis=0)
        gain_sum = gain_sum + jnp.sum((da * xhat).reshape(16, 8, 128), axis=0)
    sums_ref[...] = jnp.where(sublanes_of((8, 128)) == 0, column_sum(bias_sum), column_sum(gain_sum))
    left = place_ref[3] == 0

    @pl.when(left)
    def _():
        half_product(1, turned_ref[...], v_ref, w_ref)

    @pl.when(jnp.logical_not(left))
    def _():
        half_product(0, turned_ref[...], v_ref, w_ref)


def home_kernel(place_ref, turned_ref, v_ref, w_ref):
    left = place_ref[3] == 0

    @pl.when(left)
    def _():
        half_product(0, turned_ref[...], v_ref, w_ref)

    @pl.when(jnp.logical_not(left))
    def _():
        half_product(1, turned_ref[...], v_ref, w_ref)


def split_sums(sums):
    row = sublanes_of(sums.shape)
    high = sums.astype(BF16).astype(F32)
    middle = (sums - high).astype(BF16).astype(F32)
    low = sums - high - middle
    return jnp.where(
        row < 2, high, jnp.where(row < 4, pltpu.roll(middle, 2, 0), pltpu.roll(low, 4, 0))
    )


def join_sums(parts):
    return parts + pltpu.roll(parts, 6, 0) + pltpu.roll(parts, 4, 0)


def pair_kernel(own_ref, other_ref, sums_ref, other_sums_ref, out_ref):
    slot = split_sums(sums_ref[...] + other_sums_ref[...])
    for i in range(16):
        body = (own_ref[i] + other_ref[i]).reshape(HALF * 8, 128)
        out_ref[i] = jnp.concatenate([body, slot], axis=0).astype(BF16)


def share_kernel(in_ref, out_ref):
    rows = HALF * 8
    total = in_ref[0].astype(F32)
    for i in range(1, in_ref.shape[0]):
        total = total + in_ref[i].astype(F32)
    out_ref[:rows] = total[:rows]
    out_ref[rows:] = join_sums(total[rows:])


def finish_kernel(counted, scaling, x_ref, da_ref, norm_ref, sums_ref, gain_ref, out_ref, gain_grad_ref, bias_grad_ref):
    gain = gain_ref[...]
    mean = norm_ref[0:1]
    rstd = norm_ref[8:9]
    sums = sums_ref[HALF * 8 :]
    bias_grad_ref[...] = sums[0:1] * scaling
    gain_grad_ref[...] = sums[1:2] * scaling
    averages = group_total(gain * sums) / counted
    leading = averages[0:1]
    trailing = averages[1:2]
    xhat = (x_ref[...].astype(F32).reshape(-1, 128) - mean) * rstd
    grad = rstd * (da_ref[...] * gain - leading - xhat * trailing)
    out_ref[...] = grad.astype(BF16).reshape(out_ref.shape)


def join_kernel(scaling, place_ref, half_ref, other_ref, out_ref):
    left = place_ref[3] == 0
    half = half_ref[: HALF * 8] * scaling
    other = other_ref[: HALF * 8] * scaling
    out_ref[: HALF * 8] = jnp.where(left, half, other)
    out_ref[HALF * 8 :] = jnp.where(left, other, half)[: (TAPS - HALF) * 8]


def shape_of(shape, dtype=F32):
    return jax.ShapeDtypeStruct(shape, dtype)


def local(activations, group_norm_gain, group_norm_bias, upstream, kernel):
    frames, height, columns, channels = activations.shape
    n_time, n_rows, n_sect = (lax.axis_size(axis) for axis in ("tm", "rows", "sect"))
    cells = frames * height * columns
    total_cells = cells * n_time * n_rows * n_sect
    counted = float(total_cells * (channels // GROUPS))
    scaling = float(total_cells) ** (-0.5)
    tm, rows, sect = (lax.axis_index(axis) for axis in ("tm", "rows", "sect"))
    place = jnp.stack([tm, rows, jnp.int32(n_rows), sect]).astype(jnp.int32)
    swap = [(0, 1), (1, 0)]
    near = [(i, i ^ 1) for i in range(n_rows)]
    far = [(i, (i - 1) % n_rows if i % 2 == 0 else (i + 1) % n_rows) for i in range(n_rows)]

    x, up, facing, stat = call(
        entry_kernel,
        [
            shape_of(activations.shape, BF16),
            shape_of(upstream.shape, BF16),
            shape_of((528, channels), BF16),
            shape_of((8, channels)),
        ],
        [place, activations, upstream],
        [SMEM, ANY, ANY],
        [pltpu.SemaphoreType.DMA, pltpu.SemaphoreType.DMA],
    )
    side = lax.ppermute(facing, "sect", swap)
    message, stat = call(
        first_edge_kernel,
        [shape_of((208, channels), BF16), shape_of((8, channels))],
        [place, up, side, stat],
        [SMEM, VMEM, VMEM, VMEM],
    )
    nearer = lax.ppermute(message, "rows", near)
    message, stat = call(
        second_edge_kernel,
        [shape_of((208, channels), BF16), shape_of((8, channels))],
        [place, up, side, nearer, stat],
        [SMEM, VMEM, VMEM, VMEM, VMEM],
    )
    farther = lax.ppermute(message, "rows", far)
    pairs = [(0, 3), (1, 6), (2, 5), (4, 7)]
    groups = [[t * n_rows + r for t in range(n_time) for r in pair] for pair in pairs]
    early, stat = call(
        early_kernel,
        [shape_of((2, 10, 48, channels), BF16), shape_of((len(groups[0]), channels))],
        [place, up, side, nearer, farther, stat],
        [SMEM, VMEM, VMEM, VMEM, VMEM, VMEM],
    )
    later = lax.ppermute(early, "tm", [(i + 1, i) for i in range(n_time - 1)])
    stat = lax.all_to_all(stat[:, None], ("tm", "rows"), 0, 0, axis_index_groups=groups).reshape(-1, channels)
    spread, hidden_grad = call(
        grad_kernel,
        [shape_of((8, 256, 1152), BF16), shape_of((cells, channels))],
        [place, up, side, nearer, farther, later, kernel],
        [SMEM, VMEM, VMEM, VMEM, VMEM, VMEM, ANY],
        [pltpu.VMEM((3, 3, 3, 128, 128), BF16), pltpu.VMEM((3, 128, 1152), BF16), pltpu.SemaphoreType.DMA],
        flops=2 * cells * TAPS * channels * channels,
    )
    gain = group_norm_gain.reshape(1, channels)
    bias = group_norm_bias.reshape(1, channels)
    away, turned, norm, da, sums = call(
        functools.partial(away_kernel, counted),
        [
            shape_of((16, HALF, 8, 128)),
            shape_of((channels, cells), BF16),
            shape_of((16, channels)),
            shape_of((cells, channels)),
            shape_of((8, channels)),
        ],
        [place, x, stat, gain, bias, hidden_grad, spread],
        [SMEM] + [VMEM] * 6,
        flops=cells * TAPS * channels * channels,
    )
    arrived = lax.ppermute(away, "sect", swap)
    other_sums = lax.ppermute(sums, "sect", swap)
    (home,) = call(
        home_kernel,
        [shape_of((16, HALF, 8, 128))],
        [place, turned, spread],
        [SMEM, VMEM, VMEM],
        flops=cells * TAPS * channels * channels,
    )
    (sent,) = call(
        pair_kernel, [shape_of((16, SLOTS * 8, 128), BF16)], [home, arrived, sums, other_sums]
    )
    gathered = lax.all_to_all(sent, "tm", 0, 0)
    (half,) = call(share_kernel, [shape_of((SLOTS * 8, 128))], [gathered])
    for bits in (1, 2, 7):
        half = half + lax.ppermute(half, "rows", [(i, i ^ bits) for i in range(n_rows)])
    other = lax.ppermute(half, "sect", swap)
    input_gradient, gain_grad, bias_grad = call(
        functools.partial(finish_kernel, counted, scaling),
        [shape_of(activations.shape, BF16), shape_of((1, 128)), shape_of((1, 128))],
        [x, da, norm, half, gain],
    )
    (whole,) = call(
        functools.partial(join_kernel, scaling),
        [shape_of((TAPS * 8, 128))],
        [place, half, other],
        [SMEM, VMEM, VMEM],
    )
    weight_grad = whole.reshape(3, 3, 3, 8, 128).transpose(0, 1, 2, 4, 3)
    return (input_gradient, gain_grad.reshape(128), bias_grad.reshape(128), weight_grad)


def solution(mesh):
    return jax.shard_map(
        local,
        mesh=mesh,
        in_specs=(P("tm", "rows", "sect", None), P(), P(), P("tm", "rows", "sect", None), P()),
        out_specs=(P("tm", "rows", "sect", None), P(), P(), P(None, None, None, None, "tm")),
        check_vma=False,
    )
```

```python
import functools
import math

import jax
import jax.numpy as jnp
from jax import lax
from jax.experimental import pallas as pl
from jax.experimental.pallas import tpu as pltpu
from jax.sharding import PartitionSpec as P

GROUPS = 32
TAPS = 27
HALF = 14
SLOTS = HALF + 1
F32 = jnp.float32
BF16 = jnp.bfloat16
VMEM = pl.BlockSpec(memory_space=pltpu.VMEM)
SMEM = pl.BlockSpec(memory_space=pltpu.SMEM)
HBM = pl.BlockSpec(memory_space=pltpu.HBM)


def held(x, space):
    return pltpu.with_memory_space_constraint(x, space)


def call(body, outs, args, specs=None, scratch=(), flops=0, aliases=None):
    moved = sum(math.prod(x.shape) * jnp.dtype(x.dtype).itemsize for x in list(args) + list(outs))
    return pl.pallas_call(
        body,
        out_shape=outs,
        in_specs=specs or [VMEM] * len(args),
        out_specs=[VMEM] * len(outs),
        scratch_shapes=list(scratch),
        input_output_aliases=aliases or {},
        cost_estimate=pl.CostEstimate(flops=flops, bytes_accessed=moved, transcendentals=0),
        compiler_params=pltpu.CompilerParams(vmem_limit_bytes=24 * 1024 * 1024),
    )(*args)


def lanes_of(shape):
    return lax.broadcasted_iota(jnp.int32, shape, len(shape) - 1)


def sublanes_of(shape):
    return lax.broadcasted_iota(jnp.int32, shape, len(shape) - 2)


def group_total(v):
    lane = lanes_of(v.shape)
    v = v + jnp.where(lane % 2 == 0, pltpu.roll(v, 127, 1), pltpu.roll(v, 1, 1))
    return v + jnp.where(lane % 4 < 2, pltpu.roll(v, 126, 1), pltpu.roll(v, 2, 1))


def column_sum(v):
    part = jnp.sum(v.reshape(-1, 8, v.shape[-1]), axis=0)
    return jnp.broadcast_to(jnp.sum(part, axis=0, keepdims=True), part.shape)


def split_row(row):
    high = row.astype(BF16).astype(F32)
    middle = (row - high).astype(BF16).astype(F32)
    low = row - high - middle
    index = sublanes_of((8, 128))
    parts = jnp.where(index == 0, high, jnp.where(index == 1, middle, low))
    return jnp.concatenate([parts, parts], axis=0).astype(BF16)


def join_row(parts):
    parts = parts.astype(F32)
    return jnp.broadcast_to(parts[0:1] + parts[1:2] + parts[2:3], (8, 128))


def entry_kernel(place_ref, x_hbm, up_hbm, x_ref, up_ref, facing_ref, stat_ref, x_sem, up_sem):
    up_copy = pltpu.make_async_copy(up_hbm, up_ref, up_sem)
    x_copy = pltpu.make_async_copy(x_hbm, x_ref, x_sem)
    x_copy.start()
    up_copy.start()
    x_copy.wait()
    x = x_ref[...].astype(F32).reshape(-1, 128)
    total = group_total(column_sum(x))
    square = group_total(column_sum(x * x))
    row = jnp.where(lanes_of(total.shape) % 4 < 2, total, square)
    stat_ref[...] = row
    facing_ref[512:] = split_row(row)
    up_copy.wait()
    left = place_ref[3] == 0
    up = up_ref[...]
    facing_ref[:512] = jnp.where(left, up[:, :, 16:], up[:, :, :16]).reshape(512, 128)


def edge_of(up_ref, side_ref, bottom):
    side = side_ref[:512].reshape(4, 8, 16, 128)
    low = jnp.concatenate([up_ref[:, 7], side[:, 7]], axis=1)
    top = jnp.concatenate([up_ref[:, 0], side[:, 0]], axis=1)
    return jnp.where(bottom, low, top).reshape(192, 128)


def first_edge_kernel(place_ref, up_ref, side_ref, stat_ref, out_ref, sum_ref):
    even = place_ref[1] % 2 == 0
    row = stat_ref[...] + join_row(side_ref[512:])
    sum_ref[...] = row
    out_ref[:192] = edge_of(up_ref, side_ref, even)
    out_ref[192:] = split_row(row)


def second_edge_kernel(place_ref, up_ref, side_ref, near_ref, stat_ref, out_ref, sum_ref):
    even = place_ref[1] % 2 == 0
    row = stat_ref[...] + join_row(near_ref[192:])
    sum_ref[...] = row
    out_ref[:192] = edge_of(up_ref, side_ref, jnp.logical_not(even))
    out_ref[192:] = split_row(row)


def beyond(place_ref, near_ref, far_ref):
    even = place_ref[1] % 2 == 0
    outside = jnp.logical_or(place_ref[1] == 0, place_ref[1] == place_ref[2] - 1)
    near = near_ref[:192].reshape(4, 48, 128)
    far = far_ref[:192].reshape(4, 48, 128)
    far = jnp.where(outside, jnp.zeros_like(far), far)
    return jnp.where(even, far, near), jnp.where(even, near, far)


def early_kernel(place_ref, up_ref, side_ref, near_ref, far_ref, stat_ref, early_ref, sent_ref):
    row = stat_ref[...] + join_row(far_ref[192:])
    sent_ref[...] = jnp.broadcast_to(row[None], (sent_ref.shape[0] // 8, 8, 128)).reshape(sent_ref.shape)
    above, below = beyond(place_ref, near_ref, far_ref)
    early_ref[:, 0] = above[:2]
    early_ref[:, 9] = below[:2]
    early_ref[:, 1:9, :32] = up_ref[:2]
    early_ref[:, 1:9, 32:] = side_ref[:256].reshape(2, 8, 16, 128)


def column_taps(place_ref, rows):
    left = place_ref[3] == 0
    core = rows[:, :32]
    column = sublanes_of(core.shape)
    first = column == 0
    last = column == 31
    zero = jnp.zeros_like(core)
    ahead = pltpu.roll(rows, 47, 1)[:, :32]
    behind = pltpu.roll(rows, 1, 1)[:, :32]
    ahead = jnp.where(left, ahead + jnp.where(first, core, zero), jnp.where(last, zero, ahead))
    behind = jnp.where(left, jnp.where(first, zero, behind), behind + jnp.where(last, core, zero))
    return ahead, core, behind


def put(v_ref, f, r, b, e, rows):
    j = (b * 3 + e) * 128
    count = rows.shape[0]
    v_ref[f, r * 32 : (r + count) * 32, j : j + 128] = rows.astype(BF16).reshape(count * 32, 128)


def times_taps(lhs, taps_ref, a):
    return lax.dot_general(lhs, taps_ref[a], (((1,), (1,)), ((), ())), preferred_element_type=F32)


def own_kernel(place_ref, up_ref, side_ref, kernel_hbm, v_ref, dh_ref, taps_ref, kernel_ref, sem):
    weights = pltpu.make_async_copy(kernel_hbm, kernel_ref, sem)
    weights.start()
    row_first = place_ref[1] == 0
    row_last = place_ref[1] == place_ref[2] - 1
    for f in range(4):
        side = side_ref[f * 128 : (f + 1) * 128].reshape(8, 16, 128)
        rows = jnp.concatenate([up_ref[f].astype(F32), side.astype(F32)], axis=1)
        for e, part in enumerate(column_taps(place_ref, rows)):
            zero = jnp.zeros_like(part[0])
            top = part[1] + jnp.where(row_first, part[0], zero)
            low = part[6] + jnp.where(row_last, part[7], zero)
            put(v_ref, f, 0, 0, e, top[None])
            put(v_ref, f, 1, 0, e, part[2:8])
            put(v_ref, f, 0, 1, e, part)
            put(v_ref, f, 1, 2, e, part[0:6])
            put(v_ref, f, 7, 2, e, low[None])
    weights.wait()
    for a in range(3):
        for b in range(3):
            for e in range(3):
                j = (b * 3 + e) * 128
                taps_ref[a, :, j : j + 128] = kernel_ref[a, b, e]
    for f in range(4):
        total = None
        for a in range(3):
            if f + 2 - a < 4:
                term = times_taps(v_ref[f + 2 - a, 32:224], taps_ref, a)
                total = term if total is None else total + term
        dh_ref[f * 256 + 32 : f * 256 + 224] = total


def grad_kernel(place_ref, up_ref, side_ref, near_ref, far_ref, later_ref, taps_ref, part_ref, own_ref, v_ref, dh_ref):
    time_first = place_ref[0] == 0
    above, below = beyond(place_ref, near_ref, far_ref)
    row_first = place_ref[1] == 0
    row_last = place_ref[1] == place_ref[2] - 1
    outer = jnp.concatenate([above, below], axis=0).astype(F32)
    for e, part in enumerate(column_taps(place_ref, outer)):
        for f in range(4):
            put(v_ref, f, 0, 2, e, part[f : f + 1])
            put(v_ref, f, 7, 0, e, part[f + 4 : f + 5])
    for f in range(2):
        for e, part in enumerate(column_taps(place_ref, later_ref[f].astype(F32))):
            zero = jnp.zeros_like(part[0])
            top = part[2] + jnp.where(row_first, part[1], zero)
            low = part[7] + jnp.where(row_last, part[8], zero)
            put(v_ref, f + 4, 0, 0, e, top[None])
            put(v_ref, f + 4, 1, 0, e, part[3:10])
            put(v_ref, f + 4, 0, 1, e, part[1:9])
            put(v_ref, f + 4, 0, 2, e, part[0:7])
            put(v_ref, f + 4, 7, 2, e, low[None])

    def edges(lo, hi):
        return jnp.concatenate([v_ref[lo:hi, 0:32], v_ref[lo:hi, 224:256]], axis=1).reshape((hi - lo) * 64, 1152)

    outer = times_taps(edges(0, 4), taps_ref, 2)
    one = times_taps(edges(1, 4), taps_ref, 1)
    two = times_taps(edges(2, 4), taps_ref, 0)
    outer = outer + jnp.concatenate([one, jnp.zeros((64, 128), F32)], axis=0)
    outer = outer + jnp.concatenate([two, jnp.zeros((128, 128), F32)], axis=0)
    for f in range(4):
        dh_ref[f * 256 : f * 256 + 32] = outer[f * 64 : f * 64 + 32]
        dh_ref[f * 256 + 32 : f * 256 + 224] = part_ref[f * 256 + 32 : f * 256 + 224]
        dh_ref[f * 256 + 224 : f * 256 + 256] = outer[f * 64 + 32 : f * 64 + 64]
    dh_ref[768:1024] += times_taps(v_ref[4], taps_ref, 1)
    dh_ref[512:1024] += times_taps(v_ref[4:6].reshape(512, 1152), taps_ref, 0)

    @pl.when(time_first)
    def _():
        both = v_ref[1].astype(F32) + v_ref[0].astype(F32)
        v_ref[6] = both.astype(BF16)
        v_ref[7] = (both + v_ref[2].astype(F32)).astype(BF16)
        dh_ref[0:256] += times_taps(v_ref[0], taps_ref, 1) + times_taps(v_ref[6], taps_ref, 0)


def sums_to_pair(row):
    lane = lanes_of(row.shape)
    total = jnp.where(lane % 4 < 2, row, pltpu.roll(row, 2, 1))
    square = jnp.where(lane % 4 < 2, pltpu.roll(row, 126, 1), row)
    return total, square


def product_of(place_ref, turned, v_ref, a, lo, hi):
    if a == 2:
        return jnp.dot(turned, v_ref[0:4, :, lo:hi].reshape(1024, hi - lo), preferred_element_type=F32)
    source = jnp.where(place_ref[0] == 0, 7 - a, 2 - a)
    first = jnp.dot(turned[:, :256], v_ref[source, :, lo:hi], preferred_element_type=F32)
    rest = v_ref[3 - a : 6 - a, :, lo:hi].reshape(768, hi - lo)
    return first + jnp.dot(turned[:, 256:], rest, preferred_element_type=F32)


def half_product(place_ref, half, turned, v_ref, w_ref):
    for a, lo, hi in (((0, 0, 9), (1, 0, 5)), ((1, 5, 9), (2, 0, 9)))[half]:
        product = product_of(place_ref, turned, v_ref, a, lo * 128, hi * 128)
        for j in range(lo, hi):
            block = product[:, (j - lo) * 128 : (j - lo + 1) * 128].T.reshape(16, 8, 128)
            w_ref[:, (a * 9 + j) % HALF] = block
    if half == 1:
        w_ref[:, HALF - 1] = jnp.zeros((16, 8, 128), F32)


def away_kernel(
    counted, place_ref, x_ref, stat_ref, gain_ref, bias_ref, dh_ref, v_ref, w_ref, turned_ref, norm_ref, da_ref, sums_ref
):
    total, square = sums_to_pair(column_sum(stat_ref[...]))
    mean = total / counted
    rstd = lax.rsqrt(square / counted - mean * mean + 1e-06)
    norm_ref[0:8] = mean
    norm_ref[8:16] = rstd
    mean, rstd = mean[:1], rstd[:1]
    gain = gain_ref[...]
    bias = bias_ref[...]
    bias_sum = jnp.zeros((8, 128), F32)
    gain_sum = jnp.zeros((8, 128), F32)
    for block in range(8):
        xhat = (x_ref[block // 2, (block % 2) * 4 : (block % 2) * 4 + 4].astype(F32).reshape(128, 128) - mean) * rstd
        pre = xhat * gain + bias
        sig = 1.0 / (1.0 + jnp.exp(-pre))
        turned_ref[:, block * 128 : (block + 1) * 128] = (pre * sig).T.astype(BF16)
        da = dh_ref[block * 128 : (block + 1) * 128] * sig * (1.0 + pre * (1.0 - sig))
        da_ref[block * 128 : (block + 1) * 128] = da
        bias_sum = bias_sum + jnp.sum(da.reshape(16, 8, 128), axis=0)
        gain_sum = gain_sum + jnp.sum((da * xhat).reshape(16, 8, 128), axis=0)
    sums_ref[...] = jnp.where(sublanes_of((8, 128)) == 0, column_sum(bias_sum), column_sum(gain_sum))
    left = place_ref[3] == 0

    @pl.when(left)
    def _():
        half_product(place_ref, 1, turned_ref[...], v_ref, w_ref)

    @pl.when(jnp.logical_not(left))
    def _():
        half_product(place_ref, 0, turned_ref[...], v_ref, w_ref)


def home_kernel(place_ref, turned_ref, v_ref, w_ref):
    left = place_ref[3] == 0

    @pl.when(left)
    def _():
        half_product(place_ref, 0, turned_ref[...], v_ref, w_ref)

    @pl.when(jnp.logical_not(left))
    def _():
        half_product(place_ref, 1, turned_ref[...], v_ref, w_ref)


def split_sums(sums):
    row = sublanes_of(sums.shape)
    high = sums.astype(BF16).astype(F32)
    middle = (sums - high).astype(BF16).astype(F32)
    low = sums - high - middle
    return jnp.where(
        row < 2, high, jnp.where(row < 4, pltpu.roll(middle, 2, 0), pltpu.roll(low, 4, 0))
    )


def join_sums(parts):
    return parts + pltpu.roll(parts, 6, 0) + pltpu.roll(parts, 4, 0)


def pair_kernel(own_ref, other_ref, sums_ref, other_sums_ref, out_ref):
    slot = split_sums(sums_ref[...] + other_sums_ref[...])
    for i in range(16):
        body = (own_ref[i] + other_ref[i]).reshape(HALF * 8, 128)
        out_ref[i] = jnp.concatenate([body, slot], axis=0).astype(BF16)


def share_kernel(in_ref, out_ref):
    rows = HALF * 8
    total = in_ref[0].astype(F32)
    for i in range(1, in_ref.shape[0]):
        total = total + in_ref[i].astype(F32)
    out_ref[:rows] = total[:rows]
    out_ref[rows:] = join_sums(total[rows:])


def finish_kernel(counted, scaling, x_ref, da_ref, norm_ref, sums_ref, gain_ref, out_ref, gain_grad_ref, bias_grad_ref):
    gain = gain_ref[...]
    mean = norm_ref[0:1]
    rstd = norm_ref[8:9]
    sums = sums_ref[HALF * 8 :]
    bias_grad_ref[...] = sums[0:1] * scaling
    gain_grad_ref[...] = sums[1:2] * scaling
    averages = group_total(gain * sums) / counted
    leading = averages[0:1]
    trailing = averages[1:2]
    xhat = (x_ref[...].astype(F32).reshape(-1, 128) - mean) * rstd
    grad = rstd * (da_ref[...] * gain - leading - xhat * trailing)
    out_ref[...] = grad.astype(BF16).reshape(out_ref.shape)


def join_kernel(scaling, place_ref, half_ref, other_ref, out_ref):
    left = place_ref[3] == 0
    half = half_ref[: HALF * 8] * scaling
    other = other_ref[: HALF * 8] * scaling
    out_ref[: HALF * 8] = jnp.where(left, half, other)
    out_ref[HALF * 8 :] = jnp.where(left, other, half)[: (TAPS - HALF) * 8]


def shape_of(shape, dtype=F32):
    return jax.ShapeDtypeStruct(shape, dtype)


def local(activations, group_norm_gain, group_norm_bias, upstream, kernel):
    frames, height, columns, channels = activations.shape
    n_time, n_rows, n_sect = (lax.axis_size(axis) for axis in ("tm", "rows", "sect"))
    cells = frames * height * columns
    total_cells = cells * n_time * n_rows * n_sect
    counted = float(total_cells * (channels // GROUPS))
    scaling = float(total_cells) ** (-0.5)
    tm, rows, sect = (lax.axis_index(axis) for axis in ("tm", "rows", "sect"))
    place = jnp.stack([tm, rows, jnp.int32(n_rows), sect]).astype(jnp.int32)
    swap = [(0, 1), (1, 0)]
    near = [(i, i ^ 1) for i in range(n_rows)]
    far = [(i, (i - 1) % n_rows if i % 2 == 0 else (i + 1) % n_rows) for i in range(n_rows)]

    x, up, facing, stat = call(
        entry_kernel,
        [
            shape_of(activations.shape, BF16),
            shape_of(upstream.shape, BF16),
            shape_of((528, channels), BF16),
            shape_of((8, channels)),
        ],
        [place, held(activations, pltpu.HBM), held(upstream, pltpu.HBM)],
        [SMEM, HBM, HBM],
        [pltpu.SemaphoreType.DMA, pltpu.SemaphoreType.DMA],
    )
    side = lax.ppermute(facing, "sect", swap)
    message, stat = call(
        first_edge_kernel,
        [shape_of((208, channels), BF16), shape_of((8, channels))],
        [place, up, side, stat],
        [SMEM, VMEM, VMEM, VMEM],
    )
    nearer = lax.ppermute(message, "rows", near)
    spread, inner, taps = call(
        own_kernel,
        [
            pltpu.VMEM((8, 256, 1152), BF16),
            shape_of((cells, channels)),
            shape_of((3, channels, 9 * channels), BF16),
        ],
        [place, up, side, held(kernel, pltpu.HBM)],
        [SMEM, VMEM, VMEM, HBM],
        [pltpu.VMEM((3, 3, 3, 128, 128), BF16), pltpu.SemaphoreType.DMA],
        flops=cells * TAPS * channels * channels,
    )
    nearer, inner = lax.optimization_barrier((nearer, inner))
    message, stat = call(
        second_edge_kernel,
        [shape_of((208, channels), BF16), shape_of((8, channels))],
        [place, up, side, nearer, stat],
        [SMEM, VMEM, VMEM, VMEM, VMEM],
    )
    farther = lax.ppermute(message, "rows", far)
    pairs = [(0, 3), (1, 6), (2, 5), (4, 7)]
    groups = [[t * n_rows + r for t in range(n_time) for r in pair] for pair in pairs]
    early, stat = call(
        early_kernel,
        [shape_of((2, 10, 48, channels), BF16), shape_of((len(groups[0]), channels))],
        [place, up, side, nearer, farther, stat],
        [SMEM, VMEM, VMEM, VMEM, VMEM, VMEM],
    )
    later = lax.ppermute(early, "tm", [(i + 1, i) for i in range(n_time - 1)])
    stat = lax.all_to_all(stat[:, None], ("tm", "rows"), 0, 0, axis_index_groups=groups).reshape(-1, channels)
    stat, later = lax.optimization_barrier((stat, later))
    spread, hidden_grad = call(
        grad_kernel,
        [pltpu.VMEM((8, 256, 1152), BF16), shape_of((cells, channels))],
        [place, up, side, nearer, farther, later, taps, inner, held(spread, pltpu.VMEM)],
        [SMEM] + [VMEM] * 8,
        flops=cells * TAPS * channels * channels,
        aliases={8: 0},
    )
    gain = group_norm_gain.reshape(1, channels)
    bias = group_norm_bias.reshape(1, channels)
    away, turned, norm, da, sums = call(
        functools.partial(away_kernel, counted),
        [
            shape_of((16, HALF, 8, 128)),
            shape_of((channels, cells), BF16),
            shape_of((16, channels)),
            shape_of((cells, channels)),
            shape_of((8, channels)),
        ],
        [place, x, stat, gain, bias, hidden_grad, held(spread, pltpu.VMEM)],
        [SMEM] + [VMEM] * 6,
        flops=cells * TAPS * channels * channels,
    )
    arrived = lax.ppermute(away, "sect", swap)
    other_sums = lax.ppermute(sums, "sect", swap)
    (home,) = call(
        home_kernel,
        [shape_of((16, HALF, 8, 128))],
        [place, turned, held(spread, pltpu.VMEM)],
        [SMEM, VMEM, VMEM],
        flops=cells * TAPS * channels * channels,
    )
    (sent,) = call(
        pair_kernel, [shape_of((16, SLOTS * 8, 128), BF16)], [home, arrived, sums, other_sums]
    )
    gathered = lax.all_to_all(sent, "tm", 0, 0)
    (half,) = call(share_kernel, [shape_of((SLOTS * 8, 128))], [gathered])
    for bits in (1, 2, 7):
        half = half + lax.ppermute(half, "rows", [(i, i ^ bits) for i in range(n_rows)])
    other = lax.ppermute(half, "sect", swap)
    input_gradient, gain_grad, bias_grad = call(
        functools.partial(finish_kernel, counted, scaling),
        [shape_of(activations.shape, BF16), shape_of((1, 128)), shape_of((1, 128))],
        [x, da, norm, half, gain],
    )
    (whole,) = call(
        functools.partial(join_kernel, scaling),
        [shape_of((TAPS * 8, 128))],
        [place, half, other],
        [SMEM, VMEM, VMEM],
    )
    weight_grad = whole.reshape(3, 3, 3, 8, 128).transpose(0, 1, 2, 4, 3)
    return (input_gradient, gain_grad.reshape(128), bias_grad.reshape(128), weight_grad)


def solution(mesh):
    return jax.shard_map(
        local,
        mesh=mesh,
        in_specs=(P("tm", "rows", "sect", None), P(), P(), P("tm", "rows", "sect", None), P()),
        out_specs=(P("tm", "rows", "sect", None), P(), P(), P(None, None, None, None, "tm")),
        check_vma=False,
    )
```

```python
import functools
import math

import jax
import jax.numpy as jnp
from jax import lax
from jax.experimental import pallas as pl
from jax.experimental.pallas import tpu as pltpu
from jax.sharding import PartitionSpec as P

GROUPS = 32
TAPS = 27
HALF = 14
SLOTS = HALF + 1
F32 = jnp.float32
BF16 = jnp.bfloat16
VMEM = pl.BlockSpec(memory_space=pltpu.VMEM)
HBM = pl.BlockSpec(memory_space=pltpu.HBM)


def held(x, space):
    return pltpu.with_memory_space_constraint(x, space)


def call(body, outs, args, specs=None, scratch=(), flops=0, aliases=None):
    moved = sum(math.prod(x.shape) * jnp.dtype(x.dtype).itemsize for x in list(args) + list(outs))
    return pl.pallas_call(
        body,
        out_shape=outs,
        in_specs=specs or [VMEM] * len(args),
        out_specs=[VMEM] * len(outs),
        scratch_shapes=list(scratch),
        input_output_aliases=aliases or {},
        cost_estimate=pl.CostEstimate(flops=flops, bytes_accessed=moved, transcendentals=0),
        compiler_params=pltpu.CompilerParams(vmem_limit_bytes=24 * 1024 * 1024),
    )(*args)


def lanes_of(shape):
    return lax.broadcasted_iota(jnp.int32, shape, len(shape) - 1)


def sublanes_of(shape):
    return lax.broadcasted_iota(jnp.int32, shape, len(shape) - 2)


def group_total(v):
    lane = lanes_of(v.shape)
    v = v + jnp.where(lane % 2 == 0, pltpu.roll(v, 127, 1), pltpu.roll(v, 1, 1))
    return v + jnp.where(lane % 4 < 2, pltpu.roll(v, 126, 1), pltpu.roll(v, 2, 1))


def column_sum(v):
    part = jnp.sum(v.reshape(-1, 8, v.shape[-1]), axis=0)
    return jnp.broadcast_to(jnp.sum(part, axis=0, keepdims=True), part.shape)


def split_row(row):
    high = row.astype(BF16).astype(F32)
    middle = (row - high).astype(BF16).astype(F32)
    low = row - high - middle
    index = sublanes_of((8, 128))
    parts = jnp.where(index == 0, high, jnp.where(index == 1, middle, low))
    return jnp.concatenate([parts, parts], axis=0).astype(BF16)


def join_row(parts):
    parts = parts.astype(F32)
    return jnp.broadcast_to(parts[0:1] + parts[1:2] + parts[2:3], (8, 128))


def entry_kernel(x_hbm, up_hbm, x_ref, up_ref, facing_ref, stat_ref, x_sem, up_sem):
    up_copy = pltpu.make_async_copy(up_hbm, up_ref, up_sem)
    x_copy = pltpu.make_async_copy(x_hbm, x_ref, x_sem)
    x_copy.start()
    up_copy.start()
    x_copy.wait()
    x = x_ref[...].astype(F32).reshape(-1, 128)
    total = group_total(column_sum(x))
    square = group_total(column_sum(x * x))
    row = jnp.where(lanes_of(total.shape) % 4 < 2, total, square)
    stat_ref[...] = row
    facing_ref[512:] = split_row(row)
    up_copy.wait()
    left = lax.axis_index("sect") == 0
    up = up_ref[...]
    facing_ref[:512] = jnp.where(left, up[:, :, 16:], up[:, :, :16]).reshape(512, 128)


def edge_of(up_ref, side_ref, bottom):
    side = side_ref[:512].reshape(4, 8, 16, 128)
    low = jnp.concatenate([up_ref[:, 7], side[:, 7]], axis=1)
    top = jnp.concatenate([up_ref[:, 0], side[:, 0]], axis=1)
    return jnp.where(bottom, low, top).reshape(192, 128)


def first_edge_kernel(up_ref, side_ref, stat_ref, out_ref, sum_ref):
    even = lax.axis_index("rows") % 2 == 0
    row = stat_ref[...] + join_row(side_ref[512:])
    sum_ref[...] = row
    out_ref[:192] = edge_of(up_ref, side_ref, even)
    out_ref[192:] = split_row(row)


def second_edge_kernel(up_ref, side_ref, near_ref, stat_ref, out_ref, sum_ref):
    even = lax.axis_index("rows") % 2 == 0
    row = stat_ref[...] + join_row(near_ref[192:])
    sum_ref[...] = row
    out_ref[:192] = edge_of(up_ref, side_ref, jnp.logical_not(even))
    out_ref[192:] = split_row(row)


def beyond(near_ref, far_ref):
    even = lax.axis_index("rows") % 2 == 0
    outside = jnp.logical_or(lax.axis_index("rows") == 0, lax.axis_index("rows") == lax.axis_size("rows") - 1)
    near = near_ref[:192].reshape(4, 48, 128)
    far = far_ref[:192].reshape(4, 48, 128)
    far = jnp.where(outside, jnp.zeros_like(far), far)
    return jnp.where(even, far, near), jnp.where(even, near, far)


def early_kernel(up_ref, side_ref, near_ref, far_ref, stat_ref, early_ref, sent_ref):
    row = stat_ref[...] + join_row(far_ref[192:])
    sent_ref[...] = jnp.broadcast_to(row[None], (sent_ref.shape[0] // 8, 8, 128)).reshape(sent_ref.shape)
    above, below = beyond(near_ref, far_ref)
    early_ref[:, 0] = above[:2]
    early_ref[:, 9] = below[:2]
    early_ref[:, 1:9, :32] = up_ref[:2]
    early_ref[:, 1:9, 32:] = side_ref[:256].reshape(2, 8, 16, 128)


def column_taps(rows):
    left = lax.axis_index("sect") == 0
    core = rows[:, :32]
    column = sublanes_of(core.shape)
    first = column == 0
    last = column == 31
    zero = jnp.zeros_like(core)
    ahead = pltpu.roll(rows, 47, 1)[:, :32]
    behind = pltpu.roll(rows, 1, 1)[:, :32]
    ahead = jnp.where(left, ahead + jnp.where(first, core, zero), jnp.where(last, zero, ahead))
    behind = jnp.where(left, jnp.where(first, zero, behind), behind + jnp.where(last, core, zero))
    return ahead, core, behind


def put(v_ref, f, r, b, e, rows):
    j = (b * 3 + e) * 128
    count = rows.shape[0]
    v_ref[f, r * 32 : (r + count) * 32, j : j + 128] = rows.astype(BF16).reshape(count * 32, 128)


def times_taps(lhs, taps_ref, a):
    return lax.dot_general(lhs, taps_ref[a], (((1,), (1,)), ((), ())), preferred_element_type=F32)


def own_kernel(up_ref, side_ref, kernel_hbm, v_ref, dh_ref, taps_ref, kernel_ref, sem):
    weights = pltpu.make_async_copy(kernel_hbm, kernel_ref, sem)
    weights.start()
    row_first = lax.axis_index("rows") == 0
    row_last = lax.axis_index("rows") == lax.axis_size("rows") - 1
    for f in range(4):
        side = side_ref[f * 128 : (f + 1) * 128].reshape(8, 16, 128)
        rows = jnp.concatenate([up_ref[f].astype(F32), side.astype(F32)], axis=1)
        for e, part in enumerate(column_taps(rows)):
            zero = jnp.zeros_like(part[0])
            top = part[1] + jnp.where(row_first, part[0], zero)
            low = part[6] + jnp.where(row_last, part[7], zero)
            put(v_ref, f, 0, 0, e, top[None])
            put(v_ref, f, 1, 0, e, part[2:8])
            put(v_ref, f, 0, 1, e, part)
            put(v_ref, f, 1, 2, e, part[0:6])
            put(v_ref, f, 7, 2, e, low[None])
    weights.wait()
    for a in range(3):
        for b in range(3):
            for e in range(3):
                j = (b * 3 + e) * 128
                taps_ref[a, :, j : j + 128] = kernel_ref[a, b, e]
    for f in range(4):
        total = None
        for a in range(3):
            if f + 2 - a < 4:
                term = times_taps(v_ref[f + 2 - a, 32:224], taps_ref, a)
                total = term if total is None else total + term
        dh_ref[f * 256 + 32 : f * 256 + 224] = total


def spread_kernel(near_ref, far_ref, later_ref, own_ref, v_ref):
    above, below = beyond(near_ref, far_ref)
    row_first = lax.axis_index("rows") == 0
    row_last = lax.axis_index("rows") == lax.axis_size("rows") - 1
    outer = jnp.concatenate([above, below], axis=0).astype(F32)
    for e, part in enumerate(column_taps(outer)):
        for f in range(4):
            put(v_ref, f, 0, 2, e, part[f : f + 1])
            put(v_ref, f, 7, 0, e, part[f + 4 : f + 5])
    for f in range(2):
        for e, part in enumerate(column_taps(later_ref[f].astype(F32))):
            zero = jnp.zeros_like(part[0])
            top = part[2] + jnp.where(row_first, part[1], zero)
            low = part[7] + jnp.where(row_last, part[8], zero)
            put(v_ref, f + 4, 0, 0, e, top[None])
            put(v_ref, f + 4, 1, 0, e, part[3:10])
            put(v_ref, f + 4, 0, 1, e, part[1:9])
            put(v_ref, f + 4, 0, 2, e, part[0:7])
            put(v_ref, f + 4, 7, 2, e, low[None])

    @pl.when(lax.axis_index("tm") == 0)
    def _():
        both = v_ref[1].astype(F32) + v_ref[0].astype(F32)
        v_ref[6] = both.astype(BF16)
        v_ref[7] = (both + v_ref[2].astype(F32)).astype(BF16)


def grad_kernel(x_ref, norm_ref, gain_ref, bias_ref, taps_ref, part_ref, v_ref, da_ref, sums_ref, dh_ref):
    def edges(lo, hi):
        return jnp.concatenate([v_ref[lo:hi, 0:32], v_ref[lo:hi, 224:256]], axis=1).reshape((hi - lo) * 64, 1152)

    outer = times_taps(edges(0, 4), taps_ref, 2)
    one = times_taps(edges(1, 4), taps_ref, 1)
    two = times_taps(edges(2, 4), taps_ref, 0)
    outer = outer + jnp.concatenate([one, jnp.zeros((64, 128), F32)], axis=0)
    outer = outer + jnp.concatenate([two, jnp.zeros((128, 128), F32)], axis=0)
    for f in range(4):
        dh_ref[f * 256 : f * 256 + 32] = outer[f * 64 : f * 64 + 32]
        dh_ref[f * 256 + 32 : f * 256 + 224] = part_ref[f * 256 + 32 : f * 256 + 224]
        dh_ref[f * 256 + 224 : f * 256 + 256] = outer[f * 64 + 32 : f * 64 + 64]
    dh_ref[768:1024] += times_taps(v_ref[4], taps_ref, 1)
    dh_ref[512:1024] += times_taps(v_ref[4:6].reshape(512, 1152), taps_ref, 0)

    @pl.when(lax.axis_index("tm") == 0)
    def _():
        dh_ref[0:256] += times_taps(v_ref[0], taps_ref, 1) + times_taps(v_ref[6], taps_ref, 0)

    bias_sum = jnp.zeros((8, 128), F32)
    gain_sum = jnp.zeros((8, 128), F32)
    for block in range(8):
        xhat, pre = block_of(x_ref, norm_ref, gain_ref, bias_ref, block)
        sig = 1.0 / (1.0 + jnp.exp(-pre))
        da = dh_ref[block * 128 : (block + 1) * 128] * sig * (1.0 + pre * (1.0 - sig))
        da_ref[block * 128 : (block + 1) * 128] = da
        bias_sum = bias_sum + jnp.sum(da.reshape(16, 8, 128), axis=0)
        gain_sum = gain_sum + jnp.sum((da * xhat).reshape(16, 8, 128), axis=0)
    sums_ref[...] = jnp.where(sublanes_of((8, 128)) == 0, column_sum(bias_sum), column_sum(gain_sum))


def sums_to_pair(row):
    lane = lanes_of(row.shape)
    total = jnp.where(lane % 4 < 2, row, pltpu.roll(row, 2, 1))
    square = jnp.where(lane % 4 < 2, pltpu.roll(row, 126, 1), row)
    return total, square


def product_of(turned, v_ref, a, lo, hi):
    if a == 2:
        return jnp.dot(turned, v_ref[0:4, :, lo:hi].reshape(1024, hi - lo), preferred_element_type=F32)
    source = jnp.where(lax.axis_index("tm") == 0, 7 - a, 2 - a)
    first = jnp.dot(turned[:, :256], v_ref[source, :, lo:hi], preferred_element_type=F32)
    rest = v_ref[3 - a : 6 - a, :, lo:hi].reshape(768, hi - lo)
    return first + jnp.dot(turned[:, 256:], rest, preferred_element_type=F32)


def half_product(half, turned, v_ref, w_ref):
    for a, lo, hi in (((0, 0, 9), (1, 0, 5)), ((1, 5, 9), (2, 0, 9)))[half]:
        product = product_of(turned, v_ref, a, lo * 128, hi * 128)
        for j in range(lo, hi):
            block = product[:, (j - lo) * 128 : (j - lo + 1) * 128].T.reshape(16, 8, 128)
            w_ref[:, (a * 9 + j) % HALF] = block
    if half == 1:
        w_ref[:, HALF - 1] = jnp.zeros((16, 8, 128), F32)


def block_of(x_ref, norm_ref, gain_ref, bias_ref, block):
    half = (block % 2) * 4
    x = x_ref[block // 2, half : half + 4].astype(F32).reshape(128, 128)
    xhat = (x - norm_ref[0:1]) * norm_ref[8:9]
    return xhat, xhat * gain_ref[...] + bias_ref[...]


def away_kernel(counted, x_ref, stat_ref, gain_ref, bias_ref, v_ref, w_ref, turned_ref, norm_ref):
    total, square = sums_to_pair(column_sum(stat_ref[...]))
    mean = total / counted
    norm_ref[0:8] = mean
    norm_ref[8:16] = lax.rsqrt(square / counted - mean * mean + 1e-06)
    for block in range(8):
        _, pre = block_of(x_ref, norm_ref, gain_ref, bias_ref, block)
        hidden = pre * (1.0 / (1.0 + jnp.exp(-pre)))
        turned_ref[:, block * 128 : (block + 1) * 128] = hidden.T.astype(BF16)
    left = lax.axis_index("sect") == 0

    @pl.when(left)
    def _():
        half_product(1, turned_ref[...], v_ref, w_ref)

    @pl.when(jnp.logical_not(left))
    def _():
        half_product(0, turned_ref[...], v_ref, w_ref)


def home_kernel(turned_ref, v_ref, w_ref):
    left = lax.axis_index("sect") == 0

    @pl.when(left)
    def _():
        half_product(0, turned_ref[...], v_ref, w_ref)

    @pl.when(jnp.logical_not(left))
    def _():
        half_product(1, turned_ref[...], v_ref, w_ref)


def split_sums(sums):
    row = sublanes_of(sums.shape)
    high = sums.astype(BF16).astype(F32)
    middle = (sums - high).astype(BF16).astype(F32)
    low = sums - high - middle
    return jnp.where(
        row < 2, high, jnp.where(row < 4, pltpu.roll(middle, 2, 0), pltpu.roll(low, 4, 0))
    )


def join_sums(parts):
    return parts + pltpu.roll(parts, 6, 0) + pltpu.roll(parts, 4, 0)


def pair_kernel(own_ref, other_ref, sums_ref, other_sums_ref, out_ref):
    slot = split_sums(sums_ref[...] + other_sums_ref[...])
    for i in range(16):
        body = (own_ref[i] + other_ref[i]).reshape(HALF * 8, 128)
        out_ref[i] = jnp.concatenate([body, slot], axis=0).astype(BF16)


def power_for(values):
    most = jnp.max(jnp.max(jnp.abs(values), axis=0, keepdims=True), axis=1, keepdims=True)
    bits = jnp.log(jnp.maximum(most, 1e-30)) * 1.4426950408889634
    return jnp.clip(jnp.floor(14.0 - bits), -100.0, 100.0)


def share_kernel(in_ref, out_ref):
    rows = HALF * 8
    total = in_ref[0].astype(F32)
    for i in range(1, in_ref.shape[0]):
        total = total + in_ref[i].astype(F32)
    body = total[:rows]
    sums = join_sums(total[rows:])
    index = sublanes_of(sums.shape)
    sums = jnp.where(index < 2, sums, jnp.zeros_like(sums))
    power = power_for(body)
    power_of_sums = power_for(sums)
    slot = split_sums(sums * jnp.exp2(power_of_sums))
    slot = jnp.where(index == 6, power, jnp.where(index == 7, power_of_sums, slot))
    out_ref[:rows] = body * jnp.exp2(power)
    out_ref[rows:] = slot


def last_sum_kernel(scaling, in_ref, half_ref, sums_ref):
    rows = HALF * 8
    total = jnp.zeros((rows, 128), F32)
    sums = jnp.zeros((8, 128), F32)
    for i in range(in_ref.shape[0]):
        slot = in_ref[i, rows:]
        total = total + in_ref[i, :rows] * jnp.exp2(-slot[6:7])
        sums = sums + join_sums(slot) * jnp.exp2(-slot[7:8])
    half_ref[...] = total * scaling
    sums_ref[...] = sums


def finish_kernel(counted, scaling, x_ref, da_ref, norm_ref, sums_ref, gain_ref, out_ref, gain_grad_ref, bias_grad_ref):
    gain = gain_ref[...]
    mean = norm_ref[0:1]
    rstd = norm_ref[8:9]
    sums = sums_ref[...]
    bias_grad_ref[...] = sums[0:1] * scaling
    gain_grad_ref[...] = sums[1:2] * scaling
    averages = group_total(gain * sums) / counted
    leading = averages[0:1]
    trailing = averages[1:2]
    xhat = (x_ref[...].astype(F32).reshape(-1, 128) - mean) * rstd
    grad = rstd * (da_ref[...] * gain - leading - xhat * trailing)
    out_ref[...] = grad.astype(BF16).reshape(out_ref.shape)


def join_kernel(half_ref, other_ref, out_ref):
    left = lax.axis_index("sect") == 0
    half = half_ref[...]
    other = other_ref[...]
    out_ref[: HALF * 8] = jnp.where(left, half, other)
    out_ref[HALF * 8 :] = jnp.where(left, other, half)[: (TAPS - HALF) * 8]


def shape_of(shape, dtype=F32):
    return jax.ShapeDtypeStruct(shape, dtype)


def local(activations, group_norm_gain, group_norm_bias, upstream, kernel):
    frames, height, columns, channels = activations.shape
    n_time, n_rows, n_sect = (lax.axis_size(axis) for axis in ("tm", "rows", "sect"))
    cells = frames * height * columns
    total_cells = cells * n_time * n_rows * n_sect
    counted = float(total_cells * (channels // GROUPS))
    scaling = float(total_cells) ** (-0.5)
    swap = [(0, 1), (1, 0)]
    near = [(i, i ^ 1) for i in range(n_rows)]
    far = [(i, (i - 1) % n_rows if i % 2 == 0 else (i + 1) % n_rows) for i in range(n_rows)]

    x, up, facing, stat = call(
        entry_kernel,
        [
            shape_of(activations.shape, BF16),
            shape_of(upstream.shape, BF16),
            shape_of((528, channels), BF16),
            shape_of((8, channels)),
        ],
        [held(activations, pltpu.HBM), held(upstream, pltpu.HBM)],
        [HBM, HBM],
        [pltpu.SemaphoreType.DMA, pltpu.SemaphoreType.DMA],
    )
    side = lax.ppermute(facing, "sect", swap)
    message, stat = call(
        first_edge_kernel,
        [shape_of((208, channels), BF16), shape_of((8, channels))],
        [up, side, stat],
        [VMEM, VMEM, VMEM],
    )
    nearer = lax.ppermute(message, "rows", near)
    spread, inner, taps = call(
        own_kernel,
        [
            pltpu.VMEM((8, 256, 1152), BF16),
            shape_of((cells, channels)),
            shape_of((3, channels, 9 * channels), BF16),
        ],
        [up, side, held(kernel, pltpu.HBM)],
        [VMEM, VMEM, HBM],
        [pltpu.VMEM((3, 3, 3, 128, 128), BF16), pltpu.SemaphoreType.DMA],
        flops=cells * TAPS * channels * channels,
    )
    nearer, inner = lax.optimization_barrier((nearer, inner))
    message, stat = call(
        second_edge_kernel,
        [shape_of((208, channels), BF16), shape_of((8, channels))],
        [up, side, nearer, stat],
        [VMEM, VMEM, VMEM, VMEM],
    )
    farther = lax.ppermute(message, "rows", far)
    pairs = [(0, 3), (1, 6), (2, 5), (4, 7)]
    groups = [[t * n_rows + r for t in range(n_time) for r in pair] for pair in pairs]
    early, stat = call(
        early_kernel,
        [shape_of((2, 10, 48, channels), BF16), shape_of((len(groups[0]), channels))],
        [up, side, nearer, farther, stat],
        [VMEM, VMEM, VMEM, VMEM, VMEM],
    )
    later = lax.ppermute(early, "tm", [(i + 1, i) for i in range(n_time - 1)])
    stat = lax.all_to_all(stat[:, None], ("tm", "rows"), 0, 0, axis_index_groups=groups).reshape(-1, channels)
    stat, later = lax.optimization_barrier((stat, later))
    (spread,) = call(
        spread_kernel,
        [pltpu.VMEM((8, 256, 1152), BF16)],
        [nearer, farther, later, held(spread, pltpu.VMEM)],
        aliases={3: 0},
    )
    gain = group_norm_gain.reshape(1, channels)
    bias = group_norm_bias.reshape(1, channels)
    away, turned, norm = call(
        functools.partial(away_kernel, counted),
        [shape_of((16, HALF, 8, 128)), shape_of((channels, cells), BF16), shape_of((16, channels))],
        [x, stat, gain, bias, held(spread, pltpu.VMEM)],
        flops=cells * TAPS * channels * channels,
    )
    arrived = lax.ppermute(away, "sect", swap)
    da, sums = call(
        grad_kernel,
        [shape_of((cells, channels)), shape_of((8, channels))],
        [x, norm, gain, bias, taps, inner, held(spread, pltpu.VMEM)],
        scratch=[pltpu.VMEM((cells, channels), F32)],
        flops=cells * TAPS * channels * channels,
    )
    other_sums = lax.ppermute(sums, "sect", swap)
    (home,) = call(
        home_kernel,
        [shape_of((16, HALF, 8, 128))],
        [turned, held(spread, pltpu.VMEM)],
        flops=cells * TAPS * channels * channels,
    )
    (sent,) = call(
        pair_kernel, [shape_of((16, SLOTS * 8, 128), BF16)], [home, arrived, sums, other_sums]
    )
    gathered = lax.all_to_all(sent, "tm", 0, 0)
    (share,) = call(share_kernel, [shape_of((SLOTS * 8, 128))], [gathered])
    share = jnp.broadcast_to(share.astype(jnp.float16)[None], (n_rows, SLOTS * 8, 128))
    shares = lax.all_to_all(share, "rows", 0, 0).astype(F32)
    half, sums = call(
        functools.partial(last_sum_kernel, scaling),
        [shape_of((HALF * 8, 128)), shape_of((8, 128))],
        [shares],
    )
    other = lax.ppermute(half, "sect", swap)
    input_gradient, gain_grad, bias_grad = call(
        functools.partial(finish_kernel, counted, scaling),
        [shape_of(activations.shape, BF16), shape_of((1, 128)), shape_of((1, 128))],
        [x, da, norm, sums, gain],
    )
    (whole,) = call(join_kernel, [shape_of((TAPS * 8, 128))], [half, other])
    weight_grad = whole.reshape(3, 3, 3, 8, 128).transpose(0, 1, 2, 4, 3)
    return (input_gradient, gain_grad.reshape(128), bias_grad.reshape(128), weight_grad)


def solution(mesh):
    return jax.shard_map(
        local,
        mesh=mesh,
        in_specs=(P("tm", "rows", "sect", None), P(), P(), P("tm", "rows", "sect", None), P()),
        out_specs=(P("tm", "rows", "sect", None), P(), P(), P(None, None, None, None, "tm")),
        check_vma=False,
    )
```

```python
import functools
import math

import jax
import jax.numpy as jnp
from jax import lax
from jax.experimental import pallas as pl
from jax.experimental.pallas import tpu as pltpu
from jax.sharding import PartitionSpec as P

GROUPS = 32
TAPS = 27
HALF = 14
SLOTS = HALF + 1
F32 = jnp.float32
BF16 = jnp.bfloat16
VMEM = pl.BlockSpec(memory_space=pltpu.VMEM)
HBM = pl.BlockSpec(memory_space=pltpu.HBM)


def held(x, space):
    return pltpu.with_memory_space_constraint(x, space)


def call(body, outs, args, specs=None, scratch=(), flops=0, aliases=None, out_specs=None):
    moved = sum(math.prod(x.shape) * jnp.dtype(x.dtype).itemsize for x in list(args) + list(outs))
    return pl.pallas_call(
        body,
        out_shape=outs,
        in_specs=specs or [VMEM] * len(args),
        out_specs=out_specs or [VMEM] * len(outs),
        scratch_shapes=list(scratch),
        input_output_aliases=aliases or {},
        cost_estimate=pl.CostEstimate(flops=flops, bytes_accessed=moved, transcendentals=0),
        compiler_params=pltpu.CompilerParams(vmem_limit_bytes=24 * 1024 * 1024),
    )(*args)


def lanes_of(shape):
    return lax.broadcasted_iota(jnp.int32, shape, len(shape) - 1)


def sublanes_of(shape):
    return lax.broadcasted_iota(jnp.int32, shape, len(shape) - 2)


def group_total(v):
    lane = lanes_of(v.shape)
    v = v + jnp.where(lane % 2 == 0, pltpu.roll(v, 127, 1), pltpu.roll(v, 1, 1))
    return v + jnp.where(lane % 4 < 2, pltpu.roll(v, 126, 1), pltpu.roll(v, 2, 1))


def column_sum(v):
    part = jnp.sum(v.reshape(-1, 8, v.shape[-1]), axis=0)
    return jnp.broadcast_to(jnp.sum(part, axis=0, keepdims=True), part.shape)


def split_row(row):
    high = row.astype(BF16).astype(F32)
    middle = (row - high).astype(BF16).astype(F32)
    low = row - high - middle
    index = sublanes_of((8, 128))
    parts = jnp.where(index == 0, high, jnp.where(index == 1, middle, low))
    return jnp.concatenate([parts, parts], axis=0).astype(BF16)


def join_row(parts):
    parts = parts.astype(F32)
    return jnp.broadcast_to(parts[0:1] + parts[1:2] + parts[2:3], (8, 128))


def entry_kernel(up_hbm, x_hbm, gain_hbm, bias_hbm, up_ref, x_ref, gain_ref, bias_ref, facing_ref, sems):
    pairs = ((up_hbm, up_ref), (x_hbm, x_ref), (gain_hbm, gain_ref), (bias_hbm, bias_ref))
    copies = [pltpu.make_async_copy(source, target, sems.at[i]) for i, (source, target) in enumerate(pairs)]
    for copy in copies:
        copy.start()
    copies[0].wait()
    left = lax.axis_index("sect") == 0
    up = up_ref[...]
    facing_ref[...] = jnp.where(left, up[:, :, 16:], up[:, :, :16]).reshape(512, 128)
    for copy in copies[1:]:
        copy.wait()


def stats_kernel(x_ref, stat_ref):
    x = x_ref[...].astype(F32).reshape(-1, 128)
    total = group_total(column_sum(x))
    square = group_total(column_sum(x * x))
    stat_ref[...] = jnp.where(lanes_of(total.shape) % 4 < 2, total, square)


def edge_of(up_ref, side_ref, bottom):
    side = side_ref[...].reshape(4, 8, 16, 128)
    low = jnp.concatenate([up_ref[:, 7], side[:, 7]], axis=1)
    top = jnp.concatenate([up_ref[:, 0], side[:, 0]], axis=1)
    return jnp.where(bottom, low, top).reshape(192, 128)


def first_edge_kernel(up_ref, side_ref, stat_ref, out_ref):
    even = lax.axis_index("rows") % 2 == 0
    out_ref[:192] = edge_of(up_ref, side_ref, even)
    out_ref[192:] = split_row(stat_ref[...])


def second_edge_kernel(up_ref, side_ref, near_ref, stat_ref, out_ref, sum_ref):
    even = lax.axis_index("rows") % 2 == 0
    row = stat_ref[...] + join_row(near_ref[192:])
    sum_ref[...] = row
    out_ref[:192] = edge_of(up_ref, side_ref, jnp.logical_not(even))
    out_ref[192:] = split_row(row)


def beyond(near_ref, far_ref):
    even = lax.axis_index("rows") % 2 == 0
    outside = jnp.logical_or(lax.axis_index("rows") == 0, lax.axis_index("rows") == lax.axis_size("rows") - 1)
    near = near_ref[:192].reshape(4, 48, 128)
    far = far_ref[:192].reshape(4, 48, 128)
    far = jnp.where(outside, jnp.zeros_like(far), far)
    return jnp.where(even, far, near), jnp.where(even, near, far)


def early_kernel(up_ref, side_ref, near_ref, far_ref, stat_ref, early_ref, sent_ref):
    row = stat_ref[...] + join_row(far_ref[192:])
    sent_ref[...] = jnp.broadcast_to(row[None], (sent_ref.shape[0] // 8, 8, 128)).reshape(sent_ref.shape)
    above, below = beyond(near_ref, far_ref)
    early_ref[:, 0] = above[:2]
    early_ref[:, 9] = below[:2]
    early_ref[:, 1:9, :32] = up_ref[:2]
    early_ref[:, 1:9, 32:] = side_ref[:256].reshape(2, 8, 16, 128)


def column_taps(rows):
    left = lax.axis_index("sect") == 0
    core = rows[:, :32]
    column = sublanes_of(core.shape)
    first = column == 0
    last = column == 31
    zero = jnp.zeros_like(core)
    ahead = pltpu.roll(rows, 47, 1)[:, :32]
    behind = pltpu.roll(rows, 1, 1)[:, :32]
    ahead = jnp.where(left, ahead + jnp.where(first, core, zero), jnp.where(last, zero, ahead))
    behind = jnp.where(left, jnp.where(first, zero, behind), behind + jnp.where(last, core, zero))
    return ahead, core, behind


def put(v_ref, f, r, b, e, rows):
    j = (b * 3 + e) * 128
    count = rows.shape[0]
    v_ref[f, r * 32 : (r + count) * 32, j : j + 128] = rows.astype(BF16).reshape(count * 32, 128)


def times_taps(lhs, taps_ref, a):
    return lax.dot_general(lhs, taps_ref[a], (((1,), (1,)), ((), ())), preferred_element_type=F32)


def own_kernel(up_ref, side_ref, kernel_hbm, v_ref, dh_ref, taps_ref, kernel_ref, sem):
    weights = pltpu.make_async_copy(kernel_hbm, kernel_ref, sem)
    weights.start()
    row_first = lax.axis_index("rows") == 0
    row_last = lax.axis_index("rows") == lax.axis_size("rows") - 1
    for f in range(4):
        side = side_ref[f * 128 : (f + 1) * 128].reshape(8, 16, 128)
        rows = jnp.concatenate([up_ref[f].astype(F32), side.astype(F32)], axis=1)
        for e, part in enumerate(column_taps(rows)):
            zero = jnp.zeros_like(part[0])
            top = part[1] + jnp.where(row_first, part[0], zero)
            low = part[6] + jnp.where(row_last, part[7], zero)
            put(v_ref, f, 0, 0, e, top[None])
            put(v_ref, f, 1, 0, e, part[2:8])
            put(v_ref, f, 0, 1, e, part)
            put(v_ref, f, 1, 2, e, part[0:6])
            put(v_ref, f, 7, 2, e, low[None])
    weights.wait()
    for a in range(3):
        for b in range(3):
            for e in range(3):
                j = (b * 3 + e) * 128
                taps_ref[a, :, j : j + 128] = kernel_ref[a, b, e]
    for f in range(4):
        total = None
        for a in range(3):
            if f + 2 - a < 4:
                term = times_taps(v_ref[f + 2 - a, 32:224], taps_ref, a)
                total = term if total is None else total + term
        dh_ref[f * 256 + 32 : f * 256 + 224] = total


def spread_kernel(near_ref, far_ref, later_ref, own_ref, v_ref):
    above, below = beyond(near_ref, far_ref)
    row_first = lax.axis_index("rows") == 0
    row_last = lax.axis_index("rows") == lax.axis_size("rows") - 1
    outer = jnp.concatenate([above, below], axis=0).astype(F32)
    for e, part in enumerate(column_taps(outer)):
        for f in range(4):
            put(v_ref, f, 0, 2, e, part[f : f + 1])
            put(v_ref, f, 7, 0, e, part[f + 4 : f + 5])
    for f in range(2):
        for e, part in enumerate(column_taps(later_ref[f].astype(F32))):
            zero = jnp.zeros_like(part[0])
            top = part[2] + jnp.where(row_first, part[1], zero)
            low = part[7] + jnp.where(row_last, part[8], zero)
            put(v_ref, f + 4, 0, 0, e, top[None])
            put(v_ref, f + 4, 1, 0, e, part[3:10])
            put(v_ref, f + 4, 0, 1, e, part[1:9])
            put(v_ref, f + 4, 0, 2, e, part[0:7])
            put(v_ref, f + 4, 7, 2, e, low[None])

    @pl.when(lax.axis_index("tm") == 0)
    def _():
        both = v_ref[1].astype(F32) + v_ref[0].astype(F32)
        v_ref[6] = both.astype(BF16)
        v_ref[7] = (both + v_ref[2].astype(F32)).astype(BF16)


def grad_kernel(x_ref, norm_ref, gain_ref, bias_ref, taps_ref, part_ref, v_ref, da_ref, sums_ref, dh_ref):
    def edges(lo, hi):
        return jnp.concatenate([v_ref[lo:hi, 0:32], v_ref[lo:hi, 224:256]], axis=1).reshape((hi - lo) * 64, 1152)

    outer = times_taps(edges(0, 4), taps_ref, 2)
    one = times_taps(edges(1, 4), taps_ref, 1)
    two = times_taps(edges(2, 4), taps_ref, 0)
    outer = outer + jnp.concatenate([one, jnp.zeros((64, 128), F32)], axis=0)
    outer = outer + jnp.concatenate([two, jnp.zeros((128, 128), F32)], axis=0)
    for f in range(4):
        dh_ref[f * 256 : f * 256 + 32] = outer[f * 64 : f * 64 + 32]
        dh_ref[f * 256 + 32 : f * 256 + 224] = part_ref[f * 256 + 32 : f * 256 + 224]
        dh_ref[f * 256 + 224 : f * 256 + 256] = outer[f * 64 + 32 : f * 64 + 64]
    dh_ref[768:1024] += times_taps(v_ref[4], taps_ref, 1)
    dh_ref[512:1024] += times_taps(v_ref[4:6].reshape(512, 1152), taps_ref, 0)

    @pl.when(lax.axis_index("tm") == 0)
    def _():
        dh_ref[0:256] += times_taps(v_ref[0], taps_ref, 1) + times_taps(v_ref[6], taps_ref, 0)

    bias_sum = jnp.zeros((8, 128), F32)
    gain_sum = jnp.zeros((8, 128), F32)
    for block in range(8):
        xhat, pre = block_of(x_ref, norm_ref, gain_ref, bias_ref, block)
        sig = 1.0 / (1.0 + jnp.exp(-pre))
        da = dh_ref[block * 128 : (block + 1) * 128] * sig * (1.0 + pre * (1.0 - sig))
        da_ref[block * 128 : (block + 1) * 128] = da
        bias_sum = bias_sum + jnp.sum(da.reshape(16, 8, 128), axis=0)
        gain_sum = gain_sum + jnp.sum((da * xhat).reshape(16, 8, 128), axis=0)
    sums_ref[...] = jnp.where(sublanes_of((8, 128)) == 0, column_sum(bias_sum), column_sum(gain_sum))


def sums_to_pair(row):
    lane = lanes_of(row.shape)
    total = jnp.where(lane % 4 < 2, row, pltpu.roll(row, 2, 1))
    square = jnp.where(lane % 4 < 2, pltpu.roll(row, 126, 1), row)
    return total, square


def product_of(turned, v_ref, a, lo, hi):
    if a == 2:
        return jnp.dot(turned, v_ref[0:4, :, lo:hi].reshape(1024, hi - lo), preferred_element_type=F32)
    source = jnp.where(lax.axis_index("tm") == 0, 7 - a, 2 - a)
    first = jnp.dot(turned[:, :256], v_ref[source, :, lo:hi], preferred_element_type=F32)
    rest = v_ref[3 - a : 6 - a, :, lo:hi].reshape(768, hi - lo)
    return first + jnp.dot(turned[:, 256:], rest, preferred_element_type=F32)


def half_product(half, turned, v_ref, w_ref):
    for a, lo, hi in (((0, 0, 9), (1, 0, 5)), ((1, 5, 9), (2, 0, 9)))[half]:
        product = product_of(turned, v_ref, a, lo * 128, hi * 128)
        for j in range(lo, hi):
            block = product[:, (j - lo) * 128 : (j - lo + 1) * 128].T.reshape(16, 8, 128)
            w_ref[:, (a * 9 + j) % HALF] = block
    if half == 1:
        w_ref[:, HALF - 1] = jnp.zeros((16, 8, 128), F32)


def block_of(x_ref, norm_ref, gain_ref, bias_ref, block):
    half = (block % 2) * 4
    x = x_ref[block // 2, half : half + 4].astype(F32).reshape(128, 128)
    xhat = (x - norm_ref[0:1]) * norm_ref[8:9]
    return xhat, xhat * gain_ref[...] + bias_ref[...]


def away_kernel(counted, x_ref, stat_ref, gain_ref, bias_ref, v_ref, w_ref, turned_ref, norm_ref):
    total, square = sums_to_pair(column_sum(stat_ref[...]))
    mean = total / counted
    norm_ref[0:8] = mean
    norm_ref[8:16] = lax.rsqrt(square / counted - mean * mean + 1e-06)
    for block in range(8):
        _, pre = block_of(x_ref, norm_ref, gain_ref, bias_ref, block)
        hidden = pre * (1.0 / (1.0 + jnp.exp(-pre)))
        turned_ref[:, block * 128 : (block + 1) * 128] = hidden.T.astype(BF16)
    left = lax.axis_index("sect") == 0

    @pl.when(left)
    def _():
        half_product(1, turned_ref[...], v_ref, w_ref)

    @pl.when(jnp.logical_not(left))
    def _():
        half_product(0, turned_ref[...], v_ref, w_ref)


def home_kernel(turned_ref, v_ref, w_ref):
    left = lax.axis_index("sect") == 0

    @pl.when(left)
    def _():
        half_product(0, turned_ref[...], v_ref, w_ref)

    @pl.when(jnp.logical_not(left))
    def _():
        half_product(1, turned_ref[...], v_ref, w_ref)


def split_sums(sums):
    row = sublanes_of(sums.shape)
    high = sums.astype(BF16).astype(F32)
    middle = (sums - high).astype(BF16).astype(F32)
    low = sums - high - middle
    return jnp.where(
        row < 2, high, jnp.where(row < 4, pltpu.roll(middle, 2, 0), pltpu.roll(low, 4, 0))
    )


def join_sums(parts):
    return parts + pltpu.roll(parts, 6, 0) + pltpu.roll(parts, 4, 0)


def pair_kernel(own_ref, other_ref, sums_ref, other_sums_ref, out_ref):
    slot = split_sums(sums_ref[...] + other_sums_ref[...])
    for i in range(16):
        body = (own_ref[i] + other_ref[i]).reshape(HALF * 8, 128)
        out_ref[i] = jnp.concatenate([body, slot], axis=0).astype(BF16)


def power_for(values):
    most = jnp.max(jnp.max(jnp.abs(values), axis=0, keepdims=True), axis=1, keepdims=True)
    bits = jnp.log(jnp.maximum(most, 1e-30)) * 1.4426950408889634
    return jnp.clip(jnp.floor(14.0 - bits), -100.0, 100.0)


def share_kernel(in_ref, out_ref):
    rows = HALF * 8
    total = in_ref[0].astype(F32)
    for i in range(1, in_ref.shape[0]):
        total = total + in_ref[i].astype(F32)
    body = total[:rows]
    sums = join_sums(total[rows:])
    index = sublanes_of(sums.shape)
    sums = jnp.where(index < 2, sums, jnp.zeros_like(sums))
    power = power_for(body)
    power_of_sums = power_for(sums)
    slot = split_sums(sums * jnp.exp2(power_of_sums))
    slot = jnp.where(index == 6, power, jnp.where(index == 7, power_of_sums, slot))
    out_ref[:rows] = body * jnp.exp2(power)
    out_ref[rows:] = slot


def last_sum_kernel(scaling, in_ref, half_ref, sums_ref):
    rows = HALF * 8
    total = jnp.zeros((rows, 128), F32)
    sums = jnp.zeros((8, 128), F32)
    for i in range(in_ref.shape[0]):
        slot = in_ref[i, rows:]
        total = total + in_ref[i, :rows] * jnp.exp2(-slot[6:7])
        sums = sums + join_sums(slot) * jnp.exp2(-slot[7:8])
    half_ref[...] = total * scaling
    sums_ref[...] = sums


def finish_kernel(counted, scaling, x_ref, da_ref, norm_ref, sums_ref, gain_ref, out_hbm, gain_grad_ref, bias_grad_ref, out_ref, sems):
    gain = gain_ref[...]
    sums = sums_ref[...]
    bias_grad_ref[...] = sums[0:1] * scaling
    gain_grad_ref[...] = sums[1:2] * scaling
    averages = group_total(gain * sums) / counted
    mean = norm_ref[0:1]
    rstd = norm_ref[8:9]
    leading = averages[0:1]
    trailing = averages[1:2]
    copies = []
    for f in range(4):
        xhat = (x_ref[f].astype(F32).reshape(256, 128) - mean) * rstd
        grad = rstd * (da_ref[f * 256 : (f + 1) * 256] * gain - leading - xhat * trailing)
        out_ref[f] = grad.astype(BF16).reshape(8, 32, 128)
        copies.append(pltpu.make_async_copy(out_ref.at[f], out_hbm.at[f], sems.at[f]))
        copies[-1].start()
    for copy in copies:
        copy.wait()


def join_kernel(half_ref, other_ref, out_ref):
    left = lax.axis_index("sect") == 0
    half = half_ref[...]
    other = other_ref[...]
    out_ref[: HALF * 8] = jnp.where(left, half, other)
    out_ref[HALF * 8 :] = jnp.where(left, other, half)[: (TAPS - HALF) * 8]


def shape_of(shape, dtype=F32):
    return jax.ShapeDtypeStruct(shape, dtype)


def local(activations, group_norm_gain, group_norm_bias, upstream, kernel):
    frames, height, columns, channels = activations.shape
    n_time, n_rows, n_sect = (lax.axis_size(axis) for axis in ("tm", "rows", "sect"))
    cells = frames * height * columns
    total_cells = cells * n_time * n_rows * n_sect
    counted = float(total_cells * (channels // GROUPS))
    scaling = float(total_cells) ** (-0.5)
    swap = [(0, 1), (1, 0)]
    near = [(i, i ^ 1) for i in range(n_rows)]
    far = [(i, (i - 1) % n_rows if i % 2 == 0 else (i + 1) % n_rows) for i in range(n_rows)]

    up, x, gain, bias, facing = call(
        entry_kernel,
        [
            shape_of(upstream.shape, BF16),
            shape_of(activations.shape, BF16),
            shape_of((1, channels)),
            shape_of((1, channels)),
            shape_of((512, channels), BF16),
        ],
        [
            held(upstream, pltpu.HBM),
            held(activations, pltpu.HBM),
            held(group_norm_gain.reshape(1, channels), pltpu.HBM),
            held(group_norm_bias.reshape(1, channels), pltpu.HBM),
        ],
        [HBM] * 4,
        [pltpu.SemaphoreType.DMA((4,))],
    )
    side = lax.ppermute(facing, "sect", swap)
    (stat,) = call(stats_kernel, [shape_of((8, channels))], [x])
    (message,) = call(first_edge_kernel, [shape_of((208, channels), BF16)], [up, side, stat])
    nearer = lax.ppermute(message, "rows", near)
    spread, inner, taps = call(
        own_kernel,
        [
            pltpu.VMEM((8, 256, 1152), BF16),
            shape_of((cells, channels)),
            shape_of((3, channels, 9 * channels), BF16),
        ],
        [up, side, held(kernel, pltpu.HBM)],
        [VMEM, VMEM, HBM],
        [pltpu.VMEM((3, 3, 3, 128, 128), BF16), pltpu.SemaphoreType.DMA],
        flops=cells * TAPS * channels * channels,
    )
    nearer, inner = lax.optimization_barrier((nearer, inner))
    message, stat = call(
        second_edge_kernel,
        [shape_of((208, channels), BF16), shape_of((8, channels))],
        [up, side, nearer, stat],
        [VMEM, VMEM, VMEM, VMEM],
    )
    farther = lax.ppermute(message, "rows", far)
    pairs = [(0, 3), (1, 6), (2, 5), (4, 7)]
    groups = [
        [(t * n_rows + r) * n_sect + c for t in range(n_time) for r in pair for c in range(n_sect)]
        for pair in pairs
    ]
    early, stat = call(
        early_kernel,
        [shape_of((2, 10, 48, channels), BF16), shape_of((len(groups[0]), channels))],
        [up, side, nearer, farther, stat],
        [VMEM, VMEM, VMEM, VMEM, VMEM],
    )
    later = lax.ppermute(early, "tm", [(i + 1, i) for i in range(n_time - 1)])
    stat = lax.all_to_all(stat[:, None], ("tm", "rows", "sect"), 0, 0, axis_index_groups=groups).reshape(-1, channels)
    stat, later = lax.optimization_barrier((stat, later))
    (spread,) = call(
        spread_kernel,
        [pltpu.VMEM((8, 256, 1152), BF16)],
        [nearer, farther, later, held(spread, pltpu.VMEM)],
        aliases={3: 0},
    )
    away, turned, norm = call(
        functools.partial(away_kernel, counted),
        [shape_of((16, HALF, 8, 128)), shape_of((channels, cells), BF16), shape_of((16, channels))],
        [x, stat, gain, bias, held(spread, pltpu.VMEM)],
        flops=cells * TAPS * channels * channels,
    )
    arrived = lax.ppermute(away, "sect", swap)
    da, sums = call(
        grad_kernel,
        [shape_of((cells, channels)), shape_of((8, channels))],
        [x, norm, gain, bias, taps, inner, held(spread, pltpu.VMEM)],
        scratch=[pltpu.VMEM((cells, channels), F32)],
        flops=cells * TAPS * channels * channels,
    )
    other_sums = lax.ppermute(sums, "sect", swap)
    (home,) = call(
        home_kernel,
        [shape_of((16, HALF, 8, 128))],
        [turned, held(spread, pltpu.VMEM)],
        flops=cells * TAPS * channels * channels,
    )
    (sent,) = call(
        pair_kernel, [shape_of((16, SLOTS * 8, 128), BF16)], [home, arrived, sums, other_sums]
    )
    gathered = lax.all_to_all(sent, "tm", 0, 0)
    (share,) = call(share_kernel, [shape_of((SLOTS * 8, 128))], [gathered])
    share = jnp.broadcast_to(share.astype(jnp.float16)[None], (n_rows, SLOTS * 8, 128))
    shares = lax.all_to_all(share, "rows", 0, 0).astype(F32)
    half, sums = call(
        functools.partial(last_sum_kernel, scaling),
        [shape_of((HALF * 8, 128)), shape_of((8, 128))],
        [shares],
    )
    other = lax.ppermute(half, "sect", swap)
    input_gradient, gain_grad, bias_grad = call(
        functools.partial(finish_kernel, counted, scaling),
        [shape_of(activations.shape, BF16), shape_of((1, 128)), shape_of((1, 128))],
        [x, da, norm, sums, gain],
        scratch=[pltpu.VMEM(activations.shape, BF16), pltpu.SemaphoreType.DMA((4,))],
        out_specs=[HBM, VMEM, VMEM],
    )
    (whole,) = call(join_kernel, [shape_of((TAPS * 8, 128))], [half, other])
    weight_grad = whole.reshape(3, 3, 3, 8, 128).transpose(0, 1, 2, 4, 3)
    return (input_gradient, gain_grad.reshape(128), bias_grad.reshape(128), weight_grad)


def solution(mesh):
    return jax.shard_map(
        local,
        mesh=mesh,
        in_specs=(P("tm", "rows", "sect", None), P(), P(), P("tm", "rows", "sect", None), P()),
        out_specs=(P("tm", "rows", "sect", None), P(), P(), P(None, None, None, None, "tm")),
        check_vma=False,
    )
```

```python
import functools
import math

import jax
import jax.numpy as jnp
from jax import lax
from jax.experimental import pallas as pl
from jax.experimental.pallas import tpu as pltpu
from jax.sharding import PartitionSpec as P

GROUPS = 32
TAPS = 27
HALF = 14
SLOTS = HALF + 1
F32 = jnp.float32
BF16 = jnp.bfloat16
VMEM = pl.BlockSpec(memory_space=pltpu.VMEM)
HBM = pl.BlockSpec(memory_space=pltpu.HBM)


def held(x, space):
    return pltpu.with_memory_space_constraint(x, space)


def call(body, outs, args, specs=None, scratch=(), flops=0, aliases=None):
    moved = sum(math.prod(x.shape) * jnp.dtype(x.dtype).itemsize for x in list(args) + list(outs))
    return pl.pallas_call(
        body,
        out_shape=outs,
        in_specs=specs or [VMEM] * len(args),
        out_specs=[VMEM] * len(outs),
        scratch_shapes=list(scratch),
        input_output_aliases=aliases or {},
        cost_estimate=pl.CostEstimate(flops=flops, bytes_accessed=moved, transcendentals=0),
        compiler_params=pltpu.CompilerParams(vmem_limit_bytes=24 * 1024 * 1024),
    )(*args)


def lanes_of(shape):
    return lax.broadcasted_iota(jnp.int32, shape, len(shape) - 1)


def sublanes_of(shape):
    return lax.broadcasted_iota(jnp.int32, shape, len(shape) - 2)


def group_total(v):
    lane = lanes_of(v.shape)
    v = v + jnp.where(lane % 2 == 0, pltpu.roll(v, 127, 1), pltpu.roll(v, 1, 1))
    return v + jnp.where(lane % 4 < 2, pltpu.roll(v, 126, 1), pltpu.roll(v, 2, 1))


def column_sum(v):
    part = jnp.sum(v.reshape(-1, 8, v.shape[-1]), axis=0)
    return jnp.broadcast_to(jnp.sum(part, axis=0, keepdims=True), part.shape)


def split_row(row):
    high = row.astype(BF16).astype(F32)
    middle = (row - high).astype(BF16).astype(F32)
    low = row - high - middle
    index = sublanes_of((8, 128))
    parts = jnp.where(index == 0, high, jnp.where(index == 1, middle, low))
    return jnp.concatenate([parts, parts], axis=0).astype(BF16)


def join_row(parts):
    parts = parts.astype(F32)
    return jnp.broadcast_to(parts[0:1] + parts[1:2] + parts[2:3], (8, 128))


def entry_kernel(up_hbm, x_hbm, gain_hbm, bias_hbm, up_ref, x_ref, gain_ref, bias_ref, facing_ref, stat_ref, sems):
    pairs = ((up_hbm, up_ref), (x_hbm, x_ref), (gain_hbm, gain_ref), (bias_hbm, bias_ref))
    copies = [pltpu.make_async_copy(source, target, sems.at[i]) for i, (source, target) in enumerate(pairs)]
    for copy in copies:
        copy.start()
    copies[0].wait()
    left = lax.axis_index("sect") == 0
    up = up_ref[...]
    facing_ref[:512] = jnp.where(left, up[:, :, 16:], up[:, :, :16]).reshape(512, 128)
    for copy in copies[1:]:
        copy.wait()
    x = x_ref[...].astype(F32).reshape(-1, 128)
    total = group_total(column_sum(x))
    square = group_total(column_sum(x * x))
    row = jnp.where(lanes_of(total.shape) % 4 < 2, total, square)
    stat_ref[...] = row
    facing_ref[512:] = split_row(row)


def edge_of(up_ref, side_ref, bottom):
    side = side_ref[:512].reshape(4, 8, 16, 128)
    low = jnp.concatenate([up_ref[:, 7], side[:, 7]], axis=1)
    top = jnp.concatenate([up_ref[:, 0], side[:, 0]], axis=1)
    return jnp.where(bottom, low, top).reshape(192, 128)


def edge_kernel(up_ref, side_ref, stat_ref, near_ref, far_ref, sum_ref):
    even = lax.axis_index("rows") % 2 == 0
    row = stat_ref[...] + join_row(side_ref[512:])
    sum_ref[...] = row
    near_ref[:192] = edge_of(up_ref, side_ref, even)
    near_ref[192:] = split_row(row)
    far_ref[...] = edge_of(up_ref, side_ref, jnp.logical_not(even))


def beyond(near_ref, far_ref):
    even = lax.axis_index("rows") % 2 == 0
    outside = jnp.logical_or(lax.axis_index("rows") == 0, lax.axis_index("rows") == lax.axis_size("rows") - 1)
    near = near_ref[:192].reshape(4, 48, 128)
    far = far_ref[:192].reshape(4, 48, 128)
    far = jnp.where(outside, jnp.zeros_like(far), far)
    return jnp.where(even, far, near), jnp.where(even, near, far)


def early_kernel(up_ref, side_ref, near_ref, far_ref, stat_ref, early_ref, sent_ref):
    row = stat_ref[...] + join_row(near_ref[192:])
    sent_ref[...] = jnp.broadcast_to(row[None], (sent_ref.shape[0] // 8, 8, 128)).reshape(sent_ref.shape)
    above, below = beyond(near_ref, far_ref)
    early_ref[:, 0] = above[:2]
    early_ref[:, 9] = below[:2]
    early_ref[:, 1:9, :32] = up_ref[:2]
    early_ref[:, 1:9, 32:] = side_ref[:256].reshape(2, 8, 16, 128)


def column_taps(rows):
    left = lax.axis_index("sect") == 0
    core = rows[:, :32]
    column = sublanes_of(core.shape)
    first = column == 0
    last = column == 31
    zero = jnp.zeros_like(core)
    ahead = pltpu.roll(rows, 47, 1)[:, :32]
    behind = pltpu.roll(rows, 1, 1)[:, :32]
    ahead = jnp.where(left, ahead + jnp.where(first, core, zero), jnp.where(last, zero, ahead))
    behind = jnp.where(left, jnp.where(first, zero, behind), behind + jnp.where(last, core, zero))
    return ahead, core, behind


def put(v_ref, f, r, b, e, rows):
    j = (b * 3 + e) * 128
    count = rows.shape[0]
    v_ref[f, r * 32 : (r + count) * 32, j : j + 128] = rows.astype(BF16).reshape(count * 32, 128)


def times_taps(lhs, taps_ref, a):
    return lax.dot_general(lhs, taps_ref[a], (((1,), (1,)), ((), ())), preferred_element_type=F32)


def own_kernel(up_ref, side_ref, kernel_hbm, v_ref, dh_ref, taps_ref, kernel_ref, sem):
    weights = pltpu.make_async_copy(kernel_hbm, kernel_ref, sem)
    weights.start()
    row_first = lax.axis_index("rows") == 0
    row_last = lax.axis_index("rows") == lax.axis_size("rows") - 1
    for f in range(4):
        side = side_ref[f * 128 : (f + 1) * 128].reshape(8, 16, 128)
        rows = jnp.concatenate([up_ref[f].astype(F32), side.astype(F32)], axis=1)
        for e, part in enumerate(column_taps(rows)):
            zero = jnp.zeros_like(part[0])
            top = part[1] + jnp.where(row_first, part[0], zero)
            low = part[6] + jnp.where(row_last, part[7], zero)
            put(v_ref, f, 0, 0, e, top[None])
            put(v_ref, f, 1, 0, e, part[2:8])
            put(v_ref, f, 0, 1, e, part)
            put(v_ref, f, 1, 2, e, part[0:6])
            put(v_ref, f, 7, 2, e, low[None])
    weights.wait()
    for a in range(3):
        for b in range(3):
            for e in range(3):
                j = (b * 3 + e) * 128
                taps_ref[a, :, j : j + 128] = kernel_ref[a, b, e]
    for f in range(4):
        total = None
        for a in range(3):
            if f + 2 - a < 4:
                term = times_taps(v_ref[f + 2 - a, 32:224], taps_ref, a)
                total = term if total is None else total + term
        dh_ref[f * 256 + 32 : f * 256 + 224] = total


def spread_kernel(near_ref, far_ref, later_ref, own_ref, v_ref):
    above, below = beyond(near_ref, far_ref)
    row_first = lax.axis_index("rows") == 0
    row_last = lax.axis_index("rows") == lax.axis_size("rows") - 1
    outer = jnp.concatenate([above, below], axis=0).astype(F32)
    for e, part in enumerate(column_taps(outer)):
        for f in range(4):
            put(v_ref, f, 0, 2, e, part[f : f + 1])
            put(v_ref, f, 7, 0, e, part[f + 4 : f + 5])
    for f in range(2):
        for e, part in enumerate(column_taps(later_ref[f].astype(F32))):
            zero = jnp.zeros_like(part[0])
            top = part[2] + jnp.where(row_first, part[1], zero)
            low = part[7] + jnp.where(row_last, part[8], zero)
            put(v_ref, f + 4, 0, 0, e, top[None])
            put(v_ref, f + 4, 1, 0, e, part[3:10])
            put(v_ref, f + 4, 0, 1, e, part[1:9])
            put(v_ref, f + 4, 0, 2, e, part[0:7])
            put(v_ref, f + 4, 7, 2, e, low[None])

    @pl.when(lax.axis_index("tm") == 0)
    def _():
        both = v_ref[1].astype(F32) + v_ref[0].astype(F32)
        v_ref[6] = both.astype(BF16)
        v_ref[7] = (both + v_ref[2].astype(F32)).astype(BF16)


def grad_kernel(x_ref, norm_ref, gain_ref, bias_ref, taps_ref, part_ref, v_ref, da_ref, sums_ref, dh_ref):
    def edges(lo, hi):
        return jnp.concatenate([v_ref[lo:hi, 0:32], v_ref[lo:hi, 224:256]], axis=1).reshape((hi - lo) * 64, 1152)

    outer = times_taps(edges(0, 4), taps_ref, 2)
    one = times_taps(edges(1, 4), taps_ref, 1)
    two = times_taps(edges(2, 4), taps_ref, 0)
    outer = outer + jnp.concatenate([one, jnp.zeros((64, 128), F32)], axis=0)
    outer = outer + jnp.concatenate([two, jnp.zeros((128, 128), F32)], axis=0)
    for f in range(4):
        dh_ref[f * 256 : f * 256 + 32] = outer[f * 64 : f * 64 + 32]
        dh_ref[f * 256 + 32 : f * 256 + 224] = part_ref[f * 256 + 32 : f * 256 + 224]
        dh_ref[f * 256 + 224 : f * 256 + 256] = outer[f * 64 + 32 : f * 64 + 64]
    dh_ref[768:1024] += times_taps(v_ref[4], taps_ref, 1)
    dh_ref[512:1024] += times_taps(v_ref[4:6].reshape(512, 1152), taps_ref, 0)

    @pl.when(lax.axis_index("tm") == 0)
    def _():
        dh_ref[0:256] += times_taps(v_ref[0], taps_ref, 1) + times_taps(v_ref[6], taps_ref, 0)

    bias_sum = jnp.zeros((8, 128), F32)
    gain_sum = jnp.zeros((8, 128), F32)
    for block in range(8):
        xhat, pre = block_of(x_ref, norm_ref, gain_ref, bias_ref, block)
        sig = 1.0 / (1.0 + jnp.exp(-pre))
        da = dh_ref[block * 128 : (block + 1) * 128] * sig * (1.0 + pre * (1.0 - sig))
        da_ref[block * 128 : (block + 1) * 128] = da
        bias_sum = bias_sum + jnp.sum(da.reshape(16, 8, 128), axis=0)
        gain_sum = gain_sum + jnp.sum((da * xhat).reshape(16, 8, 128), axis=0)
    sums_ref[...] = jnp.where(sublanes_of((8, 128)) == 0, column_sum(bias_sum), column_sum(gain_sum))


def sums_to_pair(row):
    lane = lanes_of(row.shape)
    total = jnp.where(lane % 4 < 2, row, pltpu.roll(row, 2, 1))
    square = jnp.where(lane % 4 < 2, pltpu.roll(row, 126, 1), row)
    return total, square


def product_of(turned, v_ref, a, lo, hi):
    if a == 2:
        return jnp.dot(turned, v_ref[0:4, :, lo:hi].reshape(1024, hi - lo), preferred_element_type=F32)
    source = jnp.where(lax.axis_index("tm") == 0, 7 - a, 2 - a)
    first = jnp.dot(turned[:, :256], v_ref[source, :, lo:hi], preferred_element_type=F32)
    rest = v_ref[3 - a : 6 - a, :, lo:hi].reshape(768, hi - lo)
    return first + jnp.dot(turned[:, 256:], rest, preferred_element_type=F32)


def half_product(half, turned, v_ref, w_ref):
    for a, lo, hi in (((0, 0, 9), (1, 0, 5)), ((1, 5, 9), (2, 0, 9)))[half]:
        product = product_of(turned, v_ref, a, lo * 128, hi * 128)
        for j in range(lo, hi):
            block = product[:, (j - lo) * 128 : (j - lo + 1) * 128].T.reshape(16, 8, 128)
            w_ref[:, (a * 9 + j) % HALF] = block
    if half == 1:
        w_ref[:, HALF - 1] = jnp.zeros((16, 8, 128), F32)


def block_of(x_ref, norm_ref, gain_ref, bias_ref, block):
    half = (block % 2) * 4
    x = x_ref[block // 2, half : half + 4].astype(F32).reshape(128, 128)
    xhat = (x - norm_ref[0:1]) * norm_ref[8:9]
    return xhat, xhat * gain_ref[...] + bias_ref[...]


def away_kernel(counted, x_ref, stat_ref, gain_ref, bias_ref, v_ref, w_ref, turned_ref, norm_ref):
    total, square = sums_to_pair(column_sum(stat_ref[...]))
    mean = total / counted
    norm_ref[0:8] = mean
    norm_ref[8:16] = lax.rsqrt(square / counted - mean * mean + 1e-06)
    for block in range(8):
        _, pre = block_of(x_ref, norm_ref, gain_ref, bias_ref, block)
        hidden = pre * (1.0 / (1.0 + jnp.exp(-pre)))
        turned_ref[:, block * 128 : (block + 1) * 128] = hidden.T.astype(BF16)
    left = lax.axis_index("sect") == 0

    @pl.when(left)
    def _():
        half_product(1, turned_ref[...], v_ref, w_ref)

    @pl.when(jnp.logical_not(left))
    def _():
        half_product(0, turned_ref[...], v_ref, w_ref)


def home_kernel(turned_ref, v_ref, w_ref):
    left = lax.axis_index("sect") == 0

    @pl.when(left)
    def _():
        half_product(0, turned_ref[...], v_ref, w_ref)

    @pl.when(jnp.logical_not(left))
    def _():
        half_product(1, turned_ref[...], v_ref, w_ref)


def split_sums(sums):
    row = sublanes_of(sums.shape)
    high = sums.astype(BF16).astype(F32)
    middle = (sums - high).astype(BF16).astype(F32)
    low = sums - high - middle
    return jnp.where(
        row < 2, high, jnp.where(row < 4, pltpu.roll(middle, 2, 0), pltpu.roll(low, 4, 0))
    )


def join_sums(parts):
    return parts + pltpu.roll(parts, 6, 0) + pltpu.roll(parts, 4, 0)


def pair_kernel(own_ref, other_ref, sums_ref, other_sums_ref, out_ref):
    slot = split_sums(sums_ref[...] + other_sums_ref[...])
    for i in range(16):
        body = (own_ref[i] + other_ref[i]).reshape(HALF * 8, 128)
        out_ref[i] = jnp.concatenate([body, slot], axis=0).astype(BF16)


def power_for(values):
    most = jnp.max(jnp.max(jnp.abs(values), axis=0, keepdims=True), axis=1, keepdims=True)
    bits = jnp.log(jnp.maximum(most, 1e-30)) * 1.4426950408889634
    return jnp.clip(jnp.floor(14.0 - bits), -100.0, 100.0)


def share_kernel(in_ref, out_ref):
    rows = HALF * 8
    total = in_ref[0].astype(F32)
    for i in range(1, in_ref.shape[0]):
        total = total + in_ref[i].astype(F32)
    body = total[:rows]
    sums = join_sums(total[rows:])
    index = sublanes_of(sums.shape)
    sums = jnp.where(index < 2, sums, jnp.zeros_like(sums))
    power = power_for(body)
    power_of_sums = power_for(sums)
    slot = split_sums(sums * jnp.exp2(power_of_sums))
    slot = jnp.where(index == 6, power, jnp.where(index == 7, power_of_sums, slot))
    out_ref[:rows] = body * jnp.exp2(power)
    out_ref[rows:] = slot


def last_sum_kernel(scaling, in_ref, half_ref, sums_ref):
    rows = HALF * 8
    total = jnp.zeros((rows, 128), F32)
    sums = jnp.zeros((8, 128), F32)
    for i in range(in_ref.shape[0]):
        slot = in_ref[i, rows:]
        total = total + in_ref[i, :rows] * jnp.exp2(-slot[6:7])
        sums = sums + join_sums(slot) * jnp.exp2(-slot[7:8])
    half_ref[...] = total * scaling
    sums_ref[...] = sums


def finish_kernel(counted, scaling, x_ref, da_ref, norm_ref, sums_ref, gain_ref, out_ref, gain_grad_ref, bias_grad_ref):
    gain = gain_ref[...]
    mean = norm_ref[0:1]
    rstd = norm_ref[8:9]
    sums = sums_ref[...]
    bias_grad_ref[...] = sums[0:1] * scaling
    gain_grad_ref[...] = sums[1:2] * scaling
    averages = group_total(gain * sums) / counted
    leading = averages[0:1]
    trailing = averages[1:2]
    xhat = (x_ref[...].astype(F32).reshape(-1, 128) - mean) * rstd
    grad = rstd * (da_ref[...] * gain - leading - xhat * trailing)
    out_ref[...] = grad.astype(BF16).reshape(out_ref.shape)


def join_kernel(half_ref, other_ref, out_ref):
    left = lax.axis_index("sect") == 0
    half = half_ref[...]
    other = other_ref[...]
    out_ref[: HALF * 8] = jnp.where(left, half, other)
    out_ref[HALF * 8 :] = jnp.where(left, other, half)[: (TAPS - HALF) * 8]


def shape_of(shape, dtype=F32):
    return jax.ShapeDtypeStruct(shape, dtype)


def local(activations, group_norm_gain, group_norm_bias, upstream, kernel):
    frames, height, columns, channels = activations.shape
    n_time, n_rows, n_sect = (lax.axis_size(axis) for axis in ("tm", "rows", "sect"))
    cells = frames * height * columns
    total_cells = cells * n_time * n_rows * n_sect
    counted = float(total_cells * (channels // GROUPS))
    scaling = float(total_cells) ** (-0.5)
    swap = [(0, 1), (1, 0)]
    near = [(i, i ^ 1) for i in range(n_rows)]
    far = [(i, (i - 1) % n_rows if i % 2 == 0 else (i + 1) % n_rows) for i in range(n_rows)]

    up, x, gain, bias, facing, stat = call(
        entry_kernel,
        [
            shape_of(upstream.shape, BF16),
            shape_of(activations.shape, BF16),
            shape_of((1, channels)),
            shape_of((1, channels)),
            shape_of((528, channels), BF16),
            shape_of((8, channels)),
        ],
        [
            held(upstream, pltpu.HBM),
            held(activations, pltpu.HBM),
            held(group_norm_gain.reshape(1, channels), pltpu.HBM),
            held(group_norm_bias.reshape(1, channels), pltpu.HBM),
        ],
        [HBM] * 4,
        [pltpu.SemaphoreType.DMA((4,))],
    )
    side = lax.ppermute(facing, "sect", swap)
    nearer, farther, stat = call(
        edge_kernel,
        [shape_of((208, channels), BF16), shape_of((192, channels), BF16), shape_of((8, channels))],
        [up, side, stat],
    )
    nearer = lax.ppermute(nearer, "rows", near)
    farther = lax.ppermute(farther, "rows", far)
    spread, inner, taps = call(
        own_kernel,
        [
            pltpu.VMEM((8, 256, 1152), BF16),
            shape_of((cells, channels)),
            shape_of((3, channels, 9 * channels), BF16),
        ],
        [up, side, held(kernel, pltpu.HBM)],
        [VMEM, VMEM, HBM],
        [pltpu.VMEM((3, 3, 3, 128, 128), BF16), pltpu.SemaphoreType.DMA],
        flops=cells * TAPS * channels * channels,
    )
    nearer, inner = lax.optimization_barrier((nearer, inner))
    groups = [[t * n_rows + r for t in range(n_time) for r in range(p, n_rows, 2)] for p in range(2)]
    early, stat = call(
        early_kernel,
        [shape_of((2, 10, 48, channels), BF16), shape_of((len(groups[0]), channels))],
        [up, side, nearer, farther, stat],
        [VMEM, VMEM, VMEM, VMEM, VMEM],
    )
    later = lax.ppermute(early, "tm", [(i + 1, i) for i in range(n_time - 1)])
    stat = lax.all_to_all(stat[:, None], ("tm", "rows"), 0, 0, axis_index_groups=groups).reshape(-1, channels)
    stat, later = lax.optimization_barrier((stat, later))
    (spread,) = call(
        spread_kernel,
        [pltpu.VMEM((8, 256, 1152), BF16)],
        [nearer, farther, later, held(spread, pltpu.VMEM)],
        aliases={3: 0},
    )
    away, turned, norm = call(
        functools.partial(away_kernel, counted),
        [shape_of((16, HALF, 8, 128)), shape_of((channels, cells), BF16), shape_of((16, channels))],
        [x, stat, gain, bias, held(spread, pltpu.VMEM)],
        flops=cells * TAPS * channels * channels,
    )
    arrived = lax.ppermute(away, "sect", swap)
    da, sums = call(
        grad_kernel,
        [shape_of((cells, channels)), shape_of((8, channels))],
        [x, norm, gain, bias, taps, inner, held(spread, pltpu.VMEM)],
        scratch=[pltpu.VMEM((cells, channels), F32)],
        flops=cells * TAPS * channels * channels,
    )
    other_sums = lax.ppermute(sums, "sect", swap)
    (home,) = call(
        home_kernel,
        [shape_of((16, HALF, 8, 128))],
        [turned, held(spread, pltpu.VMEM)],
        flops=cells * TAPS * channels * channels,
    )
    (sent,) = call(
        pair_kernel, [shape_of((16, SLOTS * 8, 128), BF16)], [home, arrived, sums, other_sums]
    )
    gathered = lax.all_to_all(sent, "tm", 0, 0)
    (share,) = call(share_kernel, [shape_of((SLOTS * 8, 128))], [gathered])
    share = jnp.broadcast_to(share.astype(jnp.float16)[None], (n_rows, SLOTS * 8, 128))
    shares = lax.all_to_all(share, "rows", 0, 0).astype(F32)
    half, sums = call(
        functools.partial(last_sum_kernel, scaling),
        [shape_of((HALF * 8, 128)), shape_of((8, 128))],
        [shares],
    )
    other = lax.ppermute(half, "sect", swap)
    input_gradient, gain_grad, bias_grad = call(
        functools.partial(finish_kernel, counted, scaling),
        [shape_of(activations.shape, BF16), shape_of((1, 128)), shape_of((1, 128))],
        [x, da, norm, sums, gain],
    )
    (whole,) = call(join_kernel, [shape_of((TAPS * 8, 128))], [half, other])
    weight_grad = whole.reshape(3, 3, 3, 8, 128).transpose(0, 1, 2, 4, 3)
    return (input_gradient, gain_grad.reshape(128), bias_grad.reshape(128), weight_grad)


def solution(mesh):
    return jax.shard_map(
        local,
        mesh=mesh,
        in_specs=(P("tm", "rows", "sect", None), P(), P(), P("tm", "rows", "sect", None), P()),
        out_specs=(P("tm", "rows", "sect", None), P(), P(), P(None, None, None, None, "tm")),
        check_vma=False,
    )
```

```python
import functools
import math

import jax
import jax.numpy as jnp
from jax import lax
from jax.experimental import pallas as pl
from jax.experimental.pallas import tpu as pltpu
from jax.sharding import PartitionSpec as P

GROUPS = 32
TAPS = 27
HALF = 14
SLOTS = HALF + 1
F32 = jnp.float32
BF16 = jnp.bfloat16
VMEM = pl.BlockSpec(memory_space=pltpu.VMEM)
HBM = pl.BlockSpec(memory_space=pltpu.HBM)


def held(x, space):
    return pltpu.with_memory_space_constraint(x, space)


def call(body, outs, args, specs=None, scratch=(), flops=0, aliases=None):
    moved = sum(math.prod(x.shape) * jnp.dtype(x.dtype).itemsize for x in list(args) + list(outs))
    return pl.pallas_call(
        body,
        out_shape=outs,
        in_specs=specs or [VMEM] * len(args),
        out_specs=[VMEM] * len(outs),
        scratch_shapes=list(scratch),
        input_output_aliases=aliases or {},
        cost_estimate=pl.CostEstimate(flops=flops, bytes_accessed=moved, transcendentals=0),
        compiler_params=pltpu.CompilerParams(vmem_limit_bytes=24 * 1024 * 1024),
    )(*args)


def lanes_of(shape):
    return lax.broadcasted_iota(jnp.int32, shape, len(shape) - 1)


def sublanes_of(shape):
    return lax.broadcasted_iota(jnp.int32, shape, len(shape) - 2)


def group_total(v):
    lane = lanes_of(v.shape)
    v = v + jnp.where(lane % 2 == 0, pltpu.roll(v, 127, 1), pltpu.roll(v, 1, 1))
    return v + jnp.where(lane % 4 < 2, pltpu.roll(v, 126, 1), pltpu.roll(v, 2, 1))


def column_sum(v):
    part = jnp.sum(v.reshape(-1, 8, v.shape[-1]), axis=0)
    return jnp.broadcast_to(jnp.sum(part, axis=0, keepdims=True), part.shape)


def split_row(row):
    high = row.astype(BF16).astype(F32)
    middle = (row - high).astype(BF16).astype(F32)
    low = row - high - middle
    index = sublanes_of((8, 128))
    parts = jnp.where(index == 0, high, jnp.where(index == 1, middle, low))
    return jnp.concatenate([parts, parts], axis=0).astype(BF16)


def join_row(parts):
    parts = parts.astype(F32)
    return jnp.broadcast_to(parts[0:1] + parts[1:2] + parts[2:3], (8, 128))


def entry_kernel(up_hbm, x_hbm, gain_hbm, bias_hbm, up_ref, x_ref, gain_ref, bias_ref, facing_ref, stat_ref, sems):
    pairs = ((up_hbm, up_ref), (x_hbm, x_ref), (gain_hbm, gain_ref), (bias_hbm, bias_ref))
    copies = [pltpu.make_async_copy(source, target, sems.at[i]) for i, (source, target) in enumerate(pairs)]
    for copy in copies:
        copy.start()
    copies[0].wait()
    left = lax.axis_index("sect") == 0
    facing = jnp.where(left, up_ref[:, :, 16:].astype(F32)[:, :, 15], up_ref[:, :, :16].astype(F32)[:, :, 0])
    facing_ref[:32] = facing.reshape(32, 128).astype(BF16)
    for copy in copies[1:]:
        copy.wait()
    x = x_ref[...].astype(F32).reshape(-1, 128)
    total = group_total(column_sum(x))
    square = group_total(column_sum(x * x))
    row = jnp.where(lanes_of(total.shape) % 4 < 2, total, square)
    stat_ref[...] = row
    facing_ref[32:] = split_row(row)


def columns_of(side_ref):
    return side_ref[:32].astype(F32).reshape(4, 8, 128)


def edge_of(up_ref, side_ref, bottom, row):
    columns = columns_of(side_ref)
    parts = split_row(row)[:8].astype(F32)[:4]
    tail = [jnp.where(bottom, columns[:, 7], columns[:, 0]), parts, jnp.zeros((8, 128), F32)]
    main = jnp.where(bottom, up_ref[:, 7], up_ref[:, 0]).reshape(128, 128)
    return main, jnp.concatenate(tail, axis=0).astype(BF16)


def edge_kernel(up_ref, side_ref, stat_ref, near_ref, far_ref, sum_ref):
    even = lax.axis_index("rows") % 2 == 0
    row = stat_ref[...] + join_row(side_ref[32:])
    sum_ref[...] = row
    near_ref[:128], near_ref[128:] = edge_of(up_ref, side_ref, even, row)
    far_ref[:128], far_ref[128:] = edge_of(up_ref, side_ref, jnp.logical_not(even), row)


def beyond(near_ref, far_ref):
    even = lax.axis_index("rows") % 2 == 0
    outside = jnp.logical_or(lax.axis_index("rows") == 0, lax.axis_index("rows") == lax.axis_size("rows") - 1)
    near = near_ref[:128].reshape(4, 32, 128)
    far = far_ref[:128].reshape(4, 32, 128)
    far = jnp.where(outside, jnp.zeros_like(far), far)
    near_column = near_ref[128:].astype(F32)[:4]
    far_column = far_ref[128:].astype(F32)[:4]
    far_column = jnp.where(outside, jnp.zeros_like(far_column), far_column)
    above = jnp.where(even, far, near), jnp.where(even, far_column, near_column)
    below = jnp.where(even, near, far), jnp.where(even, near_column, far_column)
    return above, below


def early_kernel(up_ref, side_ref, near_ref, far_ref, stat_ref, early_ref, sent_ref):
    row = stat_ref[...] + join_row(near_ref[128:].astype(F32)[4:8])
    sent_ref[...] = jnp.broadcast_to(row[None], (sent_ref.shape[0] // 8, 8, 128)).reshape(sent_ref.shape)
    (above, above_column), (below, below_column) = beyond(near_ref, far_ref)
    columns = columns_of(side_ref)
    for f in range(2):
        early_ref[f * 320 : f * 320 + 32] = above[f]
        early_ref[f * 320 + 32 : f * 320 + 288] = up_ref[f].reshape(256, 128)
        early_ref[f * 320 + 288 : f * 320 + 320] = below[f]
        column = [above_column[f : f + 1], columns[f], below_column[f : f + 1], jnp.zeros((6, 128), F32)]
        early_ref[640 + f * 16 : 656 + f * 16] = jnp.concatenate(column, axis=0).astype(BF16)


def column_taps(core, beside):
    left = lax.axis_index("sect") == 0
    index = sublanes_of(core.shape)
    first = index == 0
    last = index == 31
    zero = jnp.zeros_like(core)
    beside = jnp.broadcast_to(beside[:, None, :], core.shape)
    ahead = jnp.where(last, jnp.where(left, beside, zero), pltpu.roll(core, 31, 1))
    behind = jnp.where(first, jnp.where(left, zero, beside), pltpu.roll(core, 1, 1))
    ahead = ahead + jnp.where(first, jnp.where(left, core, zero), zero)
    behind = behind + jnp.where(last, jnp.where(left, zero, core), zero)
    return ahead, core, behind


def put(v_ref, f, r, b, e, rows):
    j = (b * 3 + e) * 128
    count = rows.shape[0]
    v_ref[f, r * 32 : (r + count) * 32, j : j + 128] = rows.astype(BF16).reshape(count * 32, 128)


def times_taps(lhs, taps_ref, a):
    return lax.dot_general(lhs, taps_ref[a], (((1,), (1,)), ((), ())), preferred_element_type=F32)


def own_kernel(up_ref, side_ref, kernel_hbm, v_ref, dh_ref, taps_ref, kernel_ref, sem):
    weights = pltpu.make_async_copy(kernel_hbm, kernel_ref, sem)
    weights.start()
    row_first = lax.axis_index("rows") == 0
    row_last = lax.axis_index("rows") == lax.axis_size("rows") - 1
    columns = columns_of(side_ref)
    for f in range(4):
        for e, part in enumerate(column_taps(up_ref[f].astype(F32), columns[f])):
            zero = jnp.zeros_like(part[0])
            top = part[1] + jnp.where(row_first, part[0], zero)
            low = part[6] + jnp.where(row_last, part[7], zero)
            put(v_ref, f, 0, 0, e, top[None])
            put(v_ref, f, 1, 0, e, part[2:8])
            put(v_ref, f, 0, 1, e, part)
            put(v_ref, f, 1, 2, e, part[0:6])
            put(v_ref, f, 7, 2, e, low[None])
    weights.wait()
    for a in range(3):
        for b in range(3):
            for e in range(3):
                j = (b * 3 + e) * 128
                taps_ref[a, :, j : j + 128] = kernel_ref[a, b, e]
    for f in range(4):
        total = None
        for a in range(3):
            if f + 2 - a < 4:
                term = times_taps(v_ref[f + 2 - a, 32:224], taps_ref, a)
                total = term if total is None else total + term
        dh_ref[f * 256 + 32 : f * 256 + 224] = total


def spread_kernel(near_ref, far_ref, later_ref, own_ref, v_ref):
    (above, above_column), (below, below_column) = beyond(near_ref, far_ref)
    row_first = lax.axis_index("rows") == 0
    row_last = lax.axis_index("rows") == lax.axis_size("rows") - 1
    outer = jnp.concatenate([above, below], axis=0).astype(F32)
    outer_column = jnp.concatenate([above_column, below_column], axis=0)
    for e, part in enumerate(column_taps(outer, outer_column)):
        for f in range(4):
            put(v_ref, f, 0, 2, e, part[f : f + 1])
            put(v_ref, f, 7, 0, e, part[f + 4 : f + 5])
    for f in range(2):
        later = later_ref[f * 320 : f * 320 + 320].astype(F32).reshape(10, 32, 128)
        column = later_ref[640 + f * 16 : 656 + f * 16].astype(F32)[:10]
        for e, part in enumerate(column_taps(later, column)):
            zero = jnp.zeros_like(part[0])
            top = part[2] + jnp.where(row_first, part[1], zero)
            low = part[7] + jnp.where(row_last, part[8], zero)
            put(v_ref, f + 4, 0, 0, e, top[None])
            put(v_ref, f + 4, 1, 0, e, part[3:10])
            put(v_ref, f + 4, 0, 1, e, part[1:9])
            put(v_ref, f + 4, 0, 2, e, part[0:7])
            put(v_ref, f + 4, 7, 2, e, low[None])

    @pl.when(lax.axis_index("tm") == 0)
    def _():
        both = v_ref[1].astype(F32) + v_ref[0].astype(F32)
        v_ref[6] = both.astype(BF16)
        v_ref[7] = (both + v_ref[2].astype(F32)).astype(BF16)


def grad_kernel(x_ref, norm_ref, gain_ref, bias_ref, taps_ref, part_ref, v_ref, da_ref, sums_ref, dh_ref):
    def edges(lo, hi):
        return jnp.concatenate([v_ref[lo:hi, 0:32], v_ref[lo:hi, 224:256]], axis=1).reshape((hi - lo) * 64, 1152)

    outer = times_taps(edges(0, 4), taps_ref, 2)
    one = times_taps(edges(1, 4), taps_ref, 1)
    two = times_taps(edges(2, 4), taps_ref, 0)
    outer = outer + jnp.concatenate([one, jnp.zeros((64, 128), F32)], axis=0)
    outer = outer + jnp.concatenate([two, jnp.zeros((128, 128), F32)], axis=0)
    for f in range(4):
        dh_ref[f * 256 : f * 256 + 32] = outer[f * 64 : f * 64 + 32]
        dh_ref[f * 256 + 32 : f * 256 + 224] = part_ref[f * 256 + 32 : f * 256 + 224]
        dh_ref[f * 256 + 224 : f * 256 + 256] = outer[f * 64 + 32 : f * 64 + 64]
    dh_ref[768:1024] += times_taps(v_ref[4], taps_ref, 1)
    dh_ref[512:1024] += times_taps(v_ref[4:6].reshape(512, 1152), taps_ref, 0)

    @pl.when(lax.axis_index("tm") == 0)
    def _():
        dh_ref[0:256] += times_taps(v_ref[0], taps_ref, 1) + times_taps(v_ref[6], taps_ref, 0)

    bias_sum = jnp.zeros((8, 128), F32)
    gain_sum = jnp.zeros((8, 128), F32)
    for block in range(8):
        xhat, pre = block_of(x_ref, norm_ref, gain_ref, bias_ref, block)
        sig = 1.0 / (1.0 + jnp.exp(-pre))
        da = dh_ref[block * 128 : (block + 1) * 128] * sig * (1.0 + pre * (1.0 - sig))
        da_ref[block * 128 : (block + 1) * 128] = da
        bias_sum = bias_sum + jnp.sum(da.reshape(16, 8, 128), axis=0)
        gain_sum = gain_sum + jnp.sum((da * xhat).reshape(16, 8, 128), axis=0)
    sums_ref[...] = jnp.where(sublanes_of((8, 128)) == 0, column_sum(bias_sum), column_sum(gain_sum))


def sums_to_pair(row):
    lane = lanes_of(row.shape)
    total = jnp.where(lane % 4 < 2, row, pltpu.roll(row, 2, 1))
    square = jnp.where(lane % 4 < 2, pltpu.roll(row, 126, 1), row)
    return total, square


def product_of(turned, v_ref, a, lo, hi):
    if a == 2:
        return jnp.dot(turned, v_ref[0:4, :, lo:hi].reshape(1024, hi - lo), preferred_element_type=F32)
    source = jnp.where(lax.axis_index("tm") == 0, 7 - a, 2 - a)
    first = jnp.dot(turned[:, :256], v_ref[source, :, lo:hi], preferred_element_type=F32)
    rest = v_ref[3 - a : 6 - a, :, lo:hi].reshape(768, hi - lo)
    return first + jnp.dot(turned[:, 256:], rest, preferred_element_type=F32)


def half_product(half, turned, v_ref, w_ref):
    for a, lo, hi in (((0, 0, 9), (1, 0, 5)), ((1, 5, 9), (2, 0, 9)))[half]:
        product = product_of(turned, v_ref, a, lo * 128, hi * 128)
        for j in range(lo, hi):
            block = product[:, (j - lo) * 128 : (j - lo + 1) * 128].T.reshape(16, 8, 128)
            w_ref[:, (a * 9 + j) % HALF] = block
    if half == 1:
        w_ref[:, HALF - 1] = jnp.zeros((16, 8, 128), F32)


def block_of(x_ref, norm_ref, gain_ref, bias_ref, block):
    half = (block % 2) * 4
    x = x_ref[block // 2, half : half + 4].astype(F32).reshape(128, 128)
    xhat = (x - norm_ref[0:1]) * norm_ref[8:9]
    return xhat, xhat * gain_ref[...] + bias_ref[...]


def away_kernel(counted, x_ref, stat_ref, gain_ref, bias_ref, v_ref, w_ref, turned_ref, norm_ref):
    total, square = sums_to_pair(column_sum(stat_ref[...]))
    mean = total / counted
    norm_ref[0:8] = mean
    norm_ref[8:16] = lax.rsqrt(square / counted - mean * mean + 1e-06)
    for block in range(8):
        _, pre = block_of(x_ref, norm_ref, gain_ref, bias_ref, block)
        hidden = pre * (1.0 / (1.0 + jnp.exp(-pre)))
        turned_ref[:, block * 128 : (block + 1) * 128] = hidden.T.astype(BF16)
    left = lax.axis_index("sect") == 0

    @pl.when(left)
    def _():
        half_product(1, turned_ref[...], v_ref, w_ref)

    @pl.when(jnp.logical_not(left))
    def _():
        half_product(0, turned_ref[...], v_ref, w_ref)


def home_kernel(turned_ref, v_ref, w_ref):
    left = lax.axis_index("sect") == 0

    @pl.when(left)
    def _():
        half_product(0, turned_ref[...], v_ref, w_ref)

    @pl.when(jnp.logical_not(left))
    def _():
        half_product(1, turned_ref[...], v_ref, w_ref)


def split_sums(sums):
    row = sublanes_of(sums.shape)
    high = sums.astype(BF16).astype(F32)
    middle = (sums - high).astype(BF16).astype(F32)
    low = sums - high - middle
    return jnp.where(
        row < 2, high, jnp.where(row < 4, pltpu.roll(middle, 2, 0), pltpu.roll(low, 4, 0))
    )


def join_sums(parts):
    return parts + pltpu.roll(parts, 6, 0) + pltpu.roll(parts, 4, 0)


def pair_kernel(own_ref, other_ref, sums_ref, other_sums_ref, out_ref):
    slot = split_sums(sums_ref[...] + other_sums_ref[...])
    for i in range(16):
        body = (own_ref[i] + other_ref[i]).reshape(HALF * 8, 128)
        out_ref[i] = jnp.concatenate([body, slot], axis=0).astype(BF16)


def power_for(values):
    most = jnp.max(jnp.max(jnp.abs(values), axis=0, keepdims=True), axis=1, keepdims=True)
    bits = jnp.log(jnp.maximum(most, 1e-30)) * 1.4426950408889634
    return jnp.clip(jnp.floor(14.0 - bits), -100.0, 100.0)


def share_kernel(in_ref, out_ref):
    rows = HALF * 8
    total = in_ref[0].astype(F32)
    for i in range(1, in_ref.shape[0]):
        total = total + in_ref[i].astype(F32)
    body = total[:rows]
    sums = join_sums(total[rows:])
    index = sublanes_of(sums.shape)
    sums = jnp.where(index < 2, sums, jnp.zeros_like(sums))
    power = power_for(body)
    power_of_sums = power_for(sums)
    slot = split_sums(sums * jnp.exp2(power_of_sums))
    slot = jnp.where(index == 6, power, jnp.where(index == 7, power_of_sums, slot))
    out_ref[:rows] = body * jnp.exp2(power)
    out_ref[rows:] = slot


def last_sum_kernel(scaling, in_ref, half_ref, sums_ref):
    rows = HALF * 8
    total = jnp.zeros((rows, 128), F32)
    sums = jnp.zeros((8, 128), F32)
    for i in range(in_ref.shape[0]):
        slot = in_ref[i, rows:]
        total = total + in_ref[i, :rows] * jnp.exp2(-slot[6:7])
        sums = sums + join_sums(slot) * jnp.exp2(-slot[7:8])
    half_ref[...] = total * scaling
    sums_ref[...] = sums


def finish_kernel(counted, scaling, x_ref, da_ref, norm_ref, sums_ref, gain_ref, out_ref, gain_grad_ref, bias_grad_ref):
    gain = gain_ref[...]
    mean = norm_ref[0:1]
    rstd = norm_ref[8:9]
    sums = sums_ref[...]
    bias_grad_ref[...] = sums[0:1] * scaling
    gain_grad_ref[...] = sums[1:2] * scaling
    averages = group_total(gain * sums) / counted
    leading = averages[0:1]
    trailing = averages[1:2]
    xhat = (x_ref[...].astype(F32).reshape(-1, 128) - mean) * rstd
    grad = rstd * (da_ref[...] * gain - leading - xhat * trailing)
    out_ref[...] = grad.astype(BF16).reshape(out_ref.shape)


def join_kernel(half_ref, other_ref, out_ref):
    left = lax.axis_index("sect") == 0
    half = half_ref[...]
    other = other_ref[...]
    out_ref[: HALF * 8] = jnp.where(left, half, other)
    out_ref[HALF * 8 :] = jnp.where(left, other, half)[: (TAPS - HALF) * 8]


def shape_of(shape, dtype=F32):
    return jax.ShapeDtypeStruct(shape, dtype)


def local(activations, group_norm_gain, group_norm_bias, upstream, kernel):
    frames, height, columns, channels = activations.shape
    n_time, n_rows, n_sect = (lax.axis_size(axis) for axis in ("tm", "rows", "sect"))
    cells = frames * height * columns
    total_cells = cells * n_time * n_rows * n_sect
    counted = float(total_cells * (channels // GROUPS))
    scaling = float(total_cells) ** (-0.5)
    swap = [(0, 1), (1, 0)]
    near = [(i, i ^ 1) for i in range(n_rows)]
    far = [(i, (i - 1) % n_rows if i % 2 == 0 else (i + 1) % n_rows) for i in range(n_rows)]

    up, x, gain, bias, facing, stat = call(
        entry_kernel,
        [
            shape_of(upstream.shape, BF16),
            shape_of(activations.shape, BF16),
            shape_of((1, channels)),
            shape_of((1, channels)),
            shape_of((48, channels), BF16),
            shape_of((8, channels)),
        ],
        [
            held(upstream, pltpu.HBM),
            held(activations, pltpu.HBM),
            held(group_norm_gain.reshape(1, channels), pltpu.HBM),
            held(group_norm_bias.reshape(1, channels), pltpu.HBM),
        ],
        [HBM] * 4,
        [pltpu.SemaphoreType.DMA((4,))],
    )
    side = lax.ppermute(facing, "sect", swap)
    nearer, farther, stat = call(
        edge_kernel,
        [shape_of((144, channels), BF16), shape_of((144, channels), BF16), shape_of((8, channels))],
        [up, side, stat],
    )
    nearer = lax.ppermute(nearer, "rows", near)
    farther = lax.ppermute(farther, "rows", far)
    spread, inner, taps = call(
        own_kernel,
        [
            pltpu.VMEM((8, 256, 1152), BF16),
            shape_of((cells, channels)),
            shape_of((3, channels, 9 * channels), BF16),
        ],
        [up, side, held(kernel, pltpu.HBM)],
        [VMEM, VMEM, HBM],
        [pltpu.VMEM((3, 3, 3, 128, 128), BF16), pltpu.SemaphoreType.DMA],
        flops=cells * TAPS * channels * channels,
    )
    nearer, inner = lax.optimization_barrier((nearer, inner))
    groups = [[t * n_rows + r for t in range(n_time) for r in range(p, n_rows, 2)] for p in range(2)]
    early, stat = call(
        early_kernel,
        [shape_of((672, channels), BF16), shape_of((len(groups[0]), channels))],
        [up, side, nearer, farther, stat],
        [VMEM, VMEM, VMEM, VMEM, VMEM],
    )
    later = lax.ppermute(early, "tm", [(i + 1, i) for i in range(n_time - 1)])
    stat = lax.all_to_all(stat[:, None], ("tm", "rows"), 0, 0, axis_index_groups=groups).reshape(-1, channels)
    stat, later = lax.optimization_barrier((stat, later))
    (spread,) = call(
        spread_kernel,
        [pltpu.VMEM((8, 256, 1152), BF16)],
        [nearer, farther, later, held(spread, pltpu.VMEM)],
        aliases={3: 0},
    )
    away, turned, norm = call(
        functools.partial(away_kernel, counted),
        [shape_of((16, HALF, 8, 128)), shape_of((channels, cells), BF16), shape_of((16, channels))],
        [x, stat, gain, bias, held(spread, pltpu.VMEM)],
        flops=cells * TAPS * channels * channels,
    )
    arrived = lax.ppermute(away, "sect", swap)
    da, sums = call(
        grad_kernel,
        [shape_of((cells, channels)), shape_of((8, channels))],
        [x, norm, gain, bias, taps, inner, held(spread, pltpu.VMEM)],
        scratch=[pltpu.VMEM((cells, channels), F32)],
        flops=cells * TAPS * channels * channels,
    )
    other_sums = lax.ppermute(sums, "sect", swap)
    (home,) = call(
        home_kernel,
        [shape_of((16, HALF, 8, 128))],
        [turned, held(spread, pltpu.VMEM)],
        flops=cells * TAPS * channels * channels,
    )
    (sent,) = call(
        pair_kernel, [shape_of((16, SLOTS * 8, 128), BF16)], [home, arrived, sums, other_sums]
    )
    gathered = lax.all_to_all(sent, "tm", 0, 0)
    (share,) = call(share_kernel, [shape_of((SLOTS * 8, 128))], [gathered])
    share = jnp.broadcast_to(share.astype(jnp.float16)[None], (n_rows, SLOTS * 8, 128))
    shares = lax.all_to_all(share, "rows", 0, 0).astype(F32)
    half, sums = call(
        functools.partial(last_sum_kernel, scaling),
        [shape_of((HALF * 8, 128)), shape_of((8, 128))],
        [shares],
    )
    other = lax.ppermute(half, "sect", swap)
    input_gradient, gain_grad, bias_grad = call(
        functools.partial(finish_kernel, counted, scaling),
        [shape_of(activations.shape, BF16), shape_of((1, 128)), shape_of((1, 128))],
        [x, da, norm, sums, gain],
    )
    (whole,) = call(join_kernel, [shape_of((TAPS * 8, 128))], [half, other])
    weight_grad = whole.reshape(3, 3, 3, 8, 128).transpose(0, 1, 2, 4, 3)
    return (input_gradient, gain_grad.reshape(128), bias_grad.reshape(128), weight_grad)


def solution(mesh):
    return jax.shard_map(
        local,
        mesh=mesh,
        in_specs=(P("tm", "rows", "sect", None), P(), P(), P("tm", "rows", "sect", None), P()),
        out_specs=(P("tm", "rows", "sect", None), P(), P(), P(None, None, None, None, "tm")),
        check_vma=False,
    )
```

```python
import functools
import math

import jax
import jax.numpy as jnp
from jax import lax
from jax.experimental import pallas as pl
from jax.experimental.pallas import tpu as pltpu
from jax.sharding import PartitionSpec as P

GROUPS = 32
TAPS = 27
HALF = 14
SLOTS = HALF + 1
F32 = jnp.float32
BF16 = jnp.bfloat16
VMEM = pl.BlockSpec(memory_space=pltpu.VMEM)
HBM = pl.BlockSpec(memory_space=pltpu.HBM)


def held(x, space):
    return pltpu.with_memory_space_constraint(x, space)


def call(body, outs, args, specs=None, scratch=(), flops=0, aliases=None):
    moved = sum(math.prod(x.shape) * jnp.dtype(x.dtype).itemsize for x in list(args) + list(outs))
    return pl.pallas_call(
        body,
        out_shape=outs,
        in_specs=specs or [VMEM] * len(args),
        out_specs=[VMEM] * len(outs),
        scratch_shapes=list(scratch),
        input_output_aliases=aliases or {},
        cost_estimate=pl.CostEstimate(flops=flops, bytes_accessed=moved, transcendentals=0),
        compiler_params=pltpu.CompilerParams(vmem_limit_bytes=24 * 1024 * 1024),
    )(*args)


def lanes_of(shape):
    return lax.broadcasted_iota(jnp.int32, shape, len(shape) - 1)


def sublanes_of(shape):
    return lax.broadcasted_iota(jnp.int32, shape, len(shape) - 2)


def group_total(v):
    lane = lanes_of(v.shape)
    v = v + jnp.where(lane % 2 == 0, pltpu.roll(v, 127, 1), pltpu.roll(v, 1, 1))
    return v + jnp.where(lane % 4 < 2, pltpu.roll(v, 126, 1), pltpu.roll(v, 2, 1))


def column_sum(v):
    part = jnp.sum(v.reshape(-1, 8, v.shape[-1]), axis=0)
    return jnp.broadcast_to(jnp.sum(part, axis=0, keepdims=True), part.shape)


def split_row(row):
    high = row.astype(BF16).astype(F32)
    middle = (row - high).astype(BF16).astype(F32)
    low = row - high - middle
    index = sublanes_of((8, 128))
    parts = jnp.where(index == 0, high, jnp.where(index == 1, middle, low))
    return jnp.concatenate([parts, parts], axis=0).astype(BF16)


def join_row(parts):
    parts = parts.astype(F32)
    return jnp.broadcast_to(parts[0:1] + parts[1:2] + parts[2:3], (8, 128))


def entry_kernel(up_hbm, x_hbm, gain_hbm, bias_hbm, up_ref, x_ref, gain_ref, bias_ref, facing_ref, stat_ref, sems):
    pairs = ((up_hbm, up_ref), (x_hbm, x_ref), (gain_hbm, gain_ref), (bias_hbm, bias_ref))
    copies = [pltpu.make_async_copy(source, target, sems.at[i]) for i, (source, target) in enumerate(pairs)]
    for copy in copies:
        copy.start()
    copies[0].wait()
    left = lax.axis_index("sect") == 0
    facing = jnp.where(left, up_ref[:, :, 16:].astype(F32)[:, :, 15], up_ref[:, :, :16].astype(F32)[:, :, 0])
    facing_ref[:32] = facing.reshape(32, 128).astype(BF16)
    for copy in copies[1:]:
        copy.wait()
    x = x_ref[...].astype(F32).reshape(-1, 128)
    total = group_total(column_sum(x))
    square = group_total(column_sum(x * x))
    row = jnp.where(lanes_of(total.shape) % 4 < 2, total, square)
    stat_ref[...] = row
    facing_ref[32:] = split_row(row)


def columns_of(side_ref):
    return side_ref[:32].astype(F32).reshape(4, 8, 128)


def edge_of(up_ref, side_ref, bottom, row):
    columns = columns_of(side_ref)
    parts = split_row(row)[:8].astype(F32)[:4]
    tail = [jnp.where(bottom, columns[:, 7], columns[:, 0]), parts, jnp.zeros((8, 128), F32)]
    main = jnp.where(bottom, up_ref[:, 7], up_ref[:, 0]).reshape(128, 128)
    return main, jnp.concatenate(tail, axis=0).astype(BF16)


def edge_kernel(up_ref, side_ref, stat_ref, near_ref, far_ref, sum_ref):
    even = lax.axis_index("rows") % 2 == 0
    row = stat_ref[...] + join_row(side_ref[32:])
    sum_ref[...] = row
    near_ref[:128], near_ref[128:] = edge_of(up_ref, side_ref, even, row)
    far_ref[:128], far_ref[128:] = edge_of(up_ref, side_ref, jnp.logical_not(even), row)


def beyond(near_ref, far_ref):
    even = lax.axis_index("rows") % 2 == 0
    outside = jnp.logical_or(lax.axis_index("rows") == 0, lax.axis_index("rows") == lax.axis_size("rows") - 1)
    near = near_ref[:128].reshape(4, 32, 128)
    far = far_ref[:128].reshape(4, 32, 128)
    far = jnp.where(outside, jnp.zeros_like(far), far)
    near_column = near_ref[128:].astype(F32)[:4]
    far_column = far_ref[128:].astype(F32)[:4]
    far_column = jnp.where(outside, jnp.zeros_like(far_column), far_column)
    above = jnp.where(even, far, near), jnp.where(even, far_column, near_column)
    below = jnp.where(even, near, far), jnp.where(even, near_column, far_column)
    return above, below


def early_kernel(up_ref, side_ref, near_ref, far_ref, stat_ref, early_ref, sent_ref):
    row = stat_ref[...] + join_row(near_ref[128:].astype(F32)[4:8])
    sent_ref[...] = jnp.broadcast_to(row[None], (sent_ref.shape[0] // 8, 8, 128)).reshape(sent_ref.shape)
    (above, above_column), (below, below_column) = beyond(near_ref, far_ref)
    columns = columns_of(side_ref)
    for f in range(2):
        early_ref[f * 320 : f * 320 + 32] = above[f]
        early_ref[f * 320 + 32 : f * 320 + 288] = up_ref[f].reshape(256, 128)
        early_ref[f * 320 + 288 : f * 320 + 320] = below[f]
        column = [above_column[f : f + 1], columns[f], below_column[f : f + 1], jnp.zeros((6, 128), F32)]
        early_ref[640 + f * 16 : 656 + f * 16] = jnp.concatenate(column, axis=0).astype(BF16)


def column_taps(core, beside):
    left = lax.axis_index("sect") == 0
    index = sublanes_of(core.shape)
    first = index == 0
    last = index == 31
    zero = jnp.zeros_like(core)
    beside = jnp.broadcast_to(beside[:, None, :], core.shape)
    ahead = jnp.where(last, jnp.where(left, beside, zero), pltpu.roll(core, 31, 1))
    behind = jnp.where(first, jnp.where(left, zero, beside), pltpu.roll(core, 1, 1))
    ahead = ahead + jnp.where(first, jnp.where(left, core, zero), zero)
    behind = behind + jnp.where(last, jnp.where(left, zero, core), zero)
    return ahead, core, behind


def put(v_ref, f, r, b, e, rows):
    j = (b * 3 + e) * 128
    count = rows.shape[0]
    v_ref[f, r * 32 : (r + count) * 32, j : j + 128] = rows.astype(BF16).reshape(count * 32, 128)


def times_taps(lhs, taps_ref, a):
    return lax.dot_general(lhs, taps_ref[a], (((1,), (1,)), ((), ())), preferred_element_type=F32)


def own_kernel(up_ref, side_ref, kernel_hbm, v_ref, dh_ref, taps_ref, kernel_ref, sem):
    weights = pltpu.make_async_copy(kernel_hbm, kernel_ref, sem)
    weights.start()
    row_first = lax.axis_index("rows") == 0
    row_last = lax.axis_index("rows") == lax.axis_size("rows") - 1
    columns = columns_of(side_ref)
    for f in range(4):
        for e, part in enumerate(column_taps(up_ref[f].astype(F32), columns[f])):
            zero = jnp.zeros_like(part[0])
            top = part[1] + jnp.where(row_first, part[0], zero)
            low = part[6] + jnp.where(row_last, part[7], zero)
            put(v_ref, f, 0, 0, e, top[None])
            put(v_ref, f, 1, 0, e, part[2:8])
            put(v_ref, f, 0, 1, e, part)
            put(v_ref, f, 1, 2, e, part[0:6])
            put(v_ref, f, 7, 2, e, low[None])
    weights.wait()
    for a in range(3):
        for b in range(3):
            for e in range(3):
                j = (b * 3 + e) * 128
                taps_ref[a, :, j : j + 128] = kernel_ref[a, b, e]
    for f in range(4):
        total = None
        for a in range(3):
            if f + 2 - a < 4:
                term = times_taps(v_ref[f + 2 - a, 32:224], taps_ref, a)
                total = term if total is None else total + term
        dh_ref[f * 256 + 32 : f * 256 + 224] = total


def spread_kernel(near_ref, far_ref, later_ref, own_ref, v_ref):
    (above, above_column), (below, below_column) = beyond(near_ref, far_ref)
    row_first = lax.axis_index("rows") == 0
    row_last = lax.axis_index("rows") == lax.axis_size("rows") - 1
    outer = jnp.concatenate([above, below], axis=0).astype(F32)
    outer_column = jnp.concatenate([above_column, below_column], axis=0)
    for e, part in enumerate(column_taps(outer, outer_column)):
        for f in range(4):
            put(v_ref, f, 0, 2, e, part[f : f + 1])
            put(v_ref, f, 7, 0, e, part[f + 4 : f + 5])
    for f in range(2):
        later = later_ref[f * 320 : f * 320 + 320].astype(F32).reshape(10, 32, 128)
        column = later_ref[640 + f * 16 : 656 + f * 16].astype(F32)[:10]
        for e, part in enumerate(column_taps(later, column)):
            zero = jnp.zeros_like(part[0])
            top = part[2] + jnp.where(row_first, part[1], zero)
            low = part[7] + jnp.where(row_last, part[8], zero)
            put(v_ref, f + 4, 0, 0, e, top[None])
            put(v_ref, f + 4, 1, 0, e, part[3:10])
            put(v_ref, f + 4, 0, 1, e, part[1:9])
            put(v_ref, f + 4, 0, 2, e, part[0:7])
            put(v_ref, f + 4, 7, 2, e, low[None])

    @pl.when(lax.axis_index("tm") == 0)
    def _():
        both = v_ref[1].astype(F32) + v_ref[0].astype(F32)
        v_ref[6] = both.astype(BF16)
        v_ref[7] = (both + v_ref[2].astype(F32)).astype(BF16)


def grad_kernel(x_ref, norm_ref, gain_ref, bias_ref, taps_ref, part_ref, v_ref, da_ref, sums_ref, dh_ref):
    def edges(lo, hi):
        return jnp.concatenate([v_ref[lo:hi, 0:32], v_ref[lo:hi, 224:256]], axis=1).reshape((hi - lo) * 64, 1152)

    outer = times_taps(edges(0, 4), taps_ref, 2)
    one = times_taps(edges(1, 4), taps_ref, 1)
    two = times_taps(edges(2, 4), taps_ref, 0)
    outer = outer + jnp.concatenate([one, jnp.zeros((64, 128), F32)], axis=0)
    outer = outer + jnp.concatenate([two, jnp.zeros((128, 128), F32)], axis=0)
    for f in range(4):
        dh_ref[f * 256 : f * 256 + 32] = outer[f * 64 : f * 64 + 32]
        dh_ref[f * 256 + 32 : f * 256 + 224] = part_ref[f * 256 + 32 : f * 256 + 224]
        dh_ref[f * 256 + 224 : f * 256 + 256] = outer[f * 64 + 32 : f * 64 + 64]
    dh_ref[768:1024] += times_taps(v_ref[4], taps_ref, 1)
    dh_ref[512:1024] += times_taps(v_ref[4:6].reshape(512, 1152), taps_ref, 0)

    @pl.when(lax.axis_index("tm") == 0)
    def _():
        dh_ref[0:256] += times_taps(v_ref[0], taps_ref, 1) + times_taps(v_ref[6], taps_ref, 0)

    bias_sum = jnp.zeros((8, 128), F32)
    gain_sum = jnp.zeros((8, 128), F32)
    for block in range(8):
        xhat, pre = block_of(x_ref, norm_ref, gain_ref, bias_ref, block)
        sig = 1.0 / (1.0 + jnp.exp(-pre))
        da = dh_ref[block * 128 : (block + 1) * 128] * sig * (1.0 + pre * (1.0 - sig))
        da_ref[block * 128 : (block + 1) * 128] = da
        bias_sum = bias_sum + jnp.sum(da.reshape(16, 8, 128), axis=0)
        gain_sum = gain_sum + jnp.sum((da * xhat).reshape(16, 8, 128), axis=0)
    sums_ref[...] = jnp.where(sublanes_of((8, 128)) == 0, column_sum(bias_sum), column_sum(gain_sum))


def sums_to_pair(row):
    lane = lanes_of(row.shape)
    total = jnp.where(lane % 4 < 2, row, pltpu.roll(row, 2, 1))
    square = jnp.where(lane % 4 < 2, pltpu.roll(row, 126, 1), row)
    return total, square


def product_of(turned, v_ref, a, lo, hi):
    if a == 2:
        return jnp.dot(turned, v_ref[0:4, :, lo:hi].reshape(1024, hi - lo), preferred_element_type=F32)
    source = jnp.where(lax.axis_index("tm") == 0, 7 - a, 2 - a)
    first = jnp.dot(turned[:, :256], v_ref[source, :, lo:hi], preferred_element_type=F32)
    rest = v_ref[3 - a : 6 - a, :, lo:hi].reshape(768, hi - lo)
    return first + jnp.dot(turned[:, 256:], rest, preferred_element_type=F32)


def half_product(half, turned, v_ref, w_ref):
    for a, lo, hi in (((0, 0, 9), (1, 0, 5)), ((1, 5, 9), (2, 0, 9)))[half]:
        product = product_of(turned, v_ref, a, lo * 128, hi * 128)
        for j in range(lo, hi):
            block = product[:, (j - lo) * 128 : (j - lo + 1) * 128].T.reshape(16, 8, 128)
            w_ref[:, (a * 9 + j) % HALF] = block
    if half == 1:
        w_ref[:, HALF - 1] = jnp.zeros((16, 8, 128), F32)


def block_of(x_ref, norm_ref, gain_ref, bias_ref, block):
    half = (block % 2) * 4
    x = x_ref[block // 2, half : half + 4].astype(F32).reshape(128, 128)
    xhat = (x - norm_ref[0:1]) * norm_ref[8:9]
    return xhat, xhat * gain_ref[...] + bias_ref[...]


def away_kernel(counted, x_ref, stat_ref, gain_ref, bias_ref, v_ref, w_ref, turned_ref, norm_ref):
    total, square = sums_to_pair(column_sum(stat_ref[...]))
    mean = total / counted
    norm_ref[0:8] = mean
    norm_ref[8:16] = lax.rsqrt(square / counted - mean * mean + 1e-06)
    for block in range(8):
        _, pre = block_of(x_ref, norm_ref, gain_ref, bias_ref, block)
        hidden = pre * (1.0 / (1.0 + jnp.exp(-pre)))
        turned_ref[:, block * 128 : (block + 1) * 128] = hidden.T.astype(BF16)
    left = lax.axis_index("sect") == 0

    @pl.when(left)
    def _():
        half_product(1, turned_ref[...], v_ref, w_ref)

    @pl.when(jnp.logical_not(left))
    def _():
        half_product(0, turned_ref[...], v_ref, w_ref)


def home_kernel(turned_ref, v_ref, w_ref):
    left = lax.axis_index("sect") == 0

    @pl.when(left)
    def _():
        half_product(0, turned_ref[...], v_ref, w_ref)

    @pl.when(jnp.logical_not(left))
    def _():
        half_product(1, turned_ref[...], v_ref, w_ref)


def split_sums(sums):
    row = sublanes_of(sums.shape)
    high = sums.astype(BF16).astype(F32)
    middle = (sums - high).astype(BF16).astype(F32)
    low = sums - high - middle
    return jnp.where(
        row < 2, high, jnp.where(row < 4, pltpu.roll(middle, 2, 0), pltpu.roll(low, 4, 0))
    )


def join_sums(parts):
    return parts + pltpu.roll(parts, 6, 0) + pltpu.roll(parts, 4, 0)


def pair_kernel(own_ref, other_ref, sums_ref, other_sums_ref, out_ref):
    slot = split_sums(sums_ref[...] + other_sums_ref[...])
    for i in range(16):
        body = (own_ref[i] + other_ref[i]).reshape(HALF * 8, 128)
        out_ref[i] = jnp.concatenate([body, slot], axis=0).astype(BF16)


def power_for(values):
    most = jnp.max(jnp.max(jnp.abs(values), axis=0, keepdims=True), axis=1, keepdims=True)
    bits = jnp.log(jnp.maximum(most, 1e-30)) * 1.4426950408889634
    return jnp.clip(jnp.floor(14.0 - bits), -100.0, 100.0)


def share_kernel(in_ref, out_ref):
    rows = HALF * 8
    total = in_ref[0].astype(F32)
    for i in range(1, in_ref.shape[0]):
        total = total + in_ref[i].astype(F32)
    body = total[:rows]
    sums = join_sums(total[rows:])
    index = sublanes_of(sums.shape)
    sums = jnp.where(index < 2, sums, jnp.zeros_like(sums))
    power = power_for(body)
    power_of_sums = power_for(sums)
    slot = split_sums(sums * jnp.exp2(power_of_sums))
    slot = jnp.where(index == 6, power, jnp.where(index == 7, power_of_sums, slot))
    out_ref[:rows] = body * jnp.exp2(power)
    out_ref[rows:] = slot


def last_sum_kernel(scaling, in_ref, half_ref, sums_ref):
    rows = HALF * 8
    total = jnp.zeros((rows, 128), F32)
    sums = jnp.zeros((8, 128), F32)
    for i in range(in_ref.shape[0]):
        slot = in_ref[i, rows:]
        total = total + in_ref[i, :rows] * jnp.exp2(-slot[6:7])
        sums = sums + join_sums(slot) * jnp.exp2(-slot[7:8])
    half_ref[...] = total * scaling
    sums_ref[...] = sums


def finish_kernel(counted, scaling, x_ref, da_ref, norm_ref, sums_ref, gain_ref, out_ref, gain_grad_ref, bias_grad_ref):
    gain = gain_ref[...]
    mean = norm_ref[0:1]
    rstd = norm_ref[8:9]
    sums = sums_ref[...]
    bias_grad_ref[...] = sums[0:1] * scaling
    gain_grad_ref[...] = sums[1:2] * scaling
    averages = group_total(gain * sums) / counted
    leading = averages[0:1]
    trailing = averages[1:2]
    xhat = (x_ref[...].astype(F32).reshape(-1, 128) - mean) * rstd
    grad = rstd * (da_ref[...] * gain - leading - xhat * trailing)
    out_ref[...] = grad.astype(BF16).reshape(out_ref.shape)


def join_kernel(half_ref, other_ref, out_ref):
    left = lax.axis_index("sect") == 0
    half = half_ref[...]
    other = other_ref[...]
    out_ref[: HALF * 8] = jnp.where(left, half, other)
    out_ref[HALF * 8 :] = jnp.where(left, other, half)[: (TAPS - HALF) * 8]


def shape_of(shape, dtype=F32):
    return jax.ShapeDtypeStruct(shape, dtype)


def local(activations, group_norm_gain, group_norm_bias, upstream, kernel):
    frames, height, columns, channels = activations.shape
    n_time, n_rows, n_sect = (lax.axis_size(axis) for axis in ("tm", "rows", "sect"))
    cells = frames * height * columns
    total_cells = cells * n_time * n_rows * n_sect
    counted = float(total_cells * (channels // GROUPS))
    scaling = float(total_cells) ** (-0.5)
    swap = [(0, 1), (1, 0)]
    near = [(i, i ^ 1) for i in range(n_rows)]
    far = [(i, (i - 1) % n_rows if i % 2 == 0 else (i + 1) % n_rows) for i in range(n_rows)]

    up, x, gain, bias, facing, stat = call(
        entry_kernel,
        [
            shape_of(upstream.shape, BF16),
            shape_of(activations.shape, BF16),
            shape_of((1, channels)),
            shape_of((1, channels)),
            shape_of((48, channels), BF16),
            shape_of((8, channels)),
        ],
        [
            held(upstream, pltpu.HBM),
            held(activations, pltpu.HBM),
            held(group_norm_gain.reshape(1, channels), pltpu.HBM),
            held(group_norm_bias.reshape(1, channels), pltpu.HBM),
        ],
        [HBM] * 4,
        [pltpu.SemaphoreType.DMA((4,))],
    )
    side = lax.ppermute(facing, "sect", swap)
    nearer, farther, stat = call(
        edge_kernel,
        [shape_of((144, channels), BF16), shape_of((144, channels), BF16), shape_of((8, channels))],
        [up, side, stat],
    )
    nearer = lax.ppermute(nearer, "rows", near)
    farther = lax.ppermute(farther, "rows", far)
    spread, inner, taps = call(
        own_kernel,
        [
            pltpu.VMEM((8, 256, 1152), BF16),
            shape_of((cells, channels)),
            shape_of((3, channels, 9 * channels), BF16),
        ],
        [up, side, held(kernel, pltpu.HBM)],
        [VMEM, VMEM, HBM],
        [pltpu.VMEM((3, 3, 3, 128, 128), BF16), pltpu.SemaphoreType.DMA],
        flops=cells * TAPS * channels * channels,
    )
    nearer, inner = lax.optimization_barrier((nearer, inner))
    groups = [[t * n_rows + r for t in range(n_time) for r in chosen] for chosen in ((1, 2, 4, 7), (0, 3, 5, 6))]
    early, stat = call(
        early_kernel,
        [shape_of((672, channels), BF16), shape_of((len(groups[0]), channels))],
        [up, side, nearer, farther, stat],
        [VMEM, VMEM, VMEM, VMEM, VMEM],
    )
    later = lax.ppermute(early, "tm", [(i + 1, i) for i in range(n_time - 1)])
    stat = lax.all_to_all(stat[:, None], ("tm", "rows"), 0, 0, axis_index_groups=groups).reshape(-1, channels)
    stat, later = lax.optimization_barrier((stat, later))
    (spread,) = call(
        spread_kernel,
        [pltpu.VMEM((8, 256, 1152), BF16)],
        [nearer, farther, later, held(spread, pltpu.VMEM)],
        aliases={3: 0},
    )
    away, turned, norm = call(
        functools.partial(away_kernel, counted),
        [shape_of((16, HALF, 8, 128)), shape_of((channels, cells), BF16), shape_of((16, channels))],
        [x, stat, gain, bias, held(spread, pltpu.VMEM)],
        flops=cells * TAPS * channels * channels,
    )
    arrived = lax.ppermute(away, "sect", swap)
    da, sums = call(
        grad_kernel,
        [shape_of((cells, channels)), shape_of((8, channels))],
        [x, norm, gain, bias, taps, inner, held(spread, pltpu.VMEM)],
        scratch=[pltpu.VMEM((cells, channels), F32)],
        flops=cells * TAPS * channels * channels,
    )
    other_sums = lax.ppermute(sums, "sect", swap)
    (home,) = call(
        home_kernel,
        [shape_of((16, HALF, 8, 128))],
        [turned, held(spread, pltpu.VMEM)],
        flops=cells * TAPS * channels * channels,
    )
    (sent,) = call(
        pair_kernel, [shape_of((16, SLOTS * 8, 128), BF16)], [home, arrived, sums, other_sums]
    )
    gathered = lax.all_to_all(sent, "tm", 0, 0)
    (share,) = call(share_kernel, [shape_of((SLOTS * 8, 128))], [gathered])
    share = jnp.broadcast_to(share.astype(jnp.float16)[None], (n_rows, SLOTS * 8, 128))
    shares = lax.all_to_all(share, "rows", 0, 0).astype(F32)
    half, sums = call(
        functools.partial(last_sum_kernel, scaling),
        [shape_of((HALF * 8, 128)), shape_of((8, 128))],
        [shares],
    )
    other = lax.ppermute(half, "sect", swap)
    input_gradient, gain_grad, bias_grad = call(
        functools.partial(finish_kernel, counted, scaling),
        [shape_of(activations.shape, BF16), shape_of((1, 128)), shape_of((1, 128))],
        [x, da, norm, sums, gain],
    )
    (whole,) = call(join_kernel, [shape_of((TAPS * 8, 128))], [half, other])
    weight_grad = whole.reshape(3, 3, 3, 8, 128).transpose(0, 1, 2, 4, 3)
    return (input_gradient, gain_grad.reshape(128), bias_grad.reshape(128), weight_grad)


def solution(mesh):
    return jax.shard_map(
        local,
        mesh=mesh,
        in_specs=(P("tm", "rows", "sect", None), P(), P(), P("tm", "rows", "sect", None), P()),
        out_specs=(P("tm", "rows", "sect", None), P(), P(), P(None, None, None, None, "tm")),
        check_vma=False,
    )
```

```python
import functools
import math

import jax
import jax.numpy as jnp
from jax import lax
from jax.experimental import pallas as pl
from jax.experimental.pallas import tpu as pltpu
from jax.sharding import PartitionSpec as P

GROUPS = 32
TAPS = 27
HALF = 14
SLOTS = HALF + 1
F32 = jnp.float32
BF16 = jnp.bfloat16
VMEM = pl.BlockSpec(memory_space=pltpu.VMEM)
HBM = pl.BlockSpec(memory_space=pltpu.HBM)


def held(x, space):
    return pltpu.with_memory_space_constraint(x, space)


def call(body, outs, args, specs=None, scratch=(), flops=0, aliases=None):
    moved = sum(math.prod(x.shape) * jnp.dtype(x.dtype).itemsize for x in list(args) + list(outs))
    return pl.pallas_call(
        body,
        out_shape=outs,
        in_specs=specs or [VMEM] * len(args),
        out_specs=[VMEM] * len(outs),
        scratch_shapes=list(scratch),
        input_output_aliases=aliases or {},
        cost_estimate=pl.CostEstimate(flops=flops, bytes_accessed=moved, transcendentals=0),
        compiler_params=pltpu.CompilerParams(vmem_limit_bytes=24 * 1024 * 1024),
    )(*args)


def lanes_of(shape):
    return lax.broadcasted_iota(jnp.int32, shape, len(shape) - 1)


def sublanes_of(shape):
    return lax.broadcasted_iota(jnp.int32, shape, len(shape) - 2)


def group_total(v):
    lane = lanes_of(v.shape)
    v = v + jnp.where(lane % 2 == 0, pltpu.roll(v, 127, 1), pltpu.roll(v, 1, 1))
    return v + jnp.where(lane % 4 < 2, pltpu.roll(v, 126, 1), pltpu.roll(v, 2, 1))


def column_sum(v):
    part = jnp.sum(v.reshape(-1, 8, v.shape[-1]), axis=0)
    return jnp.broadcast_to(jnp.sum(part, axis=0, keepdims=True), part.shape)


def split_row(row):
    high = row.astype(BF16).astype(F32)
    middle = (row - high).astype(BF16).astype(F32)
    low = row - high - middle
    index = sublanes_of((8, 128))
    parts = jnp.where(index == 0, high, jnp.where(index == 1, middle, low))
    return jnp.concatenate([parts, parts], axis=0).astype(BF16)


def join_row(parts):
    parts = parts.astype(F32)
    return jnp.broadcast_to(parts[0:1] + parts[1:2] + parts[2:3], (8, 128))


def entry_kernel(
    up_hbm, x_hbm, gain_hbm, bias_hbm, kernel_hbm, up_ref, x_ref, gain_ref, bias_ref, kernel_ref, facing_ref, stat_ref, sems
):
    pairs = ((up_hbm, up_ref), (x_hbm, x_ref), (gain_hbm, gain_ref), (bias_hbm, bias_ref), (kernel_hbm, kernel_ref))
    copies = [pltpu.make_async_copy(source, target, sems.at[i]) for i, (source, target) in enumerate(pairs)]
    for copy in copies:
        copy.start()
    copies[0].wait()
    left = lax.axis_index("sect") == 0
    facing = jnp.where(left, up_ref[:, :, 16:].astype(F32)[:, :, 15], up_ref[:, :, :16].astype(F32)[:, :, 0])
    facing_ref[:32] = facing.reshape(32, 128).astype(BF16)
    copies[1].wait()
    x = x_ref[...].astype(F32).reshape(-1, 128)
    total = group_total(column_sum(x))
    square = group_total(column_sum(x * x))
    row = jnp.where(lanes_of(total.shape) % 4 < 2, total, square)
    stat_ref[...] = row
    facing_ref[32:] = split_row(row)
    for copy in copies[2:]:
        copy.wait()


def columns_of(side_ref):
    return side_ref[:32].astype(F32).reshape(4, 8, 128)


def edge_of(up_ref, side_ref, bottom, row):
    columns = columns_of(side_ref)
    parts = split_row(row)[:8].astype(F32)[:4]
    tail = [jnp.where(bottom, columns[:, 7], columns[:, 0]), parts, jnp.zeros((8, 128), F32)]
    main = jnp.where(bottom, up_ref[:, 7], up_ref[:, 0]).reshape(128, 128)
    return main, jnp.concatenate(tail, axis=0).astype(BF16)


def edge_kernel(up_ref, side_ref, stat_ref, near_ref, far_ref, sum_ref):
    even = lax.axis_index("rows") % 2 == 0
    row = stat_ref[...] + join_row(side_ref[32:])
    sum_ref[...] = row
    near_ref[:128], near_ref[128:] = edge_of(up_ref, side_ref, even, row)
    far_ref[:128], far_ref[128:] = edge_of(up_ref, side_ref, jnp.logical_not(even), row)


def beyond(near_ref, far_ref):
    even = lax.axis_index("rows") % 2 == 0
    outside = jnp.logical_or(lax.axis_index("rows") == 0, lax.axis_index("rows") == lax.axis_size("rows") - 1)
    near = near_ref[:128].reshape(4, 32, 128)
    far = far_ref[:128].reshape(4, 32, 128)
    far = jnp.where(outside, jnp.zeros_like(far), far)
    near_column = near_ref[128:].astype(F32)[:4]
    far_column = far_ref[128:].astype(F32)[:4]
    far_column = jnp.where(outside, jnp.zeros_like(far_column), far_column)
    above = jnp.where(even, far, near), jnp.where(even, far_column, near_column)
    below = jnp.where(even, near, far), jnp.where(even, near_column, far_column)
    return above, below


def early_kernel(up_ref, side_ref, near_ref, far_ref, stat_ref, early_ref, sent_ref):
    row = stat_ref[...] + join_row(near_ref[128:].astype(F32)[4:8])
    sent_ref[...] = jnp.broadcast_to(row[None], (sent_ref.shape[0] // 8, 8, 128)).reshape(sent_ref.shape)
    (above, above_column), (below, below_column) = beyond(near_ref, far_ref)
    columns = columns_of(side_ref)
    for f in range(2):
        early_ref[f * 320 : f * 320 + 32] = above[f]
        early_ref[f * 320 + 32 : f * 320 + 288] = up_ref[f].reshape(256, 128)
        early_ref[f * 320 + 288 : f * 320 + 320] = below[f]
        column = [above_column[f : f + 1], columns[f], below_column[f : f + 1], jnp.zeros((6, 128), F32)]
        early_ref[640 + f * 16 : 656 + f * 16] = jnp.concatenate(column, axis=0).astype(BF16)


def column_taps(core, beside):
    left = lax.axis_index("sect") == 0
    index = sublanes_of(core.shape)
    first = index == 0
    last = index == 31
    zero = jnp.zeros_like(core)
    beside = jnp.broadcast_to(beside[:, None, :], core.shape)
    ahead = jnp.where(last, jnp.where(left, beside, zero), pltpu.roll(core, 31, 1))
    behind = jnp.where(first, jnp.where(left, zero, beside), pltpu.roll(core, 1, 1))
    ahead = ahead + jnp.where(first, jnp.where(left, core, zero), zero)
    behind = behind + jnp.where(last, jnp.where(left, zero, core), zero)
    return ahead, core, behind


def put(v_ref, f, r, b, e, rows):
    j = (b * 3 + e) * 128
    count = rows.shape[0]
    v_ref[f, r * 32 : (r + count) * 32, j : j + 128] = rows.astype(BF16).reshape(count * 32, 128)


def times_taps(lhs, taps_ref, a):
    return lax.dot_general(lhs, taps_ref[a], (((1,), (1,)), ((), ())), preferred_element_type=F32)


def put_own(v_ref, f, e, part):
    zero = jnp.zeros_like(part[0])
    top = part[1] + jnp.where(lax.axis_index("rows") == 0, part[0], zero)
    low = part[6] + jnp.where(lax.axis_index("rows") == lax.axis_size("rows") - 1, part[7], zero)
    put(v_ref, f, 0, 0, e, top[None])
    put(v_ref, f, 1, 0, e, part[2:8])
    put(v_ref, f, 0, 1, e, part)
    put(v_ref, f, 1, 2, e, part[0:6])
    put(v_ref, f, 7, 2, e, low[None])


def taps_kernel(up_ref, kernel_ref, v_ref, taps_ref):
    for a in range(3):
        for b in range(3):
            for e in range(3):
                j = (b * 3 + e) * 128
                taps_ref[a, :, j : j + 128] = kernel_ref[a, b, e]
    for f in range(4):
        put_own(v_ref, f, 1, up_ref[f].astype(F32))


def own_kernel(up_ref, side_ref, taps_ref, begun_ref, v_ref, dh_ref):
    columns = columns_of(side_ref)
    for f in range(4):
        ahead, _, behind = column_taps(up_ref[f].astype(F32), columns[f])
        put_own(v_ref, f, 0, ahead)
        put_own(v_ref, f, 2, behind)
    for f in range(4):
        total = None
        for a in range(3):
            if f + 2 - a < 4:
                term = times_taps(v_ref[f + 2 - a, 32:224], taps_ref, a)
                total = term if total is None else total + term
        dh_ref[f * 256 + 32 : f * 256 + 224] = total


def spread_kernel(near_ref, far_ref, later_ref, own_ref, v_ref):
    (above, above_column), (below, below_column) = beyond(near_ref, far_ref)
    row_first = lax.axis_index("rows") == 0
    row_last = lax.axis_index("rows") == lax.axis_size("rows") - 1
    outer = jnp.concatenate([above, below], axis=0).astype(F32)
    outer_column = jnp.concatenate([above_column, below_column], axis=0)
    for e, part in enumerate(column_taps(outer, outer_column)):
        for f in range(4):
            put(v_ref, f, 0, 2, e, part[f : f + 1])
            put(v_ref, f, 7, 0, e, part[f + 4 : f + 5])
    for f in range(2):
        later = later_ref[f * 320 : f * 320 + 320].astype(F32).reshape(10, 32, 128)
        column = later_ref[640 + f * 16 : 656 + f * 16].astype(F32)[:10]
        for e, part in enumerate(column_taps(later, column)):
            zero = jnp.zeros_like(part[0])
            top = part[2] + jnp.where(row_first, part[1], zero)
            low = part[7] + jnp.where(row_last, part[8], zero)
            put(v_ref, f + 4, 0, 0, e, top[None])
            put(v_ref, f + 4, 1, 0, e, part[3:10])
            put(v_ref, f + 4, 0, 1, e, part[1:9])
            put(v_ref, f + 4, 0, 2, e, part[0:7])
            put(v_ref, f + 4, 7, 2, e, low[None])

    @pl.when(lax.axis_index("tm") == 0)
    def _():
        both = v_ref[1].astype(F32) + v_ref[0].astype(F32)
        v_ref[6] = both.astype(BF16)
        v_ref[7] = (both + v_ref[2].astype(F32)).astype(BF16)


def grad_kernel(x_ref, norm_ref, gain_ref, bias_ref, taps_ref, part_ref, v_ref, da_ref, sums_ref, dh_ref):
    def edges(lo, hi):
        return jnp.concatenate([v_ref[lo:hi, 0:32], v_ref[lo:hi, 224:256]], axis=1).reshape((hi - lo) * 64, 1152)

    outer = times_taps(edges(0, 4), taps_ref, 2)
    one = times_taps(edges(1, 4), taps_ref, 1)
    two = times_taps(edges(2, 4), taps_ref, 0)
    outer = outer + jnp.concatenate([one, jnp.zeros((64, 128), F32)], axis=0)
    outer = outer + jnp.concatenate([two, jnp.zeros((128, 128), F32)], axis=0)
    for f in range(4):
        dh_ref[f * 256 : f * 256 + 32] = outer[f * 64 : f * 64 + 32]
        dh_ref[f * 256 + 32 : f * 256 + 224] = part_ref[f * 256 + 32 : f * 256 + 224]
        dh_ref[f * 256 + 224 : f * 256 + 256] = outer[f * 64 + 32 : f * 64 + 64]
    dh_ref[768:1024] += times_taps(v_ref[4], taps_ref, 1)
    dh_ref[512:1024] += times_taps(v_ref[4:6].reshape(512, 1152), taps_ref, 0)

    @pl.when(lax.axis_index("tm") == 0)
    def _():
        dh_ref[0:256] += times_taps(v_ref[0], taps_ref, 1) + times_taps(v_ref[6], taps_ref, 0)

    bias_sum = jnp.zeros((8, 128), F32)
    gain_sum = jnp.zeros((8, 128), F32)
    for block in range(8):
        xhat, pre = block_of(x_ref, norm_ref, gain_ref, bias_ref, block)
        sig = 1.0 / (1.0 + jnp.exp(-pre))
        da = dh_ref[block * 128 : (block + 1) * 128] * sig * (1.0 + pre * (1.0 - sig))
        da_ref[block * 128 : (block + 1) * 128] = da
        bias_sum = bias_sum + jnp.sum(da.reshape(16, 8, 128), axis=0)
        gain_sum = gain_sum + jnp.sum((da * xhat).reshape(16, 8, 128), axis=0)
    sums_ref[...] = jnp.where(sublanes_of((8, 128)) == 0, column_sum(bias_sum), column_sum(gain_sum))


def sums_to_pair(row):
    lane = lanes_of(row.shape)
    total = jnp.where(lane % 4 < 2, row, pltpu.roll(row, 2, 1))
    square = jnp.where(lane % 4 < 2, pltpu.roll(row, 126, 1), row)
    return total, square


def product_of(turned, v_ref, a, lo, hi):
    if a == 2:
        return jnp.dot(turned, v_ref[0:4, :, lo:hi].reshape(1024, hi - lo), preferred_element_type=F32)
    source = jnp.where(lax.axis_index("tm") == 0, 7 - a, 2 - a)
    first = jnp.dot(turned[:, :256], v_ref[source, :, lo:hi], preferred_element_type=F32)
    rest = v_ref[3 - a : 6 - a, :, lo:hi].reshape(768, hi - lo)
    return first + jnp.dot(turned[:, 256:], rest, preferred_element_type=F32)


def half_product(half, turned, v_ref, w_ref):
    for a, lo, hi in (((0, 0, 9), (1, 0, 5)), ((1, 5, 9), (2, 0, 9)))[half]:
        product = product_of(turned, v_ref, a, lo * 128, hi * 128)
        for j in range(lo, hi):
            block = product[:, (j - lo) * 128 : (j - lo + 1) * 128].T.reshape(16, 8, 128)
            w_ref[:, (a * 9 + j) % HALF] = block
    if half == 1:
        w_ref[:, HALF - 1] = jnp.zeros((16, 8, 128), F32)


def block_of(x_ref, norm_ref, gain_ref, bias_ref, block):
    half = (block % 2) * 4
    x = x_ref[block // 2, half : half + 4].astype(F32).reshape(128, 128)
    xhat = (x - norm_ref[0:1]) * norm_ref[8:9]
    return xhat, xhat * gain_ref[...] + bias_ref[...]


def away_kernel(counted, x_ref, stat_ref, gain_ref, bias_ref, v_ref, w_ref, turned_ref, norm_ref):
    total, square = sums_to_pair(column_sum(stat_ref[...]))
    mean = total / counted
    norm_ref[0:8] = mean
    norm_ref[8:16] = lax.rsqrt(square / counted - mean * mean + 1e-06)
    for block in range(8):
        _, pre = block_of(x_ref, norm_ref, gain_ref, bias_ref, block)
        hidden = pre * (1.0 / (1.0 + jnp.exp(-pre)))
        turned_ref[:, block * 128 : (block + 1) * 128] = hidden.T.astype(BF16)
    left = lax.axis_index("sect") == 0

    @pl.when(left)
    def _():
        half_product(1, turned_ref[...], v_ref, w_ref)

    @pl.when(jnp.logical_not(left))
    def _():
        half_product(0, turned_ref[...], v_ref, w_ref)


def home_kernel(turned_ref, v_ref, w_ref):
    left = lax.axis_index("sect") == 0

    @pl.when(left)
    def _():
        half_product(0, turned_ref[...], v_ref, w_ref)

    @pl.when(jnp.logical_not(left))
    def _():
        half_product(1, turned_ref[...], v_ref, w_ref)


def split_sums(sums):
    row = sublanes_of(sums.shape)
    high = sums.astype(BF16).astype(F32)
    middle = (sums - high).astype(BF16).astype(F32)
    low = sums - high - middle
    return jnp.where(
        row < 2, high, jnp.where(row < 4, pltpu.roll(middle, 2, 0), pltpu.roll(low, 4, 0))
    )


def join_sums(parts):
    return parts + pltpu.roll(parts, 6, 0) + pltpu.roll(parts, 4, 0)


def pair_kernel(own_ref, other_ref, sums_ref, other_sums_ref, out_ref):
    slot = split_sums(sums_ref[...] + other_sums_ref[...])
    for i in range(16):
        body = (own_ref[i] + other_ref[i]).reshape(HALF * 8, 128)
        out_ref[i] = jnp.concatenate([body, slot], axis=0).astype(BF16)


def power_for(values):
    most = jnp.max(jnp.max(jnp.abs(values), axis=0, keepdims=True), axis=1, keepdims=True)
    bits = jnp.log(jnp.maximum(most, 1e-30)) * 1.4426950408889634
    return jnp.clip(jnp.floor(14.0 - bits), -100.0, 100.0)


def share_kernel(in_ref, out_ref):
    rows = HALF * 8
    total = in_ref[0].astype(F32)
    for i in range(1, in_ref.shape[0]):
        total = total + in_ref[i].astype(F32)
    body = total[:rows]
    sums = join_sums(total[rows:])
    index = sublanes_of(sums.shape)
    sums = jnp.where(index < 2, sums, jnp.zeros_like(sums))
    power = power_for(body)
    power_of_sums = power_for(sums)
    slot = split_sums(sums * jnp.exp2(power_of_sums))
    slot = jnp.where(index == 6, power, jnp.where(index == 7, power_of_sums, slot))
    out_ref[:rows] = body * jnp.exp2(power)
    out_ref[rows:] = slot


def last_sum_kernel(scaling, in_ref, half_ref, sums_ref):
    rows = HALF * 8
    total = jnp.zeros((rows, 128), F32)
    sums = jnp.zeros((8, 128), F32)
    for i in range(in_ref.shape[0]):
        slot = in_ref[i, rows:]
        total = total + in_ref[i, :rows] * jnp.exp2(-slot[6:7])
        sums = sums + join_sums(slot) * jnp.exp2(-slot[7:8])
    half_ref[...] = total * scaling
    sums_ref[...] = sums


def finish_kernel(counted, scaling, x_ref, da_ref, norm_ref, sums_ref, gain_ref, out_ref, gain_grad_ref, bias_grad_ref):
    gain = gain_ref[...]
    mean = norm_ref[0:1]
    rstd = norm_ref[8:9]
    sums = sums_ref[...]
    bias_grad_ref[...] = sums[0:1] * scaling
    gain_grad_ref[...] = sums[1:2] * scaling
    averages = group_total(gain * sums) / counted
    leading = averages[0:1]
    trailing = averages[1:2]
    xhat = (x_ref[...].astype(F32).reshape(-1, 128) - mean) * rstd
    grad = rstd * (da_ref[...] * gain - leading - xhat * trailing)
    out_ref[...] = grad.astype(BF16).reshape(out_ref.shape)


def join_kernel(half_ref, other_ref, out_ref):
    left = lax.axis_index("sect") == 0
    half = half_ref[...]
    other = other_ref[...]
    out_ref[: HALF * 8] = jnp.where(left, half, other)
    out_ref[HALF * 8 :] = jnp.where(left, other, half)[: (TAPS - HALF) * 8]


def shape_of(shape, dtype=F32):
    return jax.ShapeDtypeStruct(shape, dtype)


def local(activations, group_norm_gain, group_norm_bias, upstream, kernel):
    frames, height, columns, channels = activations.shape
    n_time, n_rows, n_sect = (lax.axis_size(axis) for axis in ("tm", "rows", "sect"))
    cells = frames * height * columns
    total_cells = cells * n_time * n_rows * n_sect
    counted = float(total_cells * (channels // GROUPS))
    scaling = float(total_cells) ** (-0.5)
    swap = [(0, 1), (1, 0)]
    near = [(i, i ^ 1) for i in range(n_rows)]
    far = [(i, (i - 1) % n_rows if i % 2 == 0 else (i + 1) % n_rows) for i in range(n_rows)]

    up, x, gain, bias, weights, facing, stat = call(
        entry_kernel,
        [
            shape_of(upstream.shape, BF16),
            shape_of(activations.shape, BF16),
            shape_of((1, channels)),
            shape_of((1, channels)),
            shape_of(kernel.shape, BF16),
            shape_of((48, channels), BF16),
            shape_of((8, channels)),
        ],
        [
            held(upstream, pltpu.HBM),
            held(activations, pltpu.HBM),
            held(group_norm_gain.reshape(1, channels), pltpu.HBM),
            held(group_norm_bias.reshape(1, channels), pltpu.HBM),
            held(kernel, pltpu.HBM),
        ],
        [HBM] * 5,
        [pltpu.SemaphoreType.DMA((5,))],
    )
    side = lax.ppermute(facing, "sect", swap)
    spread, taps = call(
        taps_kernel,
        [pltpu.VMEM((8, 256, 1152), BF16), shape_of((3, channels, 9 * channels), BF16)],
        [up, weights],
    )
    side, taps = lax.optimization_barrier((side, taps))
    nearer, farther, stat = call(
        edge_kernel,
        [shape_of((144, channels), BF16), shape_of((144, channels), BF16), shape_of((8, channels))],
        [up, side, stat],
    )
    nearer = lax.ppermute(nearer, "rows", near)
    farther = lax.ppermute(farther, "rows", far)
    spread, inner = call(
        own_kernel,
        [pltpu.VMEM((8, 256, 1152), BF16), shape_of((cells, channels))],
        [up, side, taps, held(spread, pltpu.VMEM)],
        flops=cells * TAPS * channels * channels,
        aliases={3: 0},
    )
    nearer, inner = lax.optimization_barrier((nearer, inner))
    groups = [[t * n_rows + r for t in range(n_time) for r in chosen] for chosen in ((1, 2, 4, 7), (0, 3, 5, 6))]
    early, stat = call(
        early_kernel,
        [shape_of((672, channels), BF16), shape_of((len(groups[0]), channels))],
        [up, side, nearer, farther, stat],
        [VMEM, VMEM, VMEM, VMEM, VMEM],
    )
    later = lax.ppermute(early, "tm", [(i + 1, i) for i in range(n_time - 1)])
    stat = lax.all_to_all(stat[:, None], ("tm", "rows"), 0, 0, axis_index_groups=groups).reshape(-1, channels)
    stat, later = lax.optimization_barrier((stat, later))
    (spread,) = call(
        spread_kernel,
        [pltpu.VMEM((8, 256, 1152), BF16)],
        [nearer, farther, later, held(spread, pltpu.VMEM)],
        aliases={3: 0},
    )
    away, turned, norm = call(
        functools.partial(away_kernel, counted),
        [shape_of((16, HALF, 8, 128)), shape_of((channels, cells), BF16), shape_of((16, channels))],
        [x, stat, gain, bias, held(spread, pltpu.VMEM)],
        flops=cells * TAPS * channels * channels,
    )
    arrived = lax.ppermute(away, "sect", swap)
    da, sums = call(
        grad_kernel,
        [shape_of((cells, channels)), shape_of((8, channels))],
        [x, norm, gain, bias, taps, inner, held(spread, pltpu.VMEM)],
        scratch=[pltpu.VMEM((cells, channels), F32)],
        flops=cells * TAPS * channels * channels,
    )
    other_sums = lax.ppermute(sums, "sect", swap)
    (home,) = call(
        home_kernel,
        [shape_of((16, HALF, 8, 128))],
        [turned, held(spread, pltpu.VMEM)],
        flops=cells * TAPS * channels * channels,
    )
    (sent,) = call(
        pair_kernel, [shape_of((16, SLOTS * 8, 128), BF16)], [home, arrived, sums, other_sums]
    )
    gathered = lax.all_to_all(sent, "tm", 0, 0)
    (share,) = call(share_kernel, [shape_of((SLOTS * 8, 128))], [gathered])
    share = jnp.broadcast_to(share.astype(jnp.float16)[None], (n_rows, SLOTS * 8, 128))
    shares = lax.all_to_all(share, "rows", 0, 0).astype(F32)
    half, sums = call(
        functools.partial(last_sum_kernel, scaling),
        [shape_of((HALF * 8, 128)), shape_of((8, 128))],
        [shares],
    )
    other = lax.ppermute(half, "sect", swap)
    input_gradient, gain_grad, bias_grad = call(
        functools.partial(finish_kernel, counted, scaling),
        [shape_of(activations.shape, BF16), shape_of((1, 128)), shape_of((1, 128))],
        [x, da, norm, sums, gain],
    )
    (whole,) = call(join_kernel, [shape_of((TAPS * 8, 128))], [half, other])
    weight_grad = whole.reshape(3, 3, 3, 8, 128).transpose(0, 1, 2, 4, 3)
    return (input_gradient, gain_grad.reshape(128), bias_grad.reshape(128), weight_grad)


def solution(mesh):
    return jax.shard_map(
        local,
        mesh=mesh,
        in_specs=(P("tm", "rows", "sect", None), P(), P(), P("tm", "rows", "sect", None), P()),
        out_specs=(P("tm", "rows", "sect", None), P(), P(), P(None, None, None, None, "tm")),
        check_vma=False,
    )
```

```python
import functools
import math

import jax
import jax.numpy as jnp
from jax import lax
from jax.experimental import pallas as pl
from jax.experimental.pallas import tpu as pltpu
from jax.sharding import PartitionSpec as P

GROUPS = 32
TAPS = 27
HALF = 14
SLOTS = HALF + 1
F32 = jnp.float32
BF16 = jnp.bfloat16
VMEM = pl.BlockSpec(memory_space=pltpu.VMEM)
HBM = pl.BlockSpec(memory_space=pltpu.HBM)


def held(x, space):
    return pltpu.with_memory_space_constraint(x, space)


def call(body, outs, args, specs=None, scratch=(), flops=0, aliases=None):
    moved = sum(math.prod(x.shape) * jnp.dtype(x.dtype).itemsize for x in list(args) + list(outs))
    return pl.pallas_call(
        body,
        out_shape=outs,
        in_specs=specs or [VMEM] * len(args),
        out_specs=[VMEM] * len(outs),
        scratch_shapes=list(scratch),
        input_output_aliases=aliases or {},
        cost_estimate=pl.CostEstimate(flops=flops, bytes_accessed=moved, transcendentals=0),
        compiler_params=pltpu.CompilerParams(vmem_limit_bytes=24 * 1024 * 1024),
    )(*args)


def lanes_of(shape):
    return lax.broadcasted_iota(jnp.int32, shape, len(shape) - 1)


def sublanes_of(shape):
    return lax.broadcasted_iota(jnp.int32, shape, len(shape) - 2)


def group_total(v):
    lane = lanes_of(v.shape)
    v = v + jnp.where(lane % 2 == 0, pltpu.roll(v, 127, 1), pltpu.roll(v, 1, 1))
    return v + jnp.where(lane % 4 < 2, pltpu.roll(v, 126, 1), pltpu.roll(v, 2, 1))


def column_sum(v):
    part = jnp.sum(v.reshape(-1, 8, v.shape[-1]), axis=0)
    return jnp.broadcast_to(jnp.sum(part, axis=0, keepdims=True), part.shape)


def split_row(row):
    high = row.astype(BF16).astype(F32)
    middle = (row - high).astype(BF16).astype(F32)
    low = row - high - middle
    index = sublanes_of((8, 128))
    parts = jnp.where(index == 0, high, jnp.where(index == 1, middle, low))
    return jnp.concatenate([parts, parts], axis=0).astype(BF16)


def join_row(parts):
    parts = parts.astype(F32)
    return jnp.broadcast_to(parts[0:1] + parts[1:2] + parts[2:3], (8, 128))


def entry_kernel(
    up_hbm, x_hbm, gain_hbm, bias_hbm, kernel_hbm, up_ref, x_ref, gain_ref, bias_ref, kernel_ref, facing_ref, stat_ref, sems
):
    pairs = ((up_hbm, up_ref), (x_hbm, x_ref), (gain_hbm, gain_ref), (bias_hbm, bias_ref), (kernel_hbm, kernel_ref))
    copies = [pltpu.make_async_copy(source, target, sems.at[i]) for i, (source, target) in enumerate(pairs)]
    for copy in copies:
        copy.start()
    copies[0].wait()
    left = lax.axis_index("sect") == 0
    facing = jnp.where(left, up_ref[:, :, 16:].astype(F32)[:, :, 15], up_ref[:, :, :16].astype(F32)[:, :, 0])
    facing_ref[:32] = facing.reshape(32, 128).astype(BF16)
    copies[1].wait()
    x = x_ref[...].astype(F32).reshape(-1, 128)
    total = group_total(column_sum(x))
    square = group_total(column_sum(x * x))
    row = jnp.where(lanes_of(total.shape) % 4 < 2, total, square)
    stat_ref[...] = row
    facing_ref[32:] = split_row(row)
    for copy in copies[2:]:
        copy.wait()


def columns_of(side_ref):
    return side_ref[:32].astype(F32).reshape(4, 8, 128)


def edge_of(up_ref, side_ref, bottom, row):
    columns = columns_of(side_ref)
    parts = split_row(row)[:8].astype(F32)[:4]
    tail = [jnp.where(bottom, columns[:, 7], columns[:, 0]), parts, jnp.zeros((8, 128), F32)]
    main = jnp.where(bottom, up_ref[:, 7], up_ref[:, 0]).reshape(128, 128)
    return main, jnp.concatenate(tail, axis=0).astype(BF16)


def edge_kernel(up_ref, side_ref, stat_ref, near_ref, far_ref, sum_ref):
    even = lax.axis_index("rows") % 2 == 0
    row = stat_ref[...] + join_row(side_ref[32:])
    sum_ref[...] = row
    near_ref[:128], near_ref[128:] = edge_of(up_ref, side_ref, even, row)
    far_ref[:128], far_ref[128:] = edge_of(up_ref, side_ref, jnp.logical_not(even), row)


def beyond(near_ref, far_ref):
    even = lax.axis_index("rows") % 2 == 0
    outside = jnp.logical_or(lax.axis_index("rows") == 0, lax.axis_index("rows") == lax.axis_size("rows") - 1)
    near = near_ref[:128].reshape(4, 32, 128)
    far = far_ref[:128].reshape(4, 32, 128)
    far = jnp.where(outside, jnp.zeros_like(far), far)
    near_column = near_ref[128:].astype(F32)[:4]
    far_column = far_ref[128:].astype(F32)[:4]
    far_column = jnp.where(outside, jnp.zeros_like(far_column), far_column)
    above = jnp.where(even, far, near), jnp.where(even, far_column, near_column)
    below = jnp.where(even, near, far), jnp.where(even, near_column, far_column)
    return above, below


def early_kernel(up_ref, side_ref, near_ref, far_ref, stat_ref, early_ref, sent_ref):
    row = stat_ref[...] + join_row(near_ref[128:].astype(F32)[4:8])
    sent_ref[...] = jnp.broadcast_to(row[None], (sent_ref.shape[0] // 8, 8, 128)).reshape(sent_ref.shape)
    (above, above_column), (below, below_column) = beyond(near_ref, far_ref)
    columns = columns_of(side_ref)
    for f in range(2):
        early_ref[f * 320 : f * 320 + 32] = above[f]
        early_ref[f * 320 + 32 : f * 320 + 288] = up_ref[f].reshape(256, 128)
        early_ref[f * 320 + 288 : f * 320 + 320] = below[f]
        column = [above_column[f : f + 1], columns[f], below_column[f : f + 1], jnp.zeros((6, 128), F32)]
        early_ref[640 + f * 16 : 656 + f * 16] = jnp.concatenate(column, axis=0).astype(BF16)


def column_taps(core, beside):
    left = lax.axis_index("sect") == 0
    index = sublanes_of(core.shape)
    first = index == 0
    last = index == 31
    zero = jnp.zeros_like(core)
    beside = jnp.broadcast_to(beside[:, None, :], core.shape)
    ahead = jnp.where(last, jnp.where(left, beside, zero), pltpu.roll(core, 31, 1))
    behind = jnp.where(first, jnp.where(left, zero, beside), pltpu.roll(core, 1, 1))
    ahead = ahead + jnp.where(first, jnp.where(left, core, zero), zero)
    behind = behind + jnp.where(last, jnp.where(left, zero, core), zero)
    return ahead, core, behind


def put(v_ref, f, r, b, e, rows):
    j = (b * 3 + e) * 128
    count = rows.shape[0]
    v_ref[f, r * 32 : (r + count) * 32, j : j + 128] = rows.astype(BF16).reshape(count * 32, 128)


def times_taps(lhs, taps_ref, a):
    return lax.dot_general(lhs, taps_ref[a], (((1,), (1,)), ((), ())), preferred_element_type=F32)


def put_own(v_ref, f, e, part):
    zero = jnp.zeros_like(part[0])
    top = part[1] + jnp.where(lax.axis_index("rows") == 0, part[0], zero)
    low = part[6] + jnp.where(lax.axis_index("rows") == lax.axis_size("rows") - 1, part[7], zero)
    put(v_ref, f, 0, 0, e, top[None])
    put(v_ref, f, 1, 0, e, part[2:8])
    put(v_ref, f, 0, 1, e, part)
    put(v_ref, f, 1, 2, e, part[0:6])
    put(v_ref, f, 7, 2, e, low[None])


def taps_kernel(up_ref, kernel_ref, v_ref, taps_ref):
    for a in range(3):
        for b in range(3):
            for e in range(3):
                j = (b * 3 + e) * 128
                taps_ref[a, :, j : j + 128] = kernel_ref[a, b, e]
    for f in range(4):
        put_own(v_ref, f, 1, up_ref[f].astype(F32))


def own_kernel(up_ref, side_ref, taps_ref, begun_ref, v_ref, dh_ref):
    columns = columns_of(side_ref)
    for f in range(4):
        ahead, _, behind = column_taps(up_ref[f].astype(F32), columns[f])
        put_own(v_ref, f, 0, ahead)
        put_own(v_ref, f, 2, behind)
    for f in range(4):
        total = None
        for a in range(3):
            if f + 2 - a < 4:
                term = times_taps(v_ref[f + 2 - a, 32:224], taps_ref, a)
                total = term if total is None else total + term
        dh_ref[f * 256 + 32 : f * 256 + 224] = total

    @pl.when(lax.axis_index("tm") == 0)
    def _():
        fold_first(v_ref, 32, 224)
        dh_ref[32:224] += times_taps(v_ref[0, 32:224], taps_ref, 1) + times_taps(v_ref[6, 32:224], taps_ref, 0)


def fold_first(v_ref, lo, hi):
    both = v_ref[1, lo:hi].astype(F32) + v_ref[0, lo:hi].astype(F32)
    v_ref[6, lo:hi] = both.astype(BF16)
    v_ref[7, lo:hi] = (both + v_ref[2, lo:hi].astype(F32)).astype(BF16)


def spread_edges(near_ref, far_ref, later_ref, v_ref):
    (above, above_column), (below, below_column) = beyond(near_ref, far_ref)
    row_first = lax.axis_index("rows") == 0
    row_last = lax.axis_index("rows") == lax.axis_size("rows") - 1
    outer = jnp.concatenate([above, below], axis=0).astype(F32)
    outer_column = jnp.concatenate([above_column, below_column], axis=0)
    for e, part in enumerate(column_taps(outer, outer_column)):
        for f in range(4):
            put(v_ref, f, 0, 2, e, part[f : f + 1])
            put(v_ref, f, 7, 0, e, part[f + 4 : f + 5])
    for f in range(2):
        later = later_ref[f * 320 : f * 320 + 320].astype(F32).reshape(10, 32, 128)
        column = later_ref[640 + f * 16 : 656 + f * 16].astype(F32)[:10]
        for e, part in enumerate(column_taps(later, column)):
            zero = jnp.zeros_like(part[0])
            top = part[2] + jnp.where(row_first, part[1], zero)
            low = part[7] + jnp.where(row_last, part[8], zero)
            put(v_ref, f + 4, 0, 0, e, top[None])
            put(v_ref, f + 4, 1, 0, e, part[3:10])
            put(v_ref, f + 4, 0, 1, e, part[1:9])
            put(v_ref, f + 4, 0, 2, e, part[0:7])
            put(v_ref, f + 4, 7, 2, e, low[None])

    @pl.when(lax.axis_index("tm") == 0)
    def _():
        fold_first(v_ref, 0, 32)
        fold_first(v_ref, 224, 256)


def grad_kernel(x_ref, norm_ref, gain_ref, bias_ref, taps_ref, part_ref, v_ref, da_ref, sums_ref, dh_ref):
    def edges(lo, hi):
        return jnp.concatenate([v_ref[lo:hi, 0:32], v_ref[lo:hi, 224:256]], axis=1).reshape((hi - lo) * 64, 1152)

    outer = times_taps(edges(0, 4), taps_ref, 2)
    one = times_taps(edges(1, 4), taps_ref, 1)
    two = times_taps(edges(2, 4), taps_ref, 0)
    outer = outer + jnp.concatenate([one, jnp.zeros((64, 128), F32)], axis=0)
    outer = outer + jnp.concatenate([two, jnp.zeros((128, 128), F32)], axis=0)
    for f in range(4):
        dh_ref[f * 256 : f * 256 + 32] = outer[f * 64 : f * 64 + 32]
        dh_ref[f * 256 + 32 : f * 256 + 224] = part_ref[f * 256 + 32 : f * 256 + 224]
        dh_ref[f * 256 + 224 : f * 256 + 256] = outer[f * 64 + 32 : f * 64 + 64]
    dh_ref[768:1024] += times_taps(v_ref[4], taps_ref, 1)
    dh_ref[512:1024] += times_taps(v_ref[4:6].reshape(512, 1152), taps_ref, 0)

    @pl.when(lax.axis_index("tm") == 0)
    def _():
        more = times_taps(edges(0, 1), taps_ref, 1) + times_taps(edges(6, 7), taps_ref, 0)
        dh_ref[0:32] += more[:32]
        dh_ref[224:256] += more[32:]

    bias_sum = jnp.zeros((8, 128), F32)
    gain_sum = jnp.zeros((8, 128), F32)
    for block in range(8):
        xhat, pre = block_of(x_ref, norm_ref, gain_ref, bias_ref, block)
        sig = 1.0 / (1.0 + jnp.exp(-pre))
        da = dh_ref[block * 128 : (block + 1) * 128] * sig * (1.0 + pre * (1.0 - sig))
        da_ref[block * 128 : (block + 1) * 128] = da
        bias_sum = bias_sum + jnp.sum(da.reshape(16, 8, 128), axis=0)
        gain_sum = gain_sum + jnp.sum((da * xhat).reshape(16, 8, 128), axis=0)
    sums_ref[...] = jnp.where(sublanes_of((8, 128)) == 0, column_sum(bias_sum), column_sum(gain_sum))


def sums_to_pair(row):
    lane = lanes_of(row.shape)
    total = jnp.where(lane % 4 < 2, row, pltpu.roll(row, 2, 1))
    square = jnp.where(lane % 4 < 2, pltpu.roll(row, 126, 1), row)
    return total, square


def product_of(turned, v_ref, a, lo, hi):
    if a == 2:
        return jnp.dot(turned, v_ref[0:4, :, lo:hi].reshape(1024, hi - lo), preferred_element_type=F32)
    source = jnp.where(lax.axis_index("tm") == 0, 7 - a, 2 - a)
    first = jnp.dot(turned[:, :256], v_ref[source, :, lo:hi], preferred_element_type=F32)
    rest = v_ref[3 - a : 6 - a, :, lo:hi].reshape(768, hi - lo)
    return first + jnp.dot(turned[:, 256:], rest, preferred_element_type=F32)


def half_product(half, turned, v_ref, w_ref):
    for a, lo, hi in (((0, 0, 9), (1, 0, 5)), ((1, 5, 9), (2, 0, 9)))[half]:
        product = product_of(turned, v_ref, a, lo * 128, hi * 128)
        for j in range(lo, hi):
            block = product[:, (j - lo) * 128 : (j - lo + 1) * 128].T.reshape(16, 8, 128)
            w_ref[:, (a * 9 + j) % HALF] = block
    if half == 1:
        w_ref[:, HALF - 1] = jnp.zeros((16, 8, 128), F32)


def block_of(x_ref, norm_ref, gain_ref, bias_ref, block):
    half = (block % 2) * 4
    x = x_ref[block // 2, half : half + 4].astype(F32).reshape(128, 128)
    xhat = (x - norm_ref[0:1]) * norm_ref[8:9]
    return xhat, xhat * gain_ref[...] + bias_ref[...]


def away_kernel(
    counted, near_ref, far_ref, later_ref, x_ref, stat_ref, gain_ref, bias_ref, begun_ref, w_ref, turned_ref, norm_ref, v_ref
):
    spread_edges(near_ref, far_ref, later_ref, v_ref)
    total, square = sums_to_pair(column_sum(stat_ref[...]))
    mean = total / counted
    norm_ref[0:8] = mean
    norm_ref[8:16] = lax.rsqrt(square / counted - mean * mean + 1e-06)
    for block in range(8):
        _, pre = block_of(x_ref, norm_ref, gain_ref, bias_ref, block)
        hidden = pre * (1.0 / (1.0 + jnp.exp(-pre)))
        turned_ref[:, block * 128 : (block + 1) * 128] = hidden.T.astype(BF16)
    left = lax.axis_index("sect") == 0

    @pl.when(left)
    def _():
        half_product(1, turned_ref[...], v_ref, w_ref)

    @pl.when(jnp.logical_not(left))
    def _():
        half_product(0, turned_ref[...], v_ref, w_ref)


def home_kernel(turned_ref, v_ref, w_ref):
    left = lax.axis_index("sect") == 0

    @pl.when(left)
    def _():
        half_product(0, turned_ref[...], v_ref, w_ref)

    @pl.when(jnp.logical_not(left))
    def _():
        half_product(1, turned_ref[...], v_ref, w_ref)


def split_sums(sums):
    row = sublanes_of(sums.shape)
    high = sums.astype(BF16).astype(F32)
    middle = (sums - high).astype(BF16).astype(F32)
    low = sums - high - middle
    return jnp.where(
        row < 2, high, jnp.where(row < 4, pltpu.roll(middle, 2, 0), pltpu.roll(low, 4, 0))
    )


def join_sums(parts):
    return parts + pltpu.roll(parts, 6, 0) + pltpu.roll(parts, 4, 0)


def pair_kernel(own_ref, other_ref, sums_ref, other_sums_ref, out_ref):
    slot = split_sums(sums_ref[...] + other_sums_ref[...])
    for i in range(16):
        body = (own_ref[i] + other_ref[i]).reshape(HALF * 8, 128)
        out_ref[i] = jnp.concatenate([body, slot], axis=0).astype(BF16)


def power_for(values):
    most = jnp.max(jnp.max(jnp.abs(values), axis=0, keepdims=True), axis=1, keepdims=True)
    bits = jnp.log(jnp.maximum(most, 1e-30)) * 1.4426950408889634
    return jnp.clip(jnp.floor(14.0 - bits), -100.0, 100.0)


def share_kernel(in_ref, out_ref):
    rows = HALF * 8
    total = in_ref[0].astype(F32)
    for i in range(1, in_ref.shape[0]):
        total = total + in_ref[i].astype(F32)
    body = total[:rows]
    sums = join_sums(total[rows:])
    index = sublanes_of(sums.shape)
    sums = jnp.where(index < 2, sums, jnp.zeros_like(sums))
    power = power_for(body)
    power_of_sums = power_for(sums)
    slot = split_sums(sums * jnp.exp2(power_of_sums))
    slot = jnp.where(index == 6, power, jnp.where(index == 7, power_of_sums, slot))
    out_ref[:rows] = body * jnp.exp2(power)
    out_ref[rows:] = slot


def last_sum_kernel(scaling, in_ref, half_ref, sums_ref):
    rows = HALF * 8
    total = jnp.zeros((rows, 128), F32)
    sums = jnp.zeros((8, 128), F32)
    for i in range(in_ref.shape[0]):
        slot = in_ref[i, rows:]
        total = total + in_ref[i, :rows] * jnp.exp2(-slot[6:7])
        sums = sums + join_sums(slot) * jnp.exp2(-slot[7:8])
    half_ref[...] = total * scaling
    sums_ref[...] = sums


def finish_kernel(counted, scaling, x_ref, da_ref, norm_ref, sums_ref, gain_ref, out_ref, gain_grad_ref, bias_grad_ref):
    gain = gain_ref[...]
    mean = norm_ref[0:1]
    rstd = norm_ref[8:9]
    sums = sums_ref[...]
    bias_grad_ref[...] = sums[0:1] * scaling
    gain_grad_ref[...] = sums[1:2] * scaling
    averages = group_total(gain * sums) / counted
    leading = averages[0:1]
    trailing = averages[1:2]
    xhat = (x_ref[...].astype(F32).reshape(-1, 128) - mean) * rstd
    grad = rstd * (da_ref[...] * gain - leading - xhat * trailing)
    out_ref[...] = grad.astype(BF16).reshape(out_ref.shape)


def join_kernel(half_ref, other_ref, out_ref):
    left = lax.axis_index("sect") == 0
    half = half_ref[...]
    other = other_ref[...]
    out_ref[: HALF * 8] = jnp.where(left, half, other)
    out_ref[HALF * 8 :] = jnp.where(left, other, half)[: (TAPS - HALF) * 8]


def shape_of(shape, dtype=F32):
    return jax.ShapeDtypeStruct(shape, dtype)


def local(activations, group_norm_gain, group_norm_bias, upstream, kernel):
    frames, height, columns, channels = activations.shape
    n_time, n_rows, n_sect = (lax.axis_size(axis) for axis in ("tm", "rows", "sect"))
    cells = frames * height * columns
    total_cells = cells * n_time * n_rows * n_sect
    counted = float(total_cells * (channels // GROUPS))
    scaling = float(total_cells) ** (-0.5)
    swap = [(0, 1), (1, 0)]
    near = [(i, i ^ 1) for i in range(n_rows)]
    far = [(i, (i - 1) % n_rows if i % 2 == 0 else (i + 1) % n_rows) for i in range(n_rows)]

    up, x, gain, bias, weights, facing, stat = call(
        entry_kernel,
        [
            shape_of(upstream.shape, BF16),
            shape_of(activations.shape, BF16),
            shape_of((1, channels)),
            shape_of((1, channels)),
            shape_of(kernel.shape, BF16),
            shape_of((48, channels), BF16),
            shape_of((8, channels)),
        ],
        [
            held(upstream, pltpu.HBM),
            held(activations, pltpu.HBM),
            held(group_norm_gain.reshape(1, channels), pltpu.HBM),
            held(group_norm_bias.reshape(1, channels), pltpu.HBM),
            held(kernel, pltpu.HBM),
        ],
        [HBM] * 5,
        [pltpu.SemaphoreType.DMA((5,))],
    )
    side = lax.ppermute(facing, "sect", swap)
    spread, taps = call(
        taps_kernel,
        [pltpu.VMEM((8, 256, 1152), BF16), shape_of((3, channels, 9 * channels), BF16)],
        [up, weights],
    )
    side, taps = lax.optimization_barrier((side, taps))
    nearer, farther, stat = call(
        edge_kernel,
        [shape_of((144, channels), BF16), shape_of((144, channels), BF16), shape_of((8, channels))],
        [up, side, stat],
    )
    nearer = lax.ppermute(nearer, "rows", near)
    farther = lax.ppermute(farther, "rows", far)
    spread, inner = call(
        own_kernel,
        [pltpu.VMEM((8, 256, 1152), BF16), shape_of((cells, channels))],
        [up, side, taps, held(spread, pltpu.VMEM)],
        flops=cells * TAPS * channels * channels,
        aliases={3: 0},
    )
    nearer, inner = lax.optimization_barrier((nearer, inner))
    groups = [[t * n_rows + r for t in range(n_time) for r in chosen] for chosen in ((1, 2, 4, 7), (0, 3, 5, 6))]
    early, stat = call(
        early_kernel,
        [shape_of((672, channels), BF16), shape_of((len(groups[0]), channels))],
        [up, side, nearer, farther, stat],
        [VMEM, VMEM, VMEM, VMEM, VMEM],
    )
    later = lax.ppermute(early, "tm", [(i + 1, i) for i in range(n_time - 1)])
    stat = lax.all_to_all(stat[:, None], ("tm", "rows"), 0, 0, axis_index_groups=groups).reshape(-1, channels)
    stat, later = lax.optimization_barrier((stat, later))
    away, turned, norm, spread = call(
        functools.partial(away_kernel, counted),
        [
            shape_of((16, HALF, 8, 128)),
            shape_of((channels, cells), BF16),
            shape_of((16, channels)),
            pltpu.VMEM((8, 256, 1152), BF16),
        ],
        [nearer, farther, later, x, stat, gain, bias, held(spread, pltpu.VMEM)],
        flops=cells * TAPS * channels * channels,
        aliases={7: 3},
    )
    arrived = lax.ppermute(away, "sect", swap)
    da, sums = call(
        grad_kernel,
        [shape_of((cells, channels)), shape_of((8, channels))],
        [x, norm, gain, bias, taps, inner, held(spread, pltpu.VMEM)],
        scratch=[pltpu.VMEM((cells, channels), F32)],
        flops=cells * TAPS * channels * channels,
    )
    other_sums = lax.ppermute(sums, "sect", swap)
    (home,) = call(
        home_kernel,
        [shape_of((16, HALF, 8, 128))],
        [turned, held(spread, pltpu.VMEM)],
        flops=cells * TAPS * channels * channels,
    )
    (sent,) = call(
        pair_kernel, [shape_of((16, SLOTS * 8, 128), BF16)], [home, arrived, sums, other_sums]
    )
    gathered = lax.all_to_all(sent, "tm", 0, 0)
    (share,) = call(share_kernel, [shape_of((SLOTS * 8, 128))], [gathered])
    share = jnp.broadcast_to(share.astype(jnp.float16)[None], (n_rows, SLOTS * 8, 128))
    shares = lax.all_to_all(share, "rows", 0, 0).astype(F32)
    half, sums = call(
        functools.partial(last_sum_kernel, scaling),
        [shape_of((HALF * 8, 128)), shape_of((8, 128))],
        [shares],
    )
    other = lax.ppermute(half, "sect", swap)
    input_gradient, gain_grad, bias_grad = call(
        functools.partial(finish_kernel, counted, scaling),
        [shape_of(activations.shape, BF16), shape_of((1, 128)), shape_of((1, 128))],
        [x, da, norm, sums, gain],
    )
    (whole,) = call(join_kernel, [shape_of((TAPS * 8, 128))], [half, other])
    weight_grad = whole.reshape(3, 3, 3, 8, 128).transpose(0, 1, 2, 4, 3)
    return (input_gradient, gain_grad.reshape(128), bias_grad.reshape(128), weight_grad)


def solution(mesh):
    return jax.shard_map(
        local,
        mesh=mesh,
        in_specs=(P("tm", "rows", "sect", None), P(), P(), P("tm", "rows", "sect", None), P()),
        out_specs=(P("tm", "rows", "sect", None), P(), P(), P(None, None, None, None, "tm")),
        check_vma=False,
    )
```

```python
import functools
import math

import jax
import jax.numpy as jnp
from jax import lax
from jax.experimental import pallas as pl
from jax.experimental.pallas import tpu as pltpu
from jax.sharding import PartitionSpec as P

GROUPS = 32
TAPS = 27
HALF = 14
SLOTS = HALF + 1
F32 = jnp.float32
BF16 = jnp.bfloat16
VMEM = pl.BlockSpec(memory_space=pltpu.VMEM)
HBM = pl.BlockSpec(memory_space=pltpu.HBM)


def held(x, space):
    return pltpu.with_memory_space_constraint(x, space)


def call(body, outs, args, specs=None, scratch=(), flops=0, aliases=None):
    moved = sum(math.prod(x.shape) * jnp.dtype(x.dtype).itemsize for x in list(args) + list(outs))
    return pl.pallas_call(
        body,
        out_shape=outs,
        in_specs=specs or [VMEM] * len(args),
        out_specs=[VMEM] * len(outs),
        scratch_shapes=list(scratch),
        input_output_aliases=aliases or {},
        cost_estimate=pl.CostEstimate(flops=flops, bytes_accessed=moved, transcendentals=0),
        compiler_params=pltpu.CompilerParams(vmem_limit_bytes=24 * 1024 * 1024),
    )(*args)


class Frames:
    def __init__(self, refs):
        self.refs = refs

    def __getitem__(self, index):
        index = index if isinstance(index, tuple) else (index,)
        rest = index[1:] or (slice(None),)
        if isinstance(index[0], slice):
            return jnp.stack([ref[rest] for ref in self.refs[index[0]]])
        return self.refs[index[0]][rest]

    def __setitem__(self, index, value):
        self.refs[index[0]][index[1:]] = value


def lanes_of(shape):
    return lax.broadcasted_iota(jnp.int32, shape, len(shape) - 1)


def sublanes_of(shape):
    return lax.broadcasted_iota(jnp.int32, shape, len(shape) - 2)


def group_total(v):
    lane = lanes_of(v.shape)
    v = v + jnp.where(lane % 2 == 0, pltpu.roll(v, 127, 1), pltpu.roll(v, 1, 1))
    return v + jnp.where(lane % 4 < 2, pltpu.roll(v, 126, 1), pltpu.roll(v, 2, 1))


def column_sum(v):
    part = jnp.sum(v.reshape(-1, 8, v.shape[-1]), axis=0)
    return jnp.broadcast_to(jnp.sum(part, axis=0, keepdims=True), part.shape)


def split_row(row):
    high = row.astype(BF16).astype(F32)
    middle = (row - high).astype(BF16).astype(F32)
    low = row - high - middle
    index = sublanes_of((8, 128))
    parts = jnp.where(index == 0, high, jnp.where(index == 1, middle, low))
    return jnp.concatenate([parts, parts], axis=0).astype(BF16)


def join_row(parts):
    parts = parts.astype(F32)
    return jnp.broadcast_to(parts[0:1] + parts[1:2] + parts[2:3], (8, 128))


def entry_kernel(
    up_hbm, x_hbm, gain_hbm, bias_hbm, kernel_hbm, up_ref, x_ref, gain_ref, bias_ref, kernel_ref, facing_ref, stat_ref, sems
):
    pairs = ((up_hbm, up_ref), (x_hbm, x_ref), (gain_hbm, gain_ref), (bias_hbm, bias_ref), (kernel_hbm, kernel_ref))
    copies = [pltpu.make_async_copy(source, target, sems.at[i]) for i, (source, target) in enumerate(pairs)]
    for copy in copies:
        copy.start()
    copies[0].wait()
    left = lax.axis_index("sect") == 0
    facing = jnp.where(left, up_ref[:, :, 16:].astype(F32)[:, :, 15], up_ref[:, :, :16].astype(F32)[:, :, 0])
    facing_ref[:32] = facing.reshape(32, 128).astype(BF16)
    copies[1].wait()
    x = x_ref[...].astype(F32).reshape(-1, 128)
    total = group_total(column_sum(x))
    square = group_total(column_sum(x * x))
    row = jnp.where(lanes_of(total.shape) % 4 < 2, total, square)
    stat_ref[...] = row
    facing_ref[32:] = split_row(row)
    for copy in copies[2:]:
        copy.wait()


def columns_of(side_ref):
    return side_ref[:32].astype(F32).reshape(4, 8, 128)


def edge_of(up_ref, side_ref, bottom, row):
    columns = columns_of(side_ref)
    parts = split_row(row)[:8].astype(F32)[:4]
    tail = [jnp.where(bottom, columns[:, 7], columns[:, 0]), parts, jnp.zeros((8, 128), F32)]
    main = jnp.where(bottom, up_ref[:, 7], up_ref[:, 0]).reshape(128, 128)
    return main, jnp.concatenate(tail, axis=0).astype(BF16)


def edge_kernel(up_ref, side_ref, stat_ref, near_ref, far_ref, sum_ref):
    even = lax.axis_index("rows") % 2 == 0
    row = stat_ref[...] + join_row(side_ref[32:])
    sum_ref[...] = row
    near_ref[:128], near_ref[128:] = edge_of(up_ref, side_ref, even, row)
    far_ref[:128], far_ref[128:] = edge_of(up_ref, side_ref, jnp.logical_not(even), row)


def beyond(near_ref, far_ref):
    even = lax.axis_index("rows") % 2 == 0
    outside = jnp.logical_or(lax.axis_index("rows") == 0, lax.axis_index("rows") == lax.axis_size("rows") - 1)
    near = near_ref[:128].reshape(4, 32, 128)
    far = far_ref[:128].reshape(4, 32, 128)
    far = jnp.where(outside, jnp.zeros_like(far), far)
    near_column = near_ref[128:].astype(F32)[:4]
    far_column = far_ref[128:].astype(F32)[:4]
    far_column = jnp.where(outside, jnp.zeros_like(far_column), far_column)
    above = jnp.where(even, far, near), jnp.where(even, far_column, near_column)
    below = jnp.where(even, near, far), jnp.where(even, near_column, far_column)
    return above, below


def early_kernel(up_ref, side_ref, near_ref, far_ref, stat_ref, early_ref, sent_ref, near_kept_ref, far_kept_ref):
    near_kept_ref[...] = near_ref[...]
    far_kept_ref[...] = far_ref[...]
    row = stat_ref[...] + join_row(near_ref[128:].astype(F32)[4:8])
    sent_ref[...] = jnp.broadcast_to(row[None], (sent_ref.shape[0] // 8, 8, 128)).reshape(sent_ref.shape)
    (above, above_column), (below, below_column) = beyond(near_ref, far_ref)
    columns = columns_of(side_ref)
    for f in range(2):
        early_ref[f * 320 : f * 320 + 32] = above[f]
        early_ref[f * 320 + 32 : f * 320 + 288] = up_ref[f].reshape(256, 128)
        early_ref[f * 320 + 288 : f * 320 + 320] = below[f]
        column = [above_column[f : f + 1], columns[f], below_column[f : f + 1], jnp.zeros((6, 128), F32)]
        early_ref[640 + f * 16 : 656 + f * 16] = jnp.concatenate(column, axis=0).astype(BF16)


def column_taps(core, beside):
    left = lax.axis_index("sect") == 0
    index = sublanes_of(core.shape)
    first = index == 0
    last = index == 31
    zero = jnp.zeros_like(core)
    beside = jnp.broadcast_to(beside[:, None, :], core.shape)
    ahead = jnp.where(last, jnp.where(left, beside, zero), pltpu.roll(core, 31, 1))
    behind = jnp.where(first, jnp.where(left, zero, beside), pltpu.roll(core, 1, 1))
    ahead = ahead + jnp.where(first, jnp.where(left, core, zero), zero)
    behind = behind + jnp.where(last, jnp.where(left, zero, core), zero)
    return ahead, core, behind


def put(v_ref, f, r, b, e, rows):
    j = (b * 3 + e) * 128
    count = rows.shape[0]
    v_ref[f, r * 32 : (r + count) * 32, j : j + 128] = rows.astype(BF16).reshape(count * 32, 128)


def times_taps(lhs, taps_ref, a):
    return lax.dot_general(lhs, taps_ref[a], (((1,), (1,)), ((), ())), preferred_element_type=F32)


def put_own(v_ref, f, e, part):
    zero = jnp.zeros_like(part[0])
    top = part[1] + jnp.where(lax.axis_index("rows") == 0, part[0], zero)
    low = part[6] + jnp.where(lax.axis_index("rows") == lax.axis_size("rows") - 1, part[7], zero)
    put(v_ref, f, 0, 0, e, top[None])
    put(v_ref, f, 1, 0, e, part[2:8])
    put(v_ref, f, 0, 1, e, part)
    put(v_ref, f, 1, 2, e, part[0:6])
    put(v_ref, f, 7, 2, e, low[None])


def taps_kernel(up_ref, kernel_ref, taps_ref, *v_refs):
    v_ref = Frames(v_refs)
    for a in range(3):
        for b in range(3):
            for e in range(3):
                j = (b * 3 + e) * 128
                taps_ref[a, :, j : j + 128] = kernel_ref[a, b, e]
    for f in range(4):
        put_own(v_ref, f, 1, up_ref[f].astype(F32))


def own_kernel(up_ref, side_ref, taps_ref, *refs):
    dh_ref = refs[8]
    v_ref = Frames(refs[4:8])
    columns = columns_of(side_ref)
    for f in range(4):
        ahead, _, behind = column_taps(up_ref[f].astype(F32), columns[f])
        put_own(v_ref, f, 0, ahead)
        put_own(v_ref, f, 2, behind)
    for f in range(4):
        total = None
        for a in range(3):
            if f + 2 - a < 4:
                term = times_taps(v_ref[f + 2 - a, 32:224], taps_ref, a)
                total = term if total is None else total + term
        dh_ref[f * 256 + 32 : f * 256 + 224] = total

    @pl.when(lax.axis_index("tm") == 0)
    def _():
        both = (v_ref[1, 32:224].astype(F32) + v_ref[0, 32:224].astype(F32)).astype(BF16)
        dh_ref[32:224] += times_taps(v_ref[0, 32:224], taps_ref, 1) + times_taps(both, taps_ref, 0)


def fold_first(v_ref, lo, hi):
    both = v_ref[1, lo:hi].astype(F32) + v_ref[0, lo:hi].astype(F32)
    v_ref[6, lo:hi] = both.astype(BF16)
    v_ref[7, lo:hi] = (both + v_ref[2, lo:hi].astype(F32)).astype(BF16)


def spread_edges(near_ref, far_ref, later_ref, v_ref):
    (above, above_column), (below, below_column) = beyond(near_ref, far_ref)
    row_first = lax.axis_index("rows") == 0
    row_last = lax.axis_index("rows") == lax.axis_size("rows") - 1
    outer = jnp.concatenate([above, below], axis=0).astype(F32)
    outer_column = jnp.concatenate([above_column, below_column], axis=0)
    for e, part in enumerate(column_taps(outer, outer_column)):
        for f in range(4):
            put(v_ref, f, 0, 2, e, part[f : f + 1])
            put(v_ref, f, 7, 0, e, part[f + 4 : f + 5])
    for f in range(2):
        later = later_ref[f * 320 : f * 320 + 320].astype(F32).reshape(10, 32, 128)
        column = later_ref[640 + f * 16 : 656 + f * 16].astype(F32)[:10]
        for e, part in enumerate(column_taps(later, column)):
            zero = jnp.zeros_like(part[0])
            top = part[2] + jnp.where(row_first, part[1], zero)
            low = part[7] + jnp.where(row_last, part[8], zero)
            put(v_ref, f + 4, 0, 0, e, top[None])
            put(v_ref, f + 4, 1, 0, e, part[3:10])
            put(v_ref, f + 4, 0, 1, e, part[1:9])
            put(v_ref, f + 4, 0, 2, e, part[0:7])
            put(v_ref, f + 4, 7, 2, e, low[None])

    @pl.when(lax.axis_index("tm") == 0)
    def _():
        fold_first(v_ref, 0, 256)


def grad_kernel(x_ref, norm_ref, gain_ref, bias_ref, taps_ref, part_ref, *refs):
    v_ref = Frames(refs[:8])
    da_ref, sums_ref, dh_ref = refs[8:]
    def edges(lo, hi):
        return jnp.concatenate([v_ref[lo:hi, 0:32], v_ref[lo:hi, 224:256]], axis=1).reshape((hi - lo) * 64, 1152)

    outer = times_taps(edges(0, 4), taps_ref, 2)
    one = times_taps(edges(1, 4), taps_ref, 1)
    two = times_taps(edges(2, 4), taps_ref, 0)
    outer = outer + jnp.concatenate([one, jnp.zeros((64, 128), F32)], axis=0)
    outer = outer + jnp.concatenate([two, jnp.zeros((128, 128), F32)], axis=0)
    for f in range(4):
        dh_ref[f * 256 : f * 256 + 32] = outer[f * 64 : f * 64 + 32]
        dh_ref[f * 256 + 32 : f * 256 + 224] = part_ref[f * 256 + 32 : f * 256 + 224]
        dh_ref[f * 256 + 224 : f * 256 + 256] = outer[f * 64 + 32 : f * 64 + 64]
    dh_ref[768:1024] += times_taps(v_ref[4], taps_ref, 1)
    dh_ref[512:1024] += times_taps(v_ref[4:6].reshape(512, 1152), taps_ref, 0)

    @pl.when(lax.axis_index("tm") == 0)
    def _():
        more = times_taps(edges(0, 1), taps_ref, 1) + times_taps(edges(6, 7), taps_ref, 0)
        dh_ref[0:32] += more[:32]
        dh_ref[224:256] += more[32:]

    bias_sum = jnp.zeros((8, 128), F32)
    gain_sum = jnp.zeros((8, 128), F32)
    for block in range(8):
        xhat, pre = block_of(x_ref, norm_ref, gain_ref, bias_ref, block)
        sig = 1.0 / (1.0 + jnp.exp(-pre))
        da = dh_ref[block * 128 : (block + 1) * 128] * sig * (1.0 + pre * (1.0 - sig))
        da_ref[block * 128 : (block + 1) * 128] = da
        bias_sum = bias_sum + jnp.sum(da.reshape(16, 8, 128), axis=0)
        gain_sum = gain_sum + jnp.sum((da * xhat).reshape(16, 8, 128), axis=0)
    sums_ref[...] = jnp.where(sublanes_of((8, 128)) == 0, column_sum(bias_sum), column_sum(gain_sum))


def sums_to_pair(row):
    lane = lanes_of(row.shape)
    total = jnp.where(lane % 4 < 2, row, pltpu.roll(row, 2, 1))
    square = jnp.where(lane % 4 < 2, pltpu.roll(row, 126, 1), row)
    return total, square


def product_of(turned, v_ref, a, lo, hi):
    if a == 2:
        return jnp.dot(turned, v_ref[0:4, :, lo:hi].reshape(1024, hi - lo), preferred_element_type=F32)
    source = jnp.where(lax.axis_index("tm") == 0, v_ref[7 - a, :, lo:hi], v_ref[2 - a, :, lo:hi])
    first = jnp.dot(turned[:, :256], source, preferred_element_type=F32)
    rest = v_ref[3 - a : 6 - a, :, lo:hi].reshape(768, hi - lo)
    return first + jnp.dot(turned[:, 256:], rest, preferred_element_type=F32)


def half_product(half, turned, v_ref, w_ref):
    for a, lo, hi in (((0, 0, 9), (1, 0, 5)), ((1, 5, 9), (2, 0, 9)))[half]:
        product = product_of(turned, v_ref, a, lo * 128, hi * 128)
        for j in range(lo, hi):
            block = product[:, (j - lo) * 128 : (j - lo + 1) * 128].T.reshape(16, 8, 128)
            w_ref[:, (a * 9 + j) % HALF] = block
    if half == 1:
        w_ref[:, HALF - 1] = jnp.zeros((16, 8, 128), F32)


def block_of(x_ref, norm_ref, gain_ref, bias_ref, block):
    half = (block % 2) * 4
    x = x_ref[block // 2, half : half + 4].astype(F32).reshape(128, 128)
    xhat = (x - norm_ref[0:1]) * norm_ref[8:9]
    return xhat, xhat * gain_ref[...] + bias_ref[...]


def away_kernel(
    counted,
    near_ref,
    far_ref,
    later_ref,
    x_ref,
    stat_ref,
    handed_ref,
    gain_ref,
    bias_ref,
    *refs,
):
    w_ref, turned_ref, norm_ref = refs[4:7]
    v_ref = Frames(refs[7:15])
    spread_edges(near_ref, far_ref, later_ref, v_ref)
    row = jnp.where(lax.axis_index("sect") == 0, handed_ref[...], stat_ref[...])
    total, square = sums_to_pair(jnp.broadcast_to(row, (8, 128)))
    mean = total / counted
    norm_ref[0:8] = mean
    norm_ref[8:16] = lax.rsqrt(square / counted - mean * mean + 1e-06)
    for block in range(8):
        _, pre = block_of(x_ref, norm_ref, gain_ref, bias_ref, block)
        hidden = pre * (1.0 / (1.0 + jnp.exp(-pre)))
        turned_ref[:, block * 128 : (block + 1) * 128] = hidden.T.astype(BF16)
    left = lax.axis_index("sect") == 0

    @pl.when(left)
    def _():
        half_product(1, turned_ref[...], v_ref, w_ref)

    @pl.when(jnp.logical_not(left))
    def _():
        half_product(0, turned_ref[...], v_ref, w_ref)


def home_kernel(turned_ref, *refs):
    v_ref = Frames(refs[:8])
    w_ref = refs[8]
    left = lax.axis_index("sect") == 0

    @pl.when(left)
    def _():
        half_product(0, turned_ref[...], v_ref, w_ref)

    @pl.when(jnp.logical_not(left))
    def _():
        half_product(1, turned_ref[...], v_ref, w_ref)


def split_sums(sums):
    row = sublanes_of(sums.shape)
    high = sums.astype(BF16).astype(F32)
    middle = (sums - high).astype(BF16).astype(F32)
    low = sums - high - middle
    return jnp.where(
        row < 2, high, jnp.where(row < 4, pltpu.roll(middle, 2, 0), pltpu.roll(low, 4, 0))
    )


def join_sums(parts):
    return parts + pltpu.roll(parts, 6, 0) + pltpu.roll(parts, 4, 0)


def pair_kernel(own_ref, other_ref, sums_ref, other_sums_ref, out_ref):
    slot = split_sums(sums_ref[...] + other_sums_ref[...])
    for i in range(16):
        body = (own_ref[i] + other_ref[i]).reshape(HALF * 8, 128)
        out_ref[i] = jnp.concatenate([body, slot], axis=0).astype(BF16)


def power_for(values):
    most = jnp.max(jnp.max(jnp.abs(values), axis=0, keepdims=True), axis=1, keepdims=True)
    bits = jnp.log(jnp.maximum(most, 1e-30)) * 1.4426950408889634
    return jnp.clip(jnp.floor(14.0 - bits), -100.0, 100.0)


def share_kernel(in_ref, out_ref):
    rows = HALF * 8
    total = in_ref[0].astype(F32)
    for i in range(1, in_ref.shape[0]):
        total = total + in_ref[i].astype(F32)
    body = total[:rows]
    sums = join_sums(total[rows:])
    index = sublanes_of(sums.shape)
    sums = jnp.where(index < 2, sums, jnp.zeros_like(sums))
    power = power_for(body)
    power_of_sums = power_for(sums)
    slot = split_sums(sums * jnp.exp2(power_of_sums))
    slot = jnp.where(index == 6, power, jnp.where(index == 7, power_of_sums, slot))
    out_ref[:rows] = body * jnp.exp2(power)
    out_ref[rows:] = slot


def last_sum_kernel(scaling, in_ref, half_ref, sums_ref):
    rows = HALF * 8
    total = jnp.zeros((rows, 128), F32)
    sums = jnp.zeros((8, 128), F32)
    for i in range(in_ref.shape[0]):
        slot = in_ref[i, rows:]
        total = total + in_ref[i, :rows] * jnp.exp2(-slot[6:7])
        sums = sums + join_sums(slot) * jnp.exp2(-slot[7:8])
    half_ref[...] = total * scaling
    sums_ref[...] = sums


def finish_kernel(counted, scaling, x_ref, da_ref, norm_ref, sums_ref, gain_ref, out_ref, gain_grad_ref, bias_grad_ref):
    gain = gain_ref[...]
    mean = norm_ref[0:1]
    rstd = norm_ref[8:9]
    sums = sums_ref[...]
    bias_grad_ref[...] = sums[0:1] * scaling
    gain_grad_ref[...] = sums[1:2] * scaling
    averages = group_total(gain * sums) / counted
    leading = averages[0:1]
    trailing = averages[1:2]
    xhat = (x_ref[...].astype(F32).reshape(-1, 128) - mean) * rstd
    grad = rstd * (da_ref[...] * gain - leading - xhat * trailing)
    out_ref[...] = grad.astype(BF16).reshape(out_ref.shape)


def join_kernel(half_ref, other_ref, out_ref):
    left = lax.axis_index("sect") == 0
    half = half_ref[...]
    other = other_ref[...]
    out_ref[: HALF * 8] = jnp.where(left, half, other)
    out_ref[HALF * 8 :] = jnp.where(left, other, half)[: (TAPS - HALF) * 8]


def shape_of(shape, dtype=F32):
    return jax.ShapeDtypeStruct(shape, dtype)


def local(activations, group_norm_gain, group_norm_bias, upstream, kernel):
    frames, height, columns, channels = activations.shape
    n_time, n_rows, n_sect = (lax.axis_size(axis) for axis in ("tm", "rows", "sect"))
    cells = frames * height * columns
    total_cells = cells * n_time * n_rows * n_sect
    counted = float(total_cells * (channels // GROUPS))
    scaling = float(total_cells) ** (-0.5)
    swap = [(0, 1), (1, 0)]
    near = [(i, i ^ 1) for i in range(n_rows)]
    far = [(i, (i - 1) % n_rows if i % 2 == 0 else (i + 1) % n_rows) for i in range(n_rows)]

    up, x, gain, bias, weights, facing, stat = call(
        entry_kernel,
        [
            shape_of(upstream.shape, BF16),
            pltpu.VMEM(activations.shape, BF16),
            shape_of((1, channels)),
            shape_of((1, channels)),
            shape_of(kernel.shape, BF16),
            shape_of((48, channels), BF16),
            shape_of((8, channels)),
        ],
        [
            held(upstream, pltpu.HBM),
            held(activations, pltpu.HBM),
            held(group_norm_gain.reshape(1, channels), pltpu.HBM),
            held(group_norm_bias.reshape(1, channels), pltpu.HBM),
            held(kernel, pltpu.HBM),
        ],
        [HBM] * 5,
        [pltpu.SemaphoreType.DMA((5,))],
    )
    side = lax.ppermute(facing, "sect", swap)
    frame = pltpu.VMEM((256, 1152), BF16)

    def kept(arrays):
        return [held(array, pltpu.VMEM) for array in arrays]

    taps, *spread = call(
        taps_kernel, [pltpu.VMEM((3, channels, 9 * channels), BF16)] + [frame] * 4, [up, weights]
    )
    side, taps = lax.optimization_barrier((side, taps))
    nearer, farther, stat = call(
        edge_kernel,
        [shape_of((144, channels), BF16), shape_of((144, channels), BF16), shape_of((8, channels))],
        [up, side, stat],
    )
    nearer = lax.ppermute(nearer, "rows", near)
    farther = lax.ppermute(farther, "rows", far)
    *spread, inner = call(
        own_kernel,
        [frame] * 4 + [pltpu.VMEM((cells, channels), F32)],
        [up, side] + kept([taps] + spread),
        flops=cells * TAPS * channels * channels,
        aliases={3 + f: f for f in range(4)},
    )
    nearer, inner = lax.optimization_barrier((nearer, inner))
    groups = [[t * n_rows + r for t in range(n_time) for r in chosen] for chosen in ((1, 2, 4, 7), (0, 3, 5, 6))]
    strip = pltpu.VMEM((144, channels), BF16)
    early, stat, nearer, farther = call(
        early_kernel,
        [shape_of((672, channels), BF16), shape_of((len(groups[0]), channels)), strip, strip],
        [up, side, nearer, farther, stat],
    )
    later = lax.ppermute(early, "tm", [(i + 1, i) for i in range(n_time - 1)])

    def over_groups(row):
        rows = lax.all_to_all(row[:, None], ("tm", "rows"), 0, 0, axis_index_groups=groups)
        return jnp.sum(rows, axis=0)

    on_second = lax.axis_index("sect") == 1
    stat = lax.cond(on_second, over_groups, lambda row: row[:1], stat)
    handed = lax.ppermute(stat, "sect", [(1, 0)])
    handed, later = lax.optimization_barrier((handed, later))
    away, turned, norm, *spread = call(
        functools.partial(away_kernel, counted),
        [shape_of((16, HALF, 8, 128)), shape_of((channels, cells), BF16), shape_of((16, channels))] + [frame] * 8,
        kept([nearer, farther]) + [later] + kept([x]) + [stat, handed, gain, bias] + kept(spread),
        flops=cells * TAPS * channels * channels,
        aliases={8 + f: 3 + f for f in range(4)},
    )
    arrived = lax.ppermute(away, "sect", swap)
    da, sums = call(
        grad_kernel,
        [shape_of((cells, channels)), shape_of((8, channels))],
        kept([x]) + [norm, gain, bias] + kept([taps, inner] + spread),
        scratch=[pltpu.VMEM((cells, channels), F32)],
        flops=cells * TAPS * channels * channels,
    )
    other_sums = lax.ppermute(sums, "sect", swap)
    (home,) = call(
        home_kernel,
        [shape_of((16, HALF, 8, 128))],
        [turned] + kept(spread),
        flops=cells * TAPS * channels * channels,
    )
    (sent,) = call(
        pair_kernel, [shape_of((16, SLOTS * 8, 128), BF16)], [home, arrived, sums, other_sums]
    )
    gathered = lax.all_to_all(sent, "tm", 0, 0)
    (share,) = call(share_kernel, [shape_of((SLOTS * 8, 128))], [gathered])
    share = jnp.broadcast_to(share.astype(jnp.float16)[None], (n_rows, SLOTS * 8, 128))
    shares = lax.all_to_all(share, "rows", 0, 0).astype(F32)
    half, sums = call(
        functools.partial(last_sum_kernel, scaling),
        [shape_of((HALF * 8, 128)), shape_of((8, 128))],
        [shares],
    )
    other = lax.ppermute(half, "sect", swap)
    input_gradient, gain_grad, bias_grad = call(
        functools.partial(finish_kernel, counted, scaling),
        [shape_of(activations.shape, BF16), shape_of((1, 128)), shape_of((1, 128))],
        kept([x]) + [da, norm, sums, gain],
    )
    (whole,) = call(join_kernel, [shape_of((TAPS * 8, 128))], [half, other])
    weight_grad = whole.reshape(3, 3, 3, 8, 128).transpose(0, 1, 2, 4, 3)
    return (input_gradient, gain_grad.reshape(128), bias_grad.reshape(128), weight_grad)


def solution(mesh):
    return jax.shard_map(
        local,
        mesh=mesh,
        in_specs=(P("tm", "rows", "sect", None), P(), P(), P("tm", "rows", "sect", None), P()),
        out_specs=(P("tm", "rows", "sect", None), P(), P(), P(None, None, None, None, "tm")),
        check_vma=False,
    )
```

```python
import functools
import math

import jax
import jax.numpy as jnp
from jax import lax
from jax.experimental import pallas as pl
from jax.experimental.pallas import tpu as pltpu
from jax.sharding import PartitionSpec as P

GROUPS = 32
TAPS = 27
HALF = 14
SLOTS = HALF + 1
F32 = jnp.float32
BF16 = jnp.bfloat16
VMEM = pl.BlockSpec(memory_space=pltpu.VMEM)
HBM = pl.BlockSpec(memory_space=pltpu.HBM)


def held(x, space):
    return pltpu.with_memory_space_constraint(x, space)


def call(body, outs, args, specs=None, scratch=(), flops=0, aliases=None):
    moved = sum(math.prod(x.shape) * jnp.dtype(x.dtype).itemsize for x in list(args) + list(outs))
    return pl.pallas_call(
        body,
        out_shape=outs,
        in_specs=specs or [VMEM] * len(args),
        out_specs=[VMEM] * len(outs),
        scratch_shapes=list(scratch),
        input_output_aliases=aliases or {},
        cost_estimate=pl.CostEstimate(flops=flops, bytes_accessed=moved, transcendentals=0),
        compiler_params=pltpu.CompilerParams(vmem_limit_bytes=24 * 1024 * 1024),
    )(*args)


def lanes_of(shape):
    return lax.broadcasted_iota(jnp.int32, shape, len(shape) - 1)


def sublanes_of(shape):
    return lax.broadcasted_iota(jnp.int32, shape, len(shape) - 2)


def group_total(v):
    lane = lanes_of(v.shape)
    v = v + jnp.where(lane % 2 == 0, pltpu.roll(v, 127, 1), pltpu.roll(v, 1, 1))
    return v + jnp.where(lane % 4 < 2, pltpu.roll(v, 126, 1), pltpu.roll(v, 2, 1))


def column_sum(v):
    part = jnp.sum(v.reshape(-1, 8, v.shape[-1]), axis=0)
    return jnp.broadcast_to(jnp.sum(part, axis=0, keepdims=True), part.shape)


def split_row(row):
    high = row.astype(BF16).astype(F32)
    middle = (row - high).astype(BF16).astype(F32)
    low = row - high - middle
    index = sublanes_of((8, 128))
    parts = jnp.where(index == 0, high, jnp.where(index == 1, middle, low))
    return jnp.concatenate([parts, parts], axis=0).astype(BF16)


def join_row(parts):
    parts = parts.astype(F32)
    return jnp.broadcast_to(parts[0:1] + parts[1:2] + parts[2:3], (8, 128))


def entry_kernel(
    up_hbm, x_hbm, gain_hbm, bias_hbm, kernel_hbm, up_ref, x_ref, gain_ref, bias_ref, kernel_ref, facing_ref, stat_ref, sems
):
    pairs = ((up_hbm, up_ref), (x_hbm, x_ref), (gain_hbm, gain_ref), (bias_hbm, bias_ref), (kernel_hbm, kernel_ref))
    copies = [pltpu.make_async_copy(source, target, sems.at[i]) for i, (source, target) in enumerate(pairs)]
    for copy in copies:
        copy.start()
    copies[0].wait()
    left = lax.axis_index("sect") == 0
    facing = jnp.where(left, up_ref[:, :, 16:].astype(F32)[:, :, 15], up_ref[:, :, :16].astype(F32)[:, :, 0])
    facing_ref[:32] = facing.reshape(32, 128).astype(BF16)
    copies[1].wait()
    x = x_ref[...].astype(F32).reshape(-1, 128)
    total = group_total(column_sum(x))
    square = group_total(column_sum(x * x))
    row = jnp.where(lanes_of(total.shape) % 4 < 2, total, square)
    stat_ref[...] = row
    facing_ref[32:] = split_row(row)
    for copy in copies[2:]:
        copy.wait()


def columns_of(side_ref):
    return side_ref[:32].astype(F32).reshape(4, 8, 128)


def edge_of(up_ref, side_ref, bottom, row):
    columns = columns_of(side_ref)
    parts = split_row(row)[:8].astype(F32)[:4]
    tail = [jnp.where(bottom, columns[:, 7], columns[:, 0]), parts, jnp.zeros((8, 128), F32)]
    main = jnp.where(bottom, up_ref[:, 7], up_ref[:, 0]).reshape(128, 128)
    return main, jnp.concatenate(tail, axis=0).astype(BF16)


def edge_kernel(up_ref, side_ref, stat_ref, near_ref, far_ref, sum_ref):
    even = lax.axis_index("rows") % 2 == 0
    row = stat_ref[...] + join_row(side_ref[32:])
    sum_ref[...] = row
    near_ref[:128], near_ref[128:] = edge_of(up_ref, side_ref, even, row)
    far_ref[:128], far_ref[128:] = edge_of(up_ref, side_ref, jnp.logical_not(even), row)


def beyond(near_ref, far_ref):
    even = lax.axis_index("rows") % 2 == 0
    outside = jnp.logical_or(lax.axis_index("rows") == 0, lax.axis_index("rows") == lax.axis_size("rows") - 1)
    near = near_ref[:128].reshape(4, 32, 128)
    far = far_ref[:128].reshape(4, 32, 128)
    far = jnp.where(outside, jnp.zeros_like(far), far)
    near_column = near_ref[128:].astype(F32)[:4]
    far_column = far_ref[128:].astype(F32)[:4]
    far_column = jnp.where(outside, jnp.zeros_like(far_column), far_column)
    above = jnp.where(even, far, near), jnp.where(even, far_column, near_column)
    below = jnp.where(even, near, far), jnp.where(even, near_column, far_column)
    return above, below


def early_kernel(up_ref, side_ref, near_ref, far_ref, stat_ref, early_ref, sent_ref):
    row = stat_ref[...] + join_row(near_ref[128:].astype(F32)[4:8])
    sent_ref[...] = jnp.broadcast_to(row[None], (sent_ref.shape[0] // 8, 8, 128)).reshape(sent_ref.shape)
    (above, above_column), (below, below_column) = beyond(near_ref, far_ref)
    columns = columns_of(side_ref)
    for f in range(2):
        early_ref[f * 320 : f * 320 + 32] = above[f]
        early_ref[f * 320 + 32 : f * 320 + 288] = up_ref[f].reshape(256, 128)
        early_ref[f * 320 + 288 : f * 320 + 320] = below[f]
        column = [above_column[f : f + 1], columns[f], below_column[f : f + 1], jnp.zeros((6, 128), F32)]
        early_ref[640 + f * 16 : 656 + f * 16] = jnp.concatenate(column, axis=0).astype(BF16)


def column_taps(core, beside):
    left = lax.axis_index("sect") == 0
    index = sublanes_of(core.shape)
    first = index == 0
    last = index == 31
    zero = jnp.zeros_like(core)
    beside = jnp.broadcast_to(beside[:, None, :], core.shape)
    ahead = jnp.where(last, jnp.where(left, beside, zero), pltpu.roll(core, 31, 1))
    behind = jnp.where(first, jnp.where(left, zero, beside), pltpu.roll(core, 1, 1))
    ahead = ahead + jnp.where(first, jnp.where(left, core, zero), zero)
    behind = behind + jnp.where(last, jnp.where(left, zero, core), zero)
    return ahead, core, behind


def put(v_ref, f, r, b, e, rows):
    j = (b * 3 + e) * 128
    count = rows.shape[0]
    v_ref[f, r * 32 : (r + count) * 32, j : j + 128] = rows.astype(BF16).reshape(count * 32, 128)


def times_taps(lhs, taps_ref, a):
    return lax.dot_general(lhs, taps_ref[a], (((1,), (1,)), ((), ())), preferred_element_type=F32)


def put_own(v_ref, f, e, part):
    zero = jnp.zeros_like(part[0])
    top = part[1] + jnp.where(lax.axis_index("rows") == 0, part[0], zero)
    low = part[6] + jnp.where(lax.axis_index("rows") == lax.axis_size("rows") - 1, part[7], zero)
    put(v_ref, f, 0, 0, e, top[None])
    put(v_ref, f, 1, 0, e, part[2:8])
    put(v_ref, f, 0, 1, e, part)
    put(v_ref, f, 1, 2, e, part[0:6])
    put(v_ref, f, 7, 2, e, low[None])


def taps_kernel(up_ref, kernel_ref, v_ref, taps_ref):
    for a in range(3):
        for b in range(3):
            for e in range(3):
                j = (b * 3 + e) * 128
                taps_ref[a, :, j : j + 128] = kernel_ref[a, b, e]
    for f in range(4):
        put_own(v_ref, f, 1, up_ref[f].astype(F32))


def own_kernel(up_ref, side_ref, taps_ref, begun_ref, v_ref, dh_ref):
    columns = columns_of(side_ref)
    for f in range(4):
        ahead, _, behind = column_taps(up_ref[f].astype(F32), columns[f])
        put_own(v_ref, f, 0, ahead)
        put_own(v_ref, f, 2, behind)
    for f in range(4):
        total = None
        for a in range(3):
            if f + 2 - a < 4:
                term = times_taps(v_ref[f + 2 - a, 32:224], taps_ref, a)
                total = term if total is None else total + term
        dh_ref[f * 256 + 32 : f * 256 + 224] = total

    @pl.when(lax.axis_index("tm") == 0)
    def _():
        fold_first(v_ref, 32, 224)
        dh_ref[32:224] += times_taps(v_ref[0, 32:224], taps_ref, 1) + times_taps(v_ref[6, 32:224], taps_ref, 0)


def fold_first(v_ref, lo, hi):
    both = v_ref[1, lo:hi].astype(F32) + v_ref[0, lo:hi].astype(F32)
    v_ref[6, lo:hi] = both.astype(BF16)
    v_ref[7, lo:hi] = (both + v_ref[2, lo:hi].astype(F32)).astype(BF16)


def spread_edges(near_ref, far_ref, later_ref, v_ref):
    (above, above_column), (below, below_column) = beyond(near_ref, far_ref)
    row_first = lax.axis_index("rows") == 0
    row_last = lax.axis_index("rows") == lax.axis_size("rows") - 1
    outer = jnp.concatenate([above, below], axis=0).astype(F32)
    outer_column = jnp.concatenate([above_column, below_column], axis=0)
    for e, part in enumerate(column_taps(outer, outer_column)):
        for f in range(4):
            put(v_ref, f, 0, 2, e, part[f : f + 1])
            put(v_ref, f, 7, 0, e, part[f + 4 : f + 5])
    for f in range(2):
        later = later_ref[f * 320 : f * 320 + 320].astype(F32).reshape(10, 32, 128)
        column = later_ref[640 + f * 16 : 656 + f * 16].astype(F32)[:10]
        for e, part in enumerate(column_taps(later, column)):
            zero = jnp.zeros_like(part[0])
            top = part[2] + jnp.where(row_first, part[1], zero)
            low = part[7] + jnp.where(row_last, part[8], zero)
            put(v_ref, f + 4, 0, 0, e, top[None])
            put(v_ref, f + 4, 1, 0, e, part[3:10])
            put(v_ref, f + 4, 0, 1, e, part[1:9])
            put(v_ref, f + 4, 0, 2, e, part[0:7])
            put(v_ref, f + 4, 7, 2, e, low[None])

    @pl.when(lax.axis_index("tm") == 0)
    def _():
        fold_first(v_ref, 0, 32)
        fold_first(v_ref, 224, 256)


def grad_kernel(x_ref, norm_ref, gain_ref, bias_ref, taps_ref, part_ref, v_ref, da_ref, sums_ref, dh_ref):
    def edges(lo, hi):
        return jnp.concatenate([v_ref[lo:hi, 0:32], v_ref[lo:hi, 224:256]], axis=1).reshape((hi - lo) * 64, 1152)

    outer = times_taps(edges(0, 4), taps_ref, 2)
    one = times_taps(edges(1, 4), taps_ref, 1)
    two = times_taps(edges(2, 4), taps_ref, 0)
    outer = outer + jnp.concatenate([one, jnp.zeros((64, 128), F32)], axis=0)
    outer = outer + jnp.concatenate([two, jnp.zeros((128, 128), F32)], axis=0)
    for f in range(4):
        dh_ref[f * 256 : f * 256 + 32] = outer[f * 64 : f * 64 + 32]
        dh_ref[f * 256 + 32 : f * 256 + 224] = part_ref[f * 256 + 32 : f * 256 + 224]
        dh_ref[f * 256 + 224 : f * 256 + 256] = outer[f * 64 + 32 : f * 64 + 64]
    dh_ref[768:1024] += times_taps(v_ref[4], taps_ref, 1)
    dh_ref[512:1024] += times_taps(v_ref[4:6].reshape(512, 1152), taps_ref, 0)

    @pl.when(lax.axis_index("tm") == 0)
    def _():
        more = times_taps(edges(0, 1), taps_ref, 1) + times_taps(edges(6, 7), taps_ref, 0)
        dh_ref[0:32] += more[:32]
        dh_ref[224:256] += more[32:]

    bias_sum = jnp.zeros((8, 128), F32)
    gain_sum = jnp.zeros((8, 128), F32)
    for block in range(8):
        xhat, pre = block_of(x_ref, norm_ref, gain_ref, bias_ref, block)
        sig = 1.0 / (1.0 + jnp.exp(-pre))
        da = dh_ref[block * 128 : (block + 1) * 128] * sig * (1.0 + pre * (1.0 - sig))
        da_ref[block * 128 : (block + 1) * 128] = da
        bias_sum = bias_sum + jnp.sum(da.reshape(16, 8, 128), axis=0)
        gain_sum = gain_sum + jnp.sum((da * xhat).reshape(16, 8, 128), axis=0)
    sums_ref[...] = jnp.where(sublanes_of((8, 128)) == 0, column_sum(bias_sum), column_sum(gain_sum))


def sums_to_pair(row):
    lane = lanes_of(row.shape)
    total = jnp.where(lane % 4 < 2, row, pltpu.roll(row, 2, 1))
    square = jnp.where(lane % 4 < 2, pltpu.roll(row, 126, 1), row)
    return total, square


def product_of(turned, v_ref, a, lo, hi):
    if a == 2:
        return jnp.dot(turned, v_ref[0:4, :, lo:hi].reshape(1024, hi - lo), preferred_element_type=F32)
    source = jnp.where(lax.axis_index("tm") == 0, 7 - a, 2 - a)
    first = jnp.dot(turned[:, :256], v_ref[source, :, lo:hi], preferred_element_type=F32)
    rest = v_ref[3 - a : 6 - a, :, lo:hi].reshape(768, hi - lo)
    return first + jnp.dot(turned[:, 256:], rest, preferred_element_type=F32)


def half_product(half, turned, v_ref, w_ref):
    for a, lo, hi in (((0, 0, 9), (1, 0, 5)), ((1, 5, 9), (2, 0, 9)))[half]:
        product = product_of(turned, v_ref, a, lo * 128, hi * 128)
        for j in range(lo, hi):
            block = product[:, (j - lo) * 128 : (j - lo + 1) * 128].T.reshape(16, 8, 128)
            w_ref[:, (a * 9 + j) % HALF] = block
    if half == 1:
        w_ref[:, HALF - 1] = jnp.zeros((16, 8, 128), F32)


def block_of(x_ref, norm_ref, gain_ref, bias_ref, block):
    half = (block % 2) * 4
    x = x_ref[block // 2, half : half + 4].astype(F32).reshape(128, 128)
    xhat = (x - norm_ref[0:1]) * norm_ref[8:9]
    return xhat, xhat * gain_ref[...] + bias_ref[...]


def away_kernel(
    counted, near_ref, far_ref, later_ref, x_ref, stat_ref, gain_ref, bias_ref, begun_ref, w_ref, turned_ref, norm_ref, v_ref
):
    spread_edges(near_ref, far_ref, later_ref, v_ref)
    total, square = sums_to_pair(column_sum(stat_ref[...]))
    mean = total / counted
    norm_ref[0:8] = mean
    norm_ref[8:16] = lax.rsqrt(square / counted - mean * mean + 1e-06)
    for block in range(8):
        _, pre = block_of(x_ref, norm_ref, gain_ref, bias_ref, block)
        hidden = pre * (1.0 / (1.0 + jnp.exp(-pre)))
        turned_ref[:, block * 128 : (block + 1) * 128] = hidden.astype(BF16).T
    left = lax.axis_index("sect") == 0

    @pl.when(left)
    def _():
        half_product(1, turned_ref[...], v_ref, w_ref)

    @pl.when(jnp.logical_not(left))
    def _():
        half_product(0, turned_ref[...], v_ref, w_ref)


def home_kernel(turned_ref, v_ref, w_ref):
    left = lax.axis_index("sect") == 0

    @pl.when(left)
    def _():
        half_product(0, turned_ref[...], v_ref, w_ref)

    @pl.when(jnp.logical_not(left))
    def _():
        half_product(1, turned_ref[...], v_ref, w_ref)


def split_sums(sums):
    row = sublanes_of(sums.shape)
    high = sums.astype(BF16).astype(F32)
    middle = (sums - high).astype(BF16).astype(F32)
    low = sums - high - middle
    return jnp.where(
        row < 2, high, jnp.where(row < 4, pltpu.roll(middle, 2, 0), pltpu.roll(low, 4, 0))
    )


def join_sums(parts):
    return parts + pltpu.roll(parts, 6, 0) + pltpu.roll(parts, 4, 0)


def pair_kernel(own_ref, other_ref, sums_ref, other_sums_ref, out_ref):
    slot = split_sums(sums_ref[...] + other_sums_ref[...])
    for i in range(16):
        body = (own_ref[i] + other_ref[i]).reshape(HALF * 8, 128)
        out_ref[i] = jnp.concatenate([body, slot], axis=0).astype(BF16)


def power_for(values):
    most = jnp.max(jnp.max(jnp.abs(values), axis=0, keepdims=True), axis=1, keepdims=True)
    bits = jnp.log(jnp.maximum(most, 1e-30)) * 1.4426950408889634
    return jnp.clip(jnp.floor(14.0 - bits), -100.0, 100.0)


def share_kernel(in_ref, out_ref):
    rows = HALF * 8
    total = in_ref[0].astype(F32)
    for i in range(1, in_ref.shape[0]):
        total = total + in_ref[i].astype(F32)
    body = total[:rows]
    sums = join_sums(total[rows:])
    index = sublanes_of(sums.shape)
    sums = jnp.where(index < 2, sums, jnp.zeros_like(sums))
    power = power_for(body)
    power_of_sums = power_for(sums)
    slot = split_sums(sums * jnp.exp2(power_of_sums))
    slot = jnp.where(index == 6, power, jnp.where(index == 7, power_of_sums, slot))
    out_ref[:rows] = body * jnp.exp2(power)
    out_ref[rows:] = slot


def last_sum_kernel(scaling, in_ref, half_ref, sums_ref):
    rows = HALF * 8
    total = jnp.zeros((rows, 128), F32)
    sums = jnp.zeros((8, 128), F32)
    for i in range(in_ref.shape[0]):
        slot = in_ref[i, rows:]
        total = total + in_ref[i, :rows] * jnp.exp2(-slot[6:7])
        sums = sums + join_sums(slot) * jnp.exp2(-slot[7:8])
    half_ref[...] = total * scaling
    sums_ref[...] = sums


def finish_kernel(counted, scaling, x_ref, da_ref, norm_ref, sums_ref, gain_ref, out_ref, gain_grad_ref, bias_grad_ref):
    gain = gain_ref[...]
    mean = norm_ref[0:1]
    rstd = norm_ref[8:9]
    sums = sums_ref[...]
    bias_grad_ref[...] = sums[0:1] * scaling
    gain_grad_ref[...] = sums[1:2] * scaling
    averages = group_total(gain * sums) / counted
    leading = averages[0:1]
    trailing = averages[1:2]
    xhat = (x_ref[...].astype(F32).reshape(-1, 128) - mean) * rstd
    grad = rstd * (da_ref[...] * gain - leading - xhat * trailing)
    out_ref[...] = grad.astype(BF16).reshape(out_ref.shape)


def join_kernel(half_ref, other_ref, out_ref):
    left = lax.axis_index("sect") == 0
    half = half_ref[...]
    other = other_ref[...]
    out_ref[: HALF * 8] = jnp.where(left, half, other)
    out_ref[HALF * 8 :] = jnp.where(left, other, half)[: (TAPS - HALF) * 8]


def shape_of(shape, dtype=F32):
    return jax.ShapeDtypeStruct(shape, dtype)


def local(activations, group_norm_gain, group_norm_bias, upstream, kernel):
    frames, height, columns, channels = activations.shape
    n_time, n_rows, n_sect = (lax.axis_size(axis) for axis in ("tm", "rows", "sect"))
    cells = frames * height * columns
    total_cells = cells * n_time * n_rows * n_sect
    counted = float(total_cells * (channels // GROUPS))
    scaling = float(total_cells) ** (-0.5)
    swap = [(0, 1), (1, 0)]
    near = [(i, i ^ 1) for i in range(n_rows)]
    far = [(i, (i - 1) % n_rows if i % 2 == 0 else (i + 1) % n_rows) for i in range(n_rows)]

    up, x, gain, bias, weights, facing, stat = call(
        entry_kernel,
        [
            shape_of(upstream.shape, BF16),
            shape_of(activations.shape, BF16),
            shape_of((1, channels)),
            shape_of((1, channels)),
            shape_of(kernel.shape, BF16),
            shape_of((48, channels), BF16),
            shape_of((8, channels)),
        ],
        [
            held(upstream, pltpu.HBM),
            held(activations, pltpu.HBM),
            held(group_norm_gain.reshape(1, channels), pltpu.HBM),
            held(group_norm_bias.reshape(1, channels), pltpu.HBM),
            held(kernel, pltpu.HBM),
        ],
        [HBM] * 5,
        [pltpu.SemaphoreType.DMA((5,))],
    )
    side = lax.ppermute(facing, "sect", swap)
    spread, taps = call(
        taps_kernel,
        [pltpu.VMEM((8, 256, 1152), BF16), shape_of((3, channels, 9 * channels), BF16)],
        [up, weights],
    )
    side, taps = lax.optimization_barrier((side, taps))
    nearer, farther, stat = call(
        edge_kernel,
        [shape_of((144, channels), BF16), shape_of((144, channels), BF16), shape_of((8, channels))],
        [up, side, stat],
    )
    nearer = lax.ppermute(nearer, "rows", near)
    farther = lax.ppermute(farther, "rows", far)
    spread, inner = call(
        own_kernel,
        [pltpu.VMEM((8, 256, 1152), BF16), shape_of((cells, channels))],
        [up, side, taps, held(spread, pltpu.VMEM)],
        flops=cells * TAPS * channels * channels,
        aliases={3: 0},
    )
    nearer, inner = lax.optimization_barrier((nearer, inner))
    groups = [[t * n_rows + r for t in range(n_time) for r in chosen] for chosen in ((1, 2, 4, 7), (0, 3, 5, 6))]
    early, stat = call(
        early_kernel,
        [shape_of((672, channels), BF16), shape_of((len(groups[0]), channels))],
        [up, side, nearer, farther, stat],
        [VMEM, VMEM, VMEM, VMEM, VMEM],
    )
    later = lax.ppermute(early, "tm", [(i + 1, i) for i in range(n_time - 1)])
    stat = lax.all_to_all(stat[:, None], ("tm", "rows"), 0, 0, axis_index_groups=groups).reshape(-1, channels)
    stat, later = lax.optimization_barrier((stat, later))
    away, turned, norm, spread = call(
        functools.partial(away_kernel, counted),
        [
            shape_of((16, HALF, 8, 128)),
            shape_of((channels, cells), BF16),
            shape_of((16, channels)),
            pltpu.VMEM((8, 256, 1152), BF16),
        ],
        [nearer, farther, later, x, stat, gain, bias, held(spread, pltpu.VMEM)],
        flops=cells * TAPS * channels * channels,
        aliases={7: 3},
    )
    arrived = lax.ppermute(away, "sect", swap)
    da, sums = call(
        grad_kernel,
        [shape_of((cells, channels)), shape_of((8, channels))],
        [x, norm, gain, bias, taps, inner, held(spread, pltpu.VMEM)],
        scratch=[pltpu.VMEM((cells, channels), F32)],
        flops=cells * TAPS * channels * channels,
    )
    other_sums = lax.ppermute(sums, "sect", swap)
    (home,) = call(
        home_kernel,
        [shape_of((16, HALF, 8, 128))],
        [turned, held(spread, pltpu.VMEM)],
        flops=cells * TAPS * channels * channels,
    )
    (sent,) = call(
        pair_kernel, [shape_of((16, SLOTS * 8, 128), BF16)], [home, arrived, sums, other_sums]
    )
    gathered = lax.all_to_all(sent, "tm", 0, 0)
    (share,) = call(share_kernel, [shape_of((SLOTS * 8, 128))], [gathered])
    share = jnp.broadcast_to(share.astype(jnp.float16)[None], (n_rows, SLOTS * 8, 128))
    shares = lax.all_to_all(share, "rows", 0, 0).astype(F32)
    half, sums = call(
        functools.partial(last_sum_kernel, scaling),
        [shape_of((HALF * 8, 128)), shape_of((8, 128))],
        [shares],
    )
    other = lax.ppermute(half, "sect", swap)
    input_gradient, gain_grad, bias_grad = call(
        functools.partial(finish_kernel, counted, scaling),
        [shape_of(activations.shape, BF16), shape_of((1, 128)), shape_of((1, 128))],
        [x, da, norm, sums, gain],
    )
    (whole,) = call(join_kernel, [shape_of((TAPS * 8, 128))], [half, other])
    weight_grad = whole.reshape(3, 3, 3, 8, 128).transpose(0, 1, 2, 4, 3)
    return (input_gradient, gain_grad.reshape(128), bias_grad.reshape(128), weight_grad)


def solution(mesh):
    return jax.shard_map(
        local,
        mesh=mesh,
        in_specs=(P("tm", "rows", "sect", None), P(), P(), P("tm", "rows", "sect", None), P()),
        out_specs=(P("tm", "rows", "sect", None), P(), P(), P(None, None, None, None, "tm")),
        check_vma=False,
    )
```

```python
import functools
import math

import jax
import jax.numpy as jnp
from jax import lax
from jax.experimental import pallas as pl
from jax.experimental.pallas import tpu as pltpu
from jax.sharding import PartitionSpec as P

GROUPS = 32
TAPS = 27
HALF = 14
SLOTS = HALF + 1
F32 = jnp.float32
BF16 = jnp.bfloat16
VMEM = pl.BlockSpec(memory_space=pltpu.VMEM)
HBM = pl.BlockSpec(memory_space=pltpu.HBM)


def held(x, space):
    return pltpu.with_memory_space_constraint(x, space)


def call(body, outs, args, specs=None, scratch=(), flops=0, aliases=None):
    moved = sum(math.prod(x.shape) * jnp.dtype(x.dtype).itemsize for x in list(args) + list(outs))
    return pl.pallas_call(
        body,
        out_shape=outs,
        in_specs=specs or [VMEM] * len(args),
        out_specs=[VMEM] * len(outs),
        scratch_shapes=list(scratch),
        input_output_aliases=aliases or {},
        cost_estimate=pl.CostEstimate(flops=flops, bytes_accessed=moved, transcendentals=0),
        compiler_params=pltpu.CompilerParams(vmem_limit_bytes=24 * 1024 * 1024),
    )(*args)


def lanes_of(shape):
    return lax.broadcasted_iota(jnp.int32, shape, len(shape) - 1)


def sublanes_of(shape):
    return lax.broadcasted_iota(jnp.int32, shape, len(shape) - 2)


def group_total(v):
    lane = lanes_of(v.shape)
    v = v + jnp.where(lane % 2 == 0, pltpu.roll(v, 127, 1), pltpu.roll(v, 1, 1))
    return v + jnp.where(lane % 4 < 2, pltpu.roll(v, 126, 1), pltpu.roll(v, 2, 1))


def column_sum(v):
    part = jnp.sum(v.reshape(-1, 8, v.shape[-1]), axis=0)
    return jnp.broadcast_to(jnp.sum(part, axis=0, keepdims=True), part.shape)


def split_row(row):
    high = row.astype(BF16).astype(F32)
    middle = (row - high).astype(BF16).astype(F32)
    low = row - high - middle
    index = sublanes_of((8, 128))
    parts = jnp.where(index == 0, high, jnp.where(index == 1, middle, low))
    return jnp.concatenate([parts, parts], axis=0).astype(BF16)


def join_row(parts):
    parts = parts.astype(F32)
    return jnp.broadcast_to(parts[0:1] + parts[1:2] + parts[2:3], (8, 128))


def entry_kernel(
    up_hbm, x_hbm, gain_hbm, bias_hbm, kernel_hbm, up_ref, x_ref, gain_ref, bias_ref, kernel_ref, facing_ref, stat_ref, sems
):
    pairs = ((up_hbm, up_ref), (x_hbm, x_ref), (gain_hbm, gain_ref), (bias_hbm, bias_ref), (kernel_hbm, kernel_ref))
    copies = [pltpu.make_async_copy(source, target, sems.at[i]) for i, (source, target) in enumerate(pairs)]
    for copy in copies:
        copy.start()
    copies[0].wait()
    left = lax.axis_index("sect") == 0
    facing = jnp.where(left, up_ref[:, :, 16:].astype(F32)[:, :, 15], up_ref[:, :, :16].astype(F32)[:, :, 0])
    facing_ref[:32] = facing.reshape(32, 128).astype(BF16)
    copies[1].wait()
    x = x_ref[...].astype(F32).reshape(-1, 128)
    total = group_total(column_sum(x))
    square = group_total(column_sum(x * x))
    row = jnp.where(lanes_of(total.shape) % 4 < 2, total, square)
    stat_ref[...] = row
    facing_ref[32:] = split_row(row)
    for copy in copies[2:]:
        copy.wait()


def columns_of(side_ref):
    return side_ref[:32].astype(F32).reshape(4, 8, 128)


def edge_of(up_ref, side_ref, bottom, row):
    columns = columns_of(side_ref)
    parts = split_row(row)[:8].astype(F32)[:4]
    tail = [jnp.where(bottom, columns[:, 7], columns[:, 0]), parts, jnp.zeros((8, 128), F32)]
    main = jnp.where(bottom, up_ref[:, 7], up_ref[:, 0]).reshape(128, 128)
    return main, jnp.concatenate(tail, axis=0).astype(BF16)


def edge_kernel(up_ref, side_ref, stat_ref, near_ref, far_ref, sum_ref):
    even = lax.axis_index("rows") % 2 == 0
    row = stat_ref[...] + join_row(side_ref[32:])
    sum_ref[...] = row
    near_ref[:128], near_ref[128:] = edge_of(up_ref, side_ref, even, row)
    far_ref[:128], far_ref[128:] = edge_of(up_ref, side_ref, jnp.logical_not(even), row)


def beyond(near_ref, far_ref):
    even = lax.axis_index("rows") % 2 == 0
    outside = jnp.logical_or(lax.axis_index("rows") == 0, lax.axis_index("rows") == lax.axis_size("rows") - 1)
    near = near_ref[:128].reshape(4, 32, 128)
    far = far_ref[:128].reshape(4, 32, 128)
    far = jnp.where(outside, jnp.zeros_like(far), far)
    near_column = near_ref[128:].astype(F32)[:4]
    far_column = far_ref[128:].astype(F32)[:4]
    far_column = jnp.where(outside, jnp.zeros_like(far_column), far_column)
    above = jnp.where(even, far, near), jnp.where(even, far_column, near_column)
    below = jnp.where(even, near, far), jnp.where(even, near_column, far_column)
    return above, below


def early_kernel(up_ref, side_ref, near_ref, far_ref, stat_ref, early_ref, sent_ref):
    row = stat_ref[...] + join_row(near_ref[128:].astype(F32)[4:8])
    sent_ref[...] = jnp.broadcast_to(row[None], (sent_ref.shape[0] // 8, 8, 128)).reshape(sent_ref.shape)
    (above, above_column), (below, below_column) = beyond(near_ref, far_ref)
    columns = columns_of(side_ref)
    for f in range(2):
        early_ref[f * 320 : f * 320 + 32] = above[f]
        early_ref[f * 320 + 32 : f * 320 + 288] = up_ref[f].reshape(256, 128)
        early_ref[f * 320 + 288 : f * 320 + 320] = below[f]
        column = [above_column[f : f + 1], columns[f], below_column[f : f + 1], jnp.zeros((6, 128), F32)]
        early_ref[640 + f * 16 : 656 + f * 16] = jnp.concatenate(column, axis=0).astype(BF16)


def column_taps(core, beside):
    left = lax.axis_index("sect") == 0
    index = sublanes_of(core.shape)
    first = index == 0
    last = index == 31
    zero = jnp.zeros_like(core)
    beside = jnp.broadcast_to(beside[:, None, :], core.shape)
    ahead = jnp.where(last, jnp.where(left, beside, zero), pltpu.roll(core, 31, 1))
    behind = jnp.where(first, jnp.where(left, zero, beside), pltpu.roll(core, 1, 1))
    ahead = ahead + jnp.where(first, jnp.where(left, core, zero), zero)
    behind = behind + jnp.where(last, jnp.where(left, zero, core), zero)
    return ahead, core, behind


def put(v_ref, f, r, b, e, rows):
    j = (b * 3 + e) * 128
    count = rows.shape[0]
    v_ref[f, r * 32 : (r + count) * 32, j : j + 128] = rows.astype(BF16).reshape(count * 32, 128)


def times_taps(lhs, taps_ref, a):
    return lax.dot_general(lhs, taps_ref[a], (((1,), (1,)), ((), ())), preferred_element_type=F32)


def put_own(v_ref, f, e, part):
    zero = jnp.zeros_like(part[0])
    top = part[1] + jnp.where(lax.axis_index("rows") == 0, part[0], zero)
    low = part[6] + jnp.where(lax.axis_index("rows") == lax.axis_size("rows") - 1, part[7], zero)
    put(v_ref, f, 0, 0, e, top[None])
    put(v_ref, f, 1, 0, e, part[2:8])
    put(v_ref, f, 0, 1, e, part)
    put(v_ref, f, 1, 2, e, part[0:6])
    put(v_ref, f, 7, 2, e, low[None])


def taps_kernel(up_ref, kernel_ref, v_ref, taps_ref):
    for a in range(3):
        for b in range(3):
            for e in range(3):
                j = (b * 3 + e) * 128
                taps_ref[a, :, j : j + 128] = kernel_ref[a, b, e]
    for f in range(4):
        put_own(v_ref, f, 1, up_ref[f].astype(F32))


def own_kernel(up_ref, side_ref, taps_ref, begun_ref, v_ref, dh_ref):
    columns = columns_of(side_ref)
    for f in range(4):
        ahead, _, behind = column_taps(up_ref[f].astype(F32), columns[f])
        put_own(v_ref, f, 0, ahead)
        put_own(v_ref, f, 2, behind)
    for f in range(4):
        total = None
        for a in range(3):
            if f + 2 - a < 4:
                term = times_taps(v_ref[f + 2 - a, 32:224], taps_ref, a)
                total = term if total is None else total + term
        dh_ref[f * 256 + 32 : f * 256 + 224] = total

    @pl.when(lax.axis_index("tm") == 0)
    def _():
        fold_first(v_ref, 32, 224)
        dh_ref[32:224] += times_taps(v_ref[0, 32:224], taps_ref, 1) + times_taps(v_ref[6, 32:224], taps_ref, 0)


def fold_first(v_ref, lo, hi):
    both = v_ref[1, lo:hi].astype(F32) + v_ref[0, lo:hi].astype(F32)
    v_ref[6, lo:hi] = both.astype(BF16)
    v_ref[7, lo:hi] = (both + v_ref[2, lo:hi].astype(F32)).astype(BF16)


def spread_edges(near_ref, far_ref, later_ref, v_ref):
    (above, above_column), (below, below_column) = beyond(near_ref, far_ref)
    row_first = lax.axis_index("rows") == 0
    row_last = lax.axis_index("rows") == lax.axis_size("rows") - 1
    outer = jnp.concatenate([above, below], axis=0).astype(F32)
    outer_column = jnp.concatenate([above_column, below_column], axis=0)
    for e, part in enumerate(column_taps(outer, outer_column)):
        for f in range(4):
            put(v_ref, f, 0, 2, e, part[f : f + 1])
            put(v_ref, f, 7, 0, e, part[f + 4 : f + 5])
    for f in range(2):
        later = later_ref[f * 320 : f * 320 + 320].astype(F32).reshape(10, 32, 128)
        column = later_ref[640 + f * 16 : 656 + f * 16].astype(F32)[:10]
        for e, part in enumerate(column_taps(later, column)):
            zero = jnp.zeros_like(part[0])
            top = part[2] + jnp.where(row_first, part[1], zero)
            low = part[7] + jnp.where(row_last, part[8], zero)
            put(v_ref, f + 4, 0, 0, e, top[None])
            put(v_ref, f + 4, 1, 0, e, part[3:10])
            put(v_ref, f + 4, 0, 1, e, part[1:9])
            put(v_ref, f + 4, 0, 2, e, part[0:7])
            put(v_ref, f + 4, 7, 2, e, low[None])

    @pl.when(lax.axis_index("tm") == 0)
    def _():
        fold_first(v_ref, 0, 32)
        fold_first(v_ref, 224, 256)


def grad_kernel(x_ref, norm_ref, gain_ref, bias_ref, taps_ref, part_ref, v_ref, da_ref, sums_ref, dh_ref):
    def edges(lo, hi):
        return jnp.concatenate([v_ref[lo:hi, 0:32], v_ref[lo:hi, 224:256]], axis=1).reshape((hi - lo) * 64, 1152)

    outer = times_taps(edges(0, 4), taps_ref, 2)
    one = times_taps(edges(1, 4), taps_ref, 1)
    two = times_taps(edges(2, 4), taps_ref, 0)
    outer = outer + jnp.concatenate([one, jnp.zeros((64, 128), F32)], axis=0)
    outer = outer + jnp.concatenate([two, jnp.zeros((128, 128), F32)], axis=0)
    for f in range(4):
        dh_ref[f * 256 : f * 256 + 32] = outer[f * 64 : f * 64 + 32]
        dh_ref[f * 256 + 32 : f * 256 + 224] = part_ref[f * 256 + 32 : f * 256 + 224]
        dh_ref[f * 256 + 224 : f * 256 + 256] = outer[f * 64 + 32 : f * 64 + 64]
    dh_ref[768:1024] += times_taps(v_ref[4], taps_ref, 1)
    dh_ref[512:1024] += times_taps(v_ref[4:6].reshape(512, 1152), taps_ref, 0)

    @pl.when(lax.axis_index("tm") == 0)
    def _():
        more = times_taps(edges(0, 1), taps_ref, 1) + times_taps(edges(6, 7), taps_ref, 0)
        dh_ref[0:32] += more[:32]
        dh_ref[224:256] += more[32:]

    bias_sum = jnp.zeros((8, 128), F32)
    gain_sum = jnp.zeros((8, 128), F32)
    for block in range(8):
        xhat, pre = block_of(x_ref, norm_ref, gain_ref, bias_ref, block)
        sig = 1.0 / (1.0 + jnp.exp(-pre))
        da = dh_ref[block * 128 : (block + 1) * 128] * sig * (1.0 + pre * (1.0 - sig))
        da_ref[block * 128 : (block + 1) * 128] = da
        bias_sum = bias_sum + jnp.sum(da.reshape(16, 8, 128), axis=0)
        gain_sum = gain_sum + jnp.sum((da * xhat).reshape(16, 8, 128), axis=0)
    sums_ref[...] = jnp.where(sublanes_of((8, 128)) == 0, column_sum(bias_sum), column_sum(gain_sum))


def sums_to_pair(row):
    lane = lanes_of(row.shape)
    total = jnp.where(lane % 4 < 2, row, pltpu.roll(row, 2, 1))
    square = jnp.where(lane % 4 < 2, pltpu.roll(row, 126, 1), row)
    return total, square


def product_of(turned, v_ref, a, lo, hi):
    if a == 2:
        return jnp.dot(turned, v_ref[0:4, :, lo:hi].reshape(1024, hi - lo), preferred_element_type=F32)
    source = jnp.where(lax.axis_index("tm") == 0, 7 - a, 2 - a)
    first = jnp.dot(turned[:, :256], v_ref[source, :, lo:hi], preferred_element_type=F32)
    rest = v_ref[3 - a : 6 - a, :, lo:hi].reshape(768, hi - lo)
    return first + jnp.dot(turned[:, 256:], rest, preferred_element_type=F32)


def half_product(half, turned, v_ref, w_ref):
    for a, lo, hi in (((0, 0, 9), (1, 0, 5)), ((1, 5, 9), (2, 0, 9)))[half]:
        product = product_of(turned, v_ref, a, lo * 128, hi * 128)
        for j in range(lo, hi):
            block = product[:, (j - lo) * 128 : (j - lo + 1) * 128].T.reshape(16, 8, 128)
            w_ref[:, (a * 9 + j) % HALF] = block
    if half == 1:
        w_ref[:, HALF - 1] = jnp.zeros((16, 8, 128), F32)


def block_of(x_ref, norm_ref, gain_ref, bias_ref, block):
    half = (block % 2) * 4
    x = x_ref[block // 2, half : half + 4].astype(F32).reshape(128, 128)
    xhat = (x - norm_ref[0:1]) * norm_ref[8:9]
    return xhat, xhat * gain_ref[...] + bias_ref[...]


def away_kernel(
    counted, near_ref, far_ref, later_ref, x_ref, stat_ref, gain_ref, bias_ref, begun_ref, w_ref, turned_ref, norm_ref, v_ref
):
    spread_edges(near_ref, far_ref, later_ref, v_ref)
    total, square = sums_to_pair(column_sum(stat_ref[...]))
    mean = total / counted
    norm_ref[0:8] = mean
    norm_ref[8:16] = lax.rsqrt(square / counted - mean * mean + 1e-06)
    for block in range(8):
        _, pre = block_of(x_ref, norm_ref, gain_ref, bias_ref, block)
        hidden = pre * (1.0 / (1.0 + jnp.exp(-pre)))
        turned_ref[:, block * 128 : (block + 1) * 128] = hidden.astype(BF16).T
    left = lax.axis_index("sect") == 0

    @pl.when(left)
    def _():
        half_product(1, turned_ref[...], v_ref, w_ref)

    @pl.when(jnp.logical_not(left))
    def _():
        half_product(0, turned_ref[...], v_ref, w_ref)


def home_kernel(turned_ref, v_ref, w_ref):
    left = lax.axis_index("sect") == 0

    @pl.when(left)
    def _():
        half_product(0, turned_ref[...], v_ref, w_ref)

    @pl.when(jnp.logical_not(left))
    def _():
        half_product(1, turned_ref[...], v_ref, w_ref)


def split_sums(sums):
    row = sublanes_of(sums.shape)
    high = sums.astype(BF16).astype(F32)
    middle = (sums - high).astype(BF16).astype(F32)
    low = sums - high - middle
    return jnp.where(
        row < 2, high, jnp.where(row < 4, pltpu.roll(middle, 2, 0), pltpu.roll(low, 4, 0))
    )


def join_sums(parts):
    return parts + pltpu.roll(parts, 6, 0) + pltpu.roll(parts, 4, 0)


def pair_kernel(own_ref, other_ref, sums_ref, other_sums_ref, out_ref):
    slot = split_sums(sums_ref[...] + other_sums_ref[...])
    for i in range(16):
        body = (own_ref[i] + other_ref[i]).reshape(HALF * 8, 128)
        out_ref[i] = jnp.concatenate([body, slot], axis=0).astype(BF16)


def power_for(values):
    most = jnp.max(jnp.max(jnp.abs(values), axis=0, keepdims=True), axis=1, keepdims=True)
    bits = jnp.log(jnp.maximum(most, 1e-30)) * 1.4426950408889634
    return jnp.clip(jnp.floor(14.0 - bits), -100.0, 100.0)


def share_kernel(in_ref, out_ref):
    rows = HALF * 8
    total = in_ref[0].astype(F32)
    for i in range(1, in_ref.shape[0]):
        total = total + in_ref[i].astype(F32)
    body = total[:rows]
    sums = join_sums(total[rows:])
    index = sublanes_of(sums.shape)
    sums = jnp.where(index < 2, sums, jnp.zeros_like(sums))
    power = power_for(body)
    power_of_sums = power_for(sums)
    slot = split_sums(sums * jnp.exp2(power_of_sums))
    slot = jnp.where(index == 6, power, jnp.where(index == 7, power_of_sums, slot))
    out_ref[:rows] = body * jnp.exp2(power)
    out_ref[rows:] = slot


def last_sum_kernel(scaling, in_ref, half_ref, sums_ref):
    rows = HALF * 8
    total = jnp.zeros((rows, 128), F32)
    sums = jnp.zeros((8, 128), F32)
    for i in range(in_ref.shape[0]):
        slot = in_ref[i, rows:]
        total = total + in_ref[i, :rows] * jnp.exp2(-slot[6:7])
        sums = sums + join_sums(slot) * jnp.exp2(-slot[7:8])
    half_ref[...] = total * scaling
    sums_ref[...] = sums


def finish_kernel(counted, scaling, x_ref, da_ref, norm_ref, sums_ref, gain_ref, out_ref, gain_grad_ref, bias_grad_ref):
    gain = gain_ref[...]
    mean = norm_ref[0:1]
    rstd = norm_ref[8:9]
    sums = sums_ref[...]
    bias_grad_ref[...] = sums[0:1] * scaling
    gain_grad_ref[...] = sums[1:2] * scaling
    averages = group_total(gain * sums) / counted
    leading = averages[0:1]
    trailing = averages[1:2]
    centred = x_ref[...].astype(F32).reshape(-1, 128) - mean
    grad = da_ref[...] * (rstd * gain) - rstd * leading - centred * (rstd * rstd * trailing)
    out_ref[...] = grad.astype(BF16).reshape(out_ref.shape)


def join_kernel(half_ref, other_ref, out_ref):
    left = lax.axis_index("sect") == 0
    half = half_ref[...]
    other = other_ref[...]
    out_ref[: HALF * 8] = jnp.where(left, half, other)
    out_ref[HALF * 8 :] = jnp.where(left, other, half)[: (TAPS - HALF) * 8]


def shape_of(shape, dtype=F32):
    return jax.ShapeDtypeStruct(shape, dtype)


def local(activations, group_norm_gain, group_norm_bias, upstream, kernel):
    frames, height, columns, channels = activations.shape
    n_time, n_rows, n_sect = (lax.axis_size(axis) for axis in ("tm", "rows", "sect"))
    cells = frames * height * columns
    total_cells = cells * n_time * n_rows * n_sect
    counted = float(total_cells * (channels // GROUPS))
    scaling = float(total_cells) ** (-0.5)
    swap = [(0, 1), (1, 0)]
    near = [(i, i ^ 1) for i in range(n_rows)]
    far = [(i, (i - 1) % n_rows if i % 2 == 0 else (i + 1) % n_rows) for i in range(n_rows)]

    up, x, gain, bias, weights, facing, stat = call(
        entry_kernel,
        [
            shape_of(upstream.shape, BF16),
            shape_of(activations.shape, BF16),
            shape_of((1, channels)),
            shape_of((1, channels)),
            shape_of(kernel.shape, BF16),
            shape_of((48, channels), BF16),
            shape_of((8, channels)),
        ],
        [
            held(upstream, pltpu.HBM),
            held(activations, pltpu.HBM),
            held(group_norm_gain.reshape(1, channels), pltpu.HBM),
            held(group_norm_bias.reshape(1, channels), pltpu.HBM),
            held(kernel, pltpu.HBM),
        ],
        [HBM] * 5,
        [pltpu.SemaphoreType.DMA((5,))],
    )
    side = lax.ppermute(facing, "sect", swap)
    spread, taps = call(
        taps_kernel,
        [pltpu.VMEM((8, 256, 1152), BF16), shape_of((3, channels, 9 * channels), BF16)],
        [up, weights],
    )
    side, taps = lax.optimization_barrier((side, taps))
    nearer, farther, stat = call(
        edge_kernel,
        [shape_of((144, channels), BF16), shape_of((144, channels), BF16), shape_of((8, channels))],
        [up, side, stat],
    )
    nearer = lax.ppermute(nearer, "rows", near)
    farther = lax.ppermute(farther, "rows", far)
    spread, inner = call(
        own_kernel,
        [pltpu.VMEM((8, 256, 1152), BF16), shape_of((cells, channels))],
        [up, side, taps, held(spread, pltpu.VMEM)],
        flops=cells * TAPS * channels * channels,
        aliases={3: 0},
    )
    nearer, inner = lax.optimization_barrier((nearer, inner))
    groups = [[t * n_rows + r for t in range(n_time) for r in chosen] for chosen in ((1, 2, 4, 7), (0, 3, 5, 6))]
    early, stat = call(
        early_kernel,
        [shape_of((672, channels), BF16), shape_of((len(groups[0]), channels))],
        [up, side, nearer, farther, stat],
        [VMEM, VMEM, VMEM, VMEM, VMEM],
    )
    later = lax.ppermute(early, "tm", [(i + 1, i) for i in range(n_time - 1)])
    stat = lax.all_to_all(stat[:, None], ("tm", "rows"), 0, 0, axis_index_groups=groups).reshape(-1, channels)
    stat, later = lax.optimization_barrier((stat, later))
    away, turned, norm, spread = call(
        functools.partial(away_kernel, counted),
        [
            shape_of((16, HALF, 8, 128)),
            shape_of((channels, cells), BF16),
            shape_of((16, channels)),
            pltpu.VMEM((8, 256, 1152), BF16),
        ],
        [nearer, farther, later, x, stat, gain, bias, held(spread, pltpu.VMEM)],
        flops=cells * TAPS * channels * channels,
        aliases={7: 3},
    )
    arrived = lax.ppermute(away, "sect", swap)
    da, sums = call(
        grad_kernel,
        [shape_of((cells, channels)), shape_of((8, channels))],
        [x, norm, gain, bias, taps, inner, held(spread, pltpu.VMEM)],
        scratch=[pltpu.VMEM((cells, channels), F32)],
        flops=cells * TAPS * channels * channels,
    )
    other_sums = lax.ppermute(sums, "sect", swap)
    (home,) = call(
        home_kernel,
        [shape_of((16, HALF, 8, 128))],
        [turned, held(spread, pltpu.VMEM)],
        flops=cells * TAPS * channels * channels,
    )
    (sent,) = call(
        pair_kernel, [shape_of((16, SLOTS * 8, 128), BF16)], [home, arrived, sums, other_sums]
    )
    gathered = lax.all_to_all(sent, "tm", 0, 0)
    (share,) = call(share_kernel, [shape_of((SLOTS * 8, 128))], [gathered])
    share = jnp.broadcast_to(share.astype(jnp.float16)[None], (n_rows, SLOTS * 8, 128))
    shares = lax.all_to_all(share, "rows", 0, 0).astype(F32)
    half, sums = call(
        functools.partial(last_sum_kernel, scaling),
        [shape_of((HALF * 8, 128)), shape_of((8, 128))],
        [shares],
    )
    other = lax.ppermute(half, "sect", swap)
    input_gradient, gain_grad, bias_grad = call(
        functools.partial(finish_kernel, counted, scaling),
        [shape_of(activations.shape, BF16), shape_of((1, 128)), shape_of((1, 128))],
        [x, da, norm, sums, gain],
    )
    (whole,) = call(join_kernel, [shape_of((TAPS * 8, 128))], [half, other])
    weight_grad = whole.reshape(3, 3, 3, 8, 128).transpose(0, 1, 2, 4, 3)
    return (input_gradient, gain_grad.reshape(128), bias_grad.reshape(128), weight_grad)


def solution(mesh):
    return jax.shard_map(
        local,
        mesh=mesh,
        in_specs=(P("tm", "rows", "sect", None), P(), P(), P("tm", "rows", "sect", None), P()),
        out_specs=(P("tm", "rows", "sect", None), P(), P(), P(None, None, None, None, "tm")),
        check_vma=False,
    )
```
